32 devices in a mesh: lat: 2 (over x), lon: 16 (over z, y, core).
Axes of the slice: x: 2, y: 2, z: 4, core: 2. Of those that a mesh axis runs over, the one named last changes fastest.
Arguments:
- tokens: bfloat16 [16, 32, 64, 768], P(None, 'lat', 'lon'), may hold values from -6 to 6
- channel_mask: int32 [16, 69], replicated, may hold values 0 or 1
- lead_index: int32 [16], replicated, may hold values from 0 to 31
- chan_embed: bfloat16 [69, 768], replicated, may hold values from -2 to 2
- lead_embed: bfloat16 [32, 768], replicated, may hold values from -6 to 6
- norm1_gain: bfloat16 [768], replicated, may hold values from 0.25 to 1.75
- norm1_bias: bfloat16 [768], replicated, may hold values from -3 to 3
- qkv_weight: bfloat16 [768, 2304], replicated, may hold values from -0.21875 to 0.21875
- out_weight: bfloat16 [768, 768], replicated, may hold values from -4 to 4
- out_bias: bfloat16 [768], replicated, may hold values from -3 to 3
- norm2_gain: bfloat16 [768], replicated, may hold values from 0.25 to 1.75
- norm2_bias: bfloat16 [768], replicated, may hold values from -3 to 3
- up_weight: bfloat16 [768, 3072], replicated, may hold values from -0.21875 to 0.21875
- up_bias: bfloat16 [3072], replicated, may hold values from -3 to 3
- down_weight: bfloat16 [3072, 768], replicated, may hold values from -0.109375 to 0.109375
- down_bias: bfloat16 [768], replicated, may hold values from -3 to 3
- cotangent: bfloat16 [16, 32, 64, 768], P(None, 'lat', 'lon'), may hold values from -6 to 6
Outputs:
- result: bfloat16 [16, 32, 64, 768], P(None, 'lat', 'lon')
- grad_tokens: bfloat16 [16, 32, 64, 768], P(None, 'lat', 'lon')
- grad_chan_embed: float32 [69, 768], P(None, 'lon')
- grad_lead_embed: float32 [32, 768], P(None, 'lon')
- grad_norm1_gain: float32 [768], P('lon')
- grad_norm1_bias: float32 [768], P('lon')
- grad_qkv_weight: float32 [768, 2304], P('lon')
- grad_out_weight: float32 [768, 768], P('lon')
- grad_out_bias: float32 [768], P('lon')
- grad_norm2_gain: float32 [768], P('lon')
- grad_norm2_bias: float32 [768], P('lon')
- grad_up_weight: float32 [768, 3072], P('lon')
- grad_up_bias: float32 [3072], P('lon')
- grad_down_weight: float32 [3072, 768], P('lon')
- grad_down_bias: float32 [768], P('lon')
The draws below stay inside these ranges and needn't reach their ends.
All inputs are finite; a program needn't handle non-finite values.
Results may differ from the reference program's by a relative error of at most 0.017.
Values may be sent and summed in bfloat16 or wider, within the bound.
No kernel may reach another device: no remote copies, remote signals or barrier semaphores. Data moves between devices by JAX's collectives and lax.ppermute only.
A program may use at most 512 MiB of HBM per device.

```python
import jax
import jax.numpy as jnp
from jax import lax

D = 768
HEADS = 12
FF = 3072
CHANNELS = 69
LEADS = 32
LAT = 32
LON = 64
FRAMES = 16


def touch_ends(entries, key, low, largest):
    longest = entries.shape.index(max(entries.shape))
    spots = []
    for shift in (0, 1):
        where = [jax.random.randint(jax.random.fold_in(key, axis), (), 0, length) for axis, length in enumerate(entries.shape)]
        where[longest] = (where[longest] + shift) % entries.shape[longest]
        spots.append(tuple(where))
    return entries.at[spots[0]].set(low).at[spots[1]].set(largest)


def steps_of(stream_key, shape, split, smallest, largest):
    level = 1.0
    for dim, shards_of in split:
        draws = jax.random.uniform(jax.random.fold_in(jax.random.fold_in(stream_key, 6), dim), (shards_of,), jnp.float32, smallest / len(split), largest / len(split))
        level = level * jnp.repeat(jnp.exp(draws), shape[dim] // shards_of).reshape((-1,) + (1,) * (len(shape) - 1 - dim))
    return level


def scatter_about(stream_key, extent, width, limit, cuts=(), dtype=jnp.bfloat16):
    values = jax.random.normal(stream_key, extent, jnp.float32) * width
    if len(cuts) > 0:
        values = steps_of(stream_key, extent, cuts, -0.22, 0.18) * values
    return jnp.clip(values, min=-limit, max=limit).astype(dtype)


def setup_inputs(seed: int = 0) -> dict:
    arg_keys = jax.random.split(jax.random.key(seed), 18)
    tokens = scatter_about(arg_keys[0], (FRAMES, LAT, LON, D), 1.0, 6.0, ((1, 2), (2, 16)))
    channel_mask = touch_ends((jax.random.randint(arg_keys[1], (FRAMES, CHANNELS), 0, 3) < 2).astype(jnp.int32), jax.random.fold_in(arg_keys[1], 1), 0, 1)
    lead_index = touch_ends(jax.random.randint(arg_keys[2], (FRAMES,), 0, LEADS), jax.random.fold_in(arg_keys[2], 1), 0, LEADS - 1).astype(jnp.int32)
    chan_embed = scatter_about(arg_keys[3], (CHANNELS, D), 0.15, 2.0)
    lead_embed = scatter_about(arg_keys[4], (LEADS, D), 0.5, 6.0)
    norm1_gain = jnp.clip(1.0 + 0.15 * jax.random.normal(arg_keys[5], (D,), jnp.float32), 0.25, 1.75).astype(jnp.bfloat16)
    norm1_bias = scatter_about(arg_keys[6], (D,), 0.2, 3.0)
    qkv_weight = scatter_about(arg_keys[7], (D, 3 * D), D ** -0.5, 0.21875)
    out_weight = scatter_about(arg_keys[8], (D, D), 2 ** -0.5, 4.0)
    out_bias = scatter_about(arg_keys[9], (D,), 0.2, 3.0)
    norm2_gain = jnp.clip(1.0 + 0.15 * jax.random.normal(arg_keys[10], (D,), jnp.float32), 0.25, 1.75).astype(jnp.bfloat16)
    norm2_bias = scatter_about(arg_keys[11], (D,), 0.2, 3.0)
    up_weight = scatter_about(arg_keys[12], (D, FF), D ** -0.5, 0.21875)
    up_bias = scatter_about(arg_keys[13], (FF,), 0.2, 3.0)
    down_weight = scatter_about(arg_keys[14], (FF, D), FF ** -0.5, 0.109375)
    down_bias = scatter_about(arg_keys[15], (D,), 0.2, 3.0)
    cotangent = scatter_about(arg_keys[16], (FRAMES, LAT, LON, D), 1.0, 6.0, ((1, 2), (2, 16)))
    return {"tokens": tokens, "channel_mask": channel_mask, "lead_index": lead_index, "chan_embed": chan_embed, "lead_embed": lead_embed, "norm1_gain": norm1_gain, "norm1_bias": norm1_bias, "qkv_weight": qkv_weight, "out_weight": out_weight, "out_bias": out_bias, "norm2_gain": norm2_gain, "norm2_bias": norm2_bias, "up_weight": up_weight, "up_bias": up_bias, "down_weight": down_weight, "down_bias": down_bias, "cotangent": cotangent}


@jax.custom_vjp
def low(v):
    return lax.optimization_barrier(v.astype(jnp.bfloat16)).astype(jnp.float32)

@jax.custom_vjp
def low_back(v):
    return v

def low_keep(v):
    return (low(v), None)

def low_pass(kept, grad):
    return (grad,)

def back_keep(v):
    return (v, None)

def back_low(kept, grad):
    return (low(grad),)
low.defvjp(low_keep, low_pass)
low_back.defvjp(back_keep, back_low)
EPSILON = 1e-06
SCALING = 0.125
HIGHEST = lax.Precision.HIGHEST

def layer_norm(value):
    row_mean = lax.optimization_barrier(jnp.mean(value, axis=-1, keepdims=True))
    centered = value - row_mean
    return centered * lax.rsqrt(lax.optimization_barrier(jnp.mean(centered * centered, axis=-1, keepdims=True)) + EPSILON)

def frame_attention(pieces):
    queries, keyset, valueset = pieces
    scores = low_back(jnp.einsum('qhd,khd->hqk', queries, keyset, precision=HIGHEST) * SCALING)
    attn_probs = low(jax.nn.softmax(scores, axis=-1))
    return jnp.einsum('hqk,khd->qhd', attn_probs, valueset, precision=HIGHEST)

def forward(tokens, mask_float, lead_index, chan_embed, lead_embed, norm1_gain, norm1_bias, qkv_weight, out_weight, out_bias, norm2_gain, norm2_bias, up_weight, up_bias, down_weight, down_bias):
    frames = tokens.shape[0]
    patches = LAT * LON
    head_size = D // HEADS
    flat = tokens.reshape(frames, patches, D)
    start = flat + jnp.dot(mask_float, chan_embed, precision=HIGHEST)[:, None, :]
    hidden1 = layer_norm(start) * norm1_gain + norm1_bias + lead_embed[lead_index][:, None, :]
    qkv = low_back(low(jnp.einsum('fpd,de->fpe', low(hidden1), qkv_weight, precision=HIGHEST)))
    queries = qkv[..., :D].reshape(frames, patches, HEADS, head_size)
    keyset = qkv[..., D:2 * D].reshape(frames, patches, HEADS, head_size)
    valueset = qkv[..., 2 * D:].reshape(frames, patches, HEADS, head_size)
    attended = lax.map(jax.checkpoint(frame_attention), (queries, keyset, valueset))
    attended = low_back(low(attended.reshape(frames, patches, D)))
    middle = start + low_back(jnp.einsum('fpd,de->fpe', attended, out_weight, precision=HIGHEST) + out_bias)
    hidden2 = low(layer_norm(middle) * norm2_gain + norm2_bias)
    pre_act = low_back(jnp.einsum('fpd,de->fpe', hidden2, up_weight, precision=HIGHEST) + up_bias)
    activ = low(jax.nn.gelu(pre_act))
    result = middle + low_back(jnp.einsum('fpe,ed->fpd', activ, down_weight, precision=HIGHEST) + down_bias)
    return result.reshape(tokens.shape)

def reference(tokens, channel_mask, lead_index, chan_embed, lead_embed, norm1_gain, norm1_bias, qkv_weight, out_weight, out_bias, norm2_gain, norm2_bias, up_weight, up_bias, down_weight, down_bias, cotangent):
    floats = [value.astype(jnp.float32) for value in (tokens, chan_embed, lead_embed, norm1_gain, norm1_bias, qkv_weight, out_weight, out_bias, norm2_gain, norm2_bias, up_weight, up_bias, down_weight, down_bias)]
    mask_float = channel_mask.astype(jnp.float32)

    def wrapped(*values):
        return forward(values[0], mask_float, lead_index, *values[1:])
    result, pullback = jax.vjp(wrapped, *floats)
    grads = pullback(cotangent.astype(jnp.float32))
    return (result.astype(jnp.bfloat16), grads[0].astype(jnp.bfloat16), grads[1], grads[2], grads[3], grads[4], grads[5], grads[6], grads[7], grads[8], grads[9], grads[10], grads[11], grads[12], grads[13])
```

```python
import functools
import math

import jax
import jax.numpy as jnp
from jax import lax
from jax.experimental import pallas as pl
from jax.experimental.pallas import tpu as pltpu
from jax.sharding import Mesh, PartitionSpec as P

HEADS = 12
EPSILON = 1e-06
SCALING = 0.125
LOG2E = math.log2(math.e)
F32 = jnp.float32
BF = jnp.bfloat16
NN = (((1,), (0,)), ((), ()))
NT = (((1,), (1,)), ((), ()))
TN = (((0,), (0,)), ((), ()))
VMEM_LIMIT = 56 << 20


def mm(a, b, dims=NN):
    return lax.dot_general(a, b, dims, preferred_element_type=F32)


def of_head(value, head, axis=1):
    lane = lax.broadcasted_iota(jnp.int32, value.shape, axis)
    return jnp.where((lane // 64) == head, value, jnp.zeros_like(value))


def attend_kernel(q_ref, k0, k1, v0, v1, o_ref, full_ref, lse_ref):
    q = q_ref[...]
    ones = jnp.ones(v0.shape, BF)
    val0 = jnp.concatenate([v0[...], ones], 1)
    val1 = jnp.concatenate([v1[...], ones], 1)
    outs, logs = [], []
    for head in range(2):
        qm = of_head(q, head)
        s0 = mm(qm, k0[...], NT)
        s1 = mm(qm, k1[...], NT)
        top = jnp.max(jnp.maximum(s0, s1), axis=1, keepdims=True)
        p0 = jnp.exp2(s0 - top).astype(BF)
        p1 = jnp.exp2(s1 - top).astype(BF)
        both = mm(p0, val0) + mm(p1, val1)
        total = both[:, 128:]
        outs.append(both[:, :128] / total)
        logs.append(top + jnp.log2(total))
    lane = lax.broadcasted_iota(jnp.int32, outs[0].shape, 1)
    both = jnp.where(lane < 64, outs[0], outs[1])
    o_ref[...] = both.astype(BF)
    full_ref[...] = both
    turned = jnp.where(lane < 64, logs[0], logs[1]).T
    lse_ref[0:4, :] = turned[0:4]
    lse_ref[4:8, :] = turned[64:68]


def attend(q, kv_own, kv_peer, frames):
    tokens, width = q.shape
    pairs = width // 128
    n = tokens // frames
    bq = min(512, n)
    nb = n // bq
    qs = pl.BlockSpec((bq, 128), lambda f, p, j: (f * nb + j, p))
    ks = pl.BlockSpec((n, 128), lambda f, p, j: (f, p))
    vs = pl.BlockSpec((n, 128), lambda f, p, j: (f, pairs + p))
    ls = pl.BlockSpec((8, bq), lambda f, p, j: (p, f * nb + j))
    return pl.pallas_call(
        attend_kernel,
        grid=(frames, pairs, nb),
        in_specs=[qs, ks, ks, vs, vs],
        out_specs=[qs, qs, ls],
        out_shape=[
            jax.ShapeDtypeStruct((tokens, width), BF),
            jax.ShapeDtypeStruct((tokens, width), F32),
            jax.ShapeDtypeStruct((pairs * 8, tokens), F32),
        ],
        compiler_params=pltpu.CompilerParams(vmem_limit_bytes=VMEM_LIMIT),
        cost_estimate=pl.CostEstimate(
            flops=50_000_000_000, bytes_accessed=12_000_000, transcendentals=0
        ),
        name="attend",
    )(q, kv_own, kv_peer, kv_own, kv_peer)


def attend_back_kernel(
    q_ref, k0, k1, v0, v1, go_ref, o_ref, lse_ref, dq_ref, dk0, dk1, dv0, dv1, dka, dva
):
    j = pl.program_id(2)
    q = q_ref[...]
    go = go_ref[...]
    prod = (go.astype(F32) * o_ref[...]).T
    dq = None
    for part, (k, v) in enumerate(((k0, v0), (k1, v1))):
        keys = k[...]
        vals = v[...]
        turned = keys.T
        acc_v = acc_k = None
        for head in range(2):
            qm = of_head(q, head)
            gom = of_head(go, head)
            lse = lse_ref[4 * head : 4 * head + 1, :]
            delta = jnp.sum(prod[64 * head : 64 * head + 64], axis=0, keepdims=True)
            probs = jnp.exp2(mm(keys, qm, NT) - lse)
            ds = (probs * (mm(vals, gom, NT) - delta)).astype(BF)
            probs = probs.astype(BF)
            a = mm(probs, gom)
            b = mm(ds, qm)
            c = mm(of_head(turned, head, 0), ds)
            dq = c if dq is None else dq + c
            acc_v = a if acc_v is None else acc_v + a
            acc_k = b if acc_k is None else acc_k + b

        @pl.when(j == 0)
        def _():
            dva[part] = acc_v
            dka[part] = acc_k

        @pl.when(j > 0)
        def _():
            dva[part] += acc_v
            dka[part] += acc_k

    dq_ref[...] = (dq * SCALING).T.astype(BF)

    @pl.when(j == pl.num_programs(2) - 1)
    def _():
        back = SCALING / (SCALING * LOG2E)
        dk0[...] = (dka[0] * back).astype(BF)
        dk1[...] = (dka[1] * back).astype(BF)
        dv0[...] = dva[0].astype(BF)
        dv1[...] = dva[1].astype(BF)


def attend_back(q, kv_own, kv_peer, go, att, lse, frames, first, count):
    tokens, width = q.shape
    pairs = width // 128
    n = tokens // frames
    bq = min(512, n)
    nb = n // bq
    qs = pl.BlockSpec((bq, 128), lambda f, p, j: (f * nb + j, first + p))
    ks = pl.BlockSpec((n, 128), lambda f, p, j: (f, first + p))
    vs = pl.BlockSpec((n, 128), lambda f, p, j: (f, pairs + first + p))
    ls = pl.BlockSpec((8, bq), lambda f, p, j: (first + p, f * nb + j))
    qo = pl.BlockSpec((bq, 128), lambda f, p, j: (f * nb + j, p))
    ko = pl.BlockSpec((n, 128), lambda f, p, j: (f, p))
    shape = jax.ShapeDtypeStruct((tokens, 128 * count), BF)
    return pl.pallas_call(
        attend_back_kernel,
        grid=(frames, count, nb),
        in_specs=[qs, ks, ks, vs, vs, qs, qs, ls],
        out_specs=[qo, ko, ko, ko, ko],
        out_shape=[shape] * 5,
        scratch_shapes=[pltpu.VMEM((2, n, 128), F32)] * 2,
        compiler_params=pltpu.CompilerParams(vmem_limit_bytes=VMEM_LIMIT),
        cost_estimate=pl.CostEstimate(
            flops=14_000_000_000 * count, bytes_accessed=3_000_000 * count, transcendentals=0
        ),
        name="attend_back",
    )(q, kv_own, kv_peer, kv_own, kv_peer, go, att, lse)


def swap_pairs(size, bit):
    return [(i, i ^ (1 << bit)) for i in range(size)]


def halve(value, axis, bit, dim):
    size = lax.axis_size(axis)
    mine = (lax.axis_index(axis) >> bit) & 1
    keep = lax.dynamic_index_in_dim(value, mine, dim, keepdims=False)
    send = lax.dynamic_index_in_dim(value, 1 - mine, dim, keepdims=False)
    return keep + lax.ppermute(send, axis, swap_pairs(size, bit))


def bits_of(size):
    return size.bit_length() - 1


def scatter_sum(value, lat_first):
    lat, chips = lax.axis_size("lat"), lax.axis_size("chip")
    lb, cb = bits_of(lat), bits_of(chips)
    _, rows, cols = value.shape
    value = halve(value.reshape((chips, 2, rows, cols)), "core", 0, 1)

    def over_lat(value):
        lead = value.shape[0]
        for bit in reversed(range(lb)):
            value = value.reshape((lead, 2, value.shape[-2] // 2, cols))
            value = halve(value, "lat", bit, 1)
        return value

    def over_chip(value, bit):
        lead, left, width = value.shape
        value = value.reshape((lead // 2, 2, left, width))
        return halve(value, "chip", bit, 1)

    order = list(range(cb))
    if lat_first:
        value = over_lat(value)
        for bit in order:
            value = over_chip(value, bit)
    else:
        for bit in order[:1]:
            value = over_chip(value, bit)
        value = over_lat(value)
        for bit in order[1:]:
            value = over_chip(value, bit)
    value = value.reshape(value.shape[-2:])
    for bit in range(lb):
        other = lax.ppermute(value, "lat", swap_pairs(lat, bit))
        high = ((lax.axis_index("lat") >> bit) & 1) == 1
        value = jnp.where(
            high,
            jnp.concatenate([other, value], 0),
            jnp.concatenate([value, other], 0),
        )
    return value


def layer_norm(value):
    row_mean = jnp.mean(value, axis=-1, keepdims=True)
    centered = value - row_mean
    inverse = lax.rsqrt(jnp.mean(centered * centered, axis=-1, keepdims=True) + EPSILON)
    return centered * inverse, inverse


def norm_back(grad_hat, normed, inverse):
    first = jnp.mean(grad_hat, axis=-1, keepdims=True)
    second = jnp.mean(grad_hat * normed, axis=-1, keepdims=True)
    return inverse * (grad_hat - first - normed * second)


def to_frames(value, chips):
    frames_all, rows, cols, width = value.shape
    frames = frames_all // chips
    value = value.reshape(frames_all, rows * cols, width)
    value = lax.all_to_all(value, ("lat", "chip"), 0, 0, tiled=True)
    if frames > 1:
        value = value.reshape(chips, frames, rows * cols, width).swapaxes(0, 1)
    return value.reshape(-1, width)


def to_places(value, chips, frames_all, rows, cols):
    width = value.shape[-1]
    frames = frames_all // chips
    if frames > 1:
        value = value.reshape(frames, chips, rows * cols, width).swapaxes(0, 1)
    value = value.reshape(frames_all, rows * cols, width)
    value = lax.all_to_all(value, ("lat", "chip"), 0, 0, tiled=True)
    return value.reshape(frames_all, rows, cols, width)


def on_device(
    tokens,
    channel_mask,
    lead_index,
    chan_embed,
    lead_embed,
    norm1_gain,
    norm1_bias,
    qkv_weight,
    out_weight,
    out_bias,
    norm2_gain,
    norm2_bias,
    up_weight,
    up_bias,
    down_weight,
    down_bias,
    cotangent,
):
    lat = lax.axis_size("lat")
    chips = lat * lax.axis_size("chip")
    lon = 2 * lax.axis_size("chip")
    frames_all, rows_here, cols_here, width = tokens.shape
    frames = frames_all // chips
    leads = lead_embed.shape[0]
    place = (lax.axis_index("chip") * 2) + lax.axis_index("core")
    core_swap = swap_pairs(2, 0)

    local_in = to_frames(tokens, chips)
    local_cot = to_frames(cotangent, chips)
    count = local_in.shape[0]
    n = count // frames

    first = lax.axis_index(("lat", "chip")) * frames
    mask_here = lax.dynamic_slice_in_dim(channel_mask, first, frames, 0).astype(BF)
    lead_here = lax.dynamic_slice_in_dim(lead_index, first, frames, 0)
    lead_onehot = (lead_here[:, None] == jnp.arange(leads, dtype=jnp.int32)[None, :]).astype(BF)
    chan_add = mm(mask_here, chan_embed)
    lead_add = mm(lead_onehot, lead_embed)
    gain_one = norm1_gain.astype(F32)
    gain_two = norm2_gain.astype(F32)

    start = local_in.astype(F32).reshape(frames, n, width) + chan_add[:, None, :]
    normed1, inverse1 = layer_norm(start)
    hidden1 = normed1 * gain_one + norm1_bias.astype(F32) + lead_add[:, None, :]
    start = start.reshape(count, width)
    hidden1 = hidden1.astype(BF).reshape(count, width)
    kv_own = mm(hidden1, qkv_weight[:, width:]).astype(BF)
    kv_peer = lax.ppermute(kv_own, "core", core_swap)
    queries = (mm(hidden1, qkv_weight[:, :width]) * (SCALING * LOG2E)).astype(BF)
    attended, attended32, lse = attend(queries, kv_own, kv_peer, frames)

    middle = start + mm(attended, out_weight) + out_bias.astype(F32)
    normed2, inverse2 = layer_norm(middle)
    hidden2 = (normed2 * gain_two + norm2_bias.astype(F32)).astype(BF)
    pre_act = mm(hidden2, up_weight) + up_bias.astype(F32)
    activ = jax.nn.gelu(pre_act).astype(BF)
    result = middle + mm(activ, down_weight) + down_bias.astype(F32)
    out_patch = to_places(result.astype(BF), chips, frames_all, rows_here, cols_here)

    grad_res = local_cot.astype(F32)
    grad_down = mm(activ, local_cot, TN).astype(BF)
    grad_down_bias = jnp.sum(grad_res, axis=0)
    grad_activ = mm(local_cot, down_weight, NT)
    unused, gelu_pull = jax.vjp(jax.nn.gelu, pre_act)
    grad_pre32 = gelu_pull(grad_activ)[0]
    grad_pre = grad_pre32.astype(BF)
    grad_up = mm(hidden2, grad_pre, TN).astype(BF)
    grad_up_bias = jnp.sum(grad_pre.astype(F32), axis=0)
    grad_hidden2 = mm(grad_pre, up_weight, NT)
    grad_gain2 = jnp.sum(grad_hidden2 * normed2, axis=0)
    grad_bias2 = jnp.sum(grad_hidden2, axis=0)
    grad_middle = grad_res + norm_back(grad_hidden2 * gain_two, normed2, inverse2)
    grad_branch = grad_middle.astype(BF)
    grad_out = mm(attended, grad_branch, TN).astype(BF)
    grad_out_bias = jnp.sum(grad_branch.astype(F32), axis=0)
    grad_att = mm(grad_branch, out_weight, NT).astype(BF)

    share = width // lon
    ff_parts = grad_up_bias.shape[0] // width
    early = jnp.stack(
        [grad_down_bias, grad_gain2, grad_bias2, grad_out_bias]
        + [x for x in grad_up_bias.reshape(lon, ff_parts, share).swapaxes(0, 1).reshape(ff_parts, -1)]
    )
    early = early.reshape(4 + ff_parts, lon, share).swapaxes(0, 1).astype(BF)
    early = jnp.pad(early, ((0, 0), (0, 16 - early.shape[1]), (0, width - share)))
    grad_out = jnp.concatenate([grad_out.reshape(lon, share, width), early], 1)

    sum_down = scatter_sum(grad_down.reshape(lon, -1, width), True)
    sum_up = scatter_sum(grad_up.reshape(lon, share, -1), False)
    sum_out = scatter_sum(grad_out, True)

    step = 2
    pairs = width // 128
    dqs, dks, dvs = [], [], []
    for pair in range(0, pairs, step):
        dq, dk0, dk1, dv0, dv1 = attend_back(
            queries, kv_own, kv_peer, grad_att, attended32, lse, frames, pair, step
        )
        got_k = lax.ppermute(dk1, "core", core_swap)
        got_v = lax.ppermute(dv1, "core", core_swap)
        dqs.append(dq)
        dks.append(dk0 + got_k)
        dvs.append(dv0 + got_v)
    grad_qkv = jnp.concatenate(dqs + dks + dvs, axis=1)

    grad_hidden1 = mm(grad_qkv, qkv_weight, NT).reshape(frames, n, width)
    normed1 = normed1.reshape(frames, n, width)
    grad_gain1 = jnp.sum(grad_hidden1 * normed1, axis=(0, 1))
    grad_bias1 = jnp.sum(grad_hidden1, axis=1)
    grad_start = grad_middle.reshape(frames, n, width) + norm_back(
        grad_hidden1 * gain_one, normed1, inverse1
    )
    grad_frame = jnp.sum(grad_start, axis=1)
    grad_patch = to_places(
        grad_start.astype(BF).reshape(count, width), chips, frames_all, rows_here, cols_here
    )
    grad_qkv_weight = mm(hidden1, grad_qkv, TN).astype(BF).reshape(lon, share, -1)
    half = grad_qkv_weight.shape[-1] // 2
    sum_qkv = jnp.concatenate(
        [
            scatter_sum(grad_qkv_weight[..., :half], True),
            scatter_sum(grad_qkv_weight[..., half:], False),
        ],
        axis=1,
    )
    late = jnp.concatenate([grad_bias1, grad_frame, grad_gain1[None]], 0)
    late = lax.all_gather(late, ("lat", "chip", "core"), axis=0)
    late = lax.dynamic_slice_in_dim(late, place * share, share, 2)
    bias_of = late[:, :frames].reshape(chips, 2, frames, share).sum(1).reshape(frames_all, share)
    start_of = late[:, frames : 2 * frames].reshape(chips, 2, frames, share).sum(1)
    start_of = start_of.reshape(frames_all, share)
    sum_gain1 = late[:, 2 * frames].sum(0)
    hot = (lead_index[:, None] == jnp.arange(leads, dtype=jnp.int32)[None, :]).astype(F32)
    sum_lead = jnp.dot(hot.T, bias_of, precision=lax.Precision.HIGHEST)
    sum_chan = jnp.dot(
        channel_mask.astype(F32).T, start_of, precision=lax.Precision.HIGHEST
    )
    small = sum_out[share:, :share].astype(F32)
    return (
        out_patch,
        grad_patch,
        sum_chan,
        sum_lead,
        sum_gain1,
        bias_of.sum(0),
        sum_qkv.astype(F32),
        sum_out[:share].astype(F32),
        small[3],
        small[1],
        small[2],
        sum_up.astype(F32),
        small[4 : 4 + ff_parts].reshape(-1),
        sum_down.astype(F32),
        small[0],
    )


def solution(mesh):
    lat, lon = mesh.shape["lat"], mesh.shape["lon"]
    fine = Mesh(mesh.devices.reshape(lat, lon // 2, 2), ("lat", "chip", "core"))
    places = P(None, "lat", ("chip", "core"), None)
    wide = ("chip", "core")
    return jax.shard_map(
        on_device,
        mesh=fine,
        in_specs=(places,) + (P(),) * 15 + (places,),
        out_specs=(
            places,
            places,
            P(None, wide),
            P(None, wide),
            P(wide),
            P(wide),
            P(wide, None),
            P(wide, None),
            P(wide),
            P(wide),
            P(wide),
            P(wide, None),
            P(wide),
            P(wide, None),
            P(wide),
        ),
        check_vma=False,
    )
```

```python
import functools
import math

import jax
import jax.numpy as jnp
from jax import lax
from jax.experimental import pallas as pl
from jax.experimental.pallas import tpu as pltpu
from jax.sharding import Mesh, PartitionSpec as P

HEADS = 12
EPSILON = 1e-06
SCALING = 0.125
LOG2E = math.log2(math.e)
F32 = jnp.float32
BF = jnp.bfloat16
NN = (((1,), (0,)), ((), ()))
NT = (((1,), (1,)), ((), ()))
TN = (((0,), (0,)), ((), ()))
VMEM_LIMIT = 56 << 20


def mm(a, b, dims=NN):
    return lax.dot_general(a, b, dims, preferred_element_type=F32)


def of_head(value, head, axis=1):
    lane = lax.broadcasted_iota(jnp.int32, value.shape, axis)
    return jnp.where((lane // 64) == head, value, jnp.zeros_like(value))


def sds(shape, dtype):
    return jax.ShapeDtypeStruct(shape, dtype)


def call(kernel, name, grid, ins, outs, scratch=(), flops=0, deps=()):
    given, skipped = len(ins), len(deps)

    def body(*refs):
        kernel(*refs[:given], *refs[given + skipped :])

    anywhere = pl.BlockSpec(memory_space=pl.ANY)
    moved = sum(math.prod(a.shape) * a.dtype.itemsize for a, spec in list(ins) + list(outs))
    return pl.pallas_call(
        body,
        grid=grid,
        in_specs=[spec for a, spec in ins] + [anywhere] * skipped,
        out_specs=[spec for a, spec in outs],
        out_shape=[a for a, spec in outs],
        scratch_shapes=list(scratch),
        compiler_params=pltpu.CompilerParams(vmem_limit_bytes=VMEM_LIMIT),
        cost_estimate=pl.CostEstimate(flops=flops, bytes_accessed=moved, transcendentals=0),
        name=name,
    )(*[a for a, spec in ins], *deps)


def attend_kernel(q_ref, k0, k1, v0, v1, o_ref, full_ref, lse_ref):
    q = q_ref[...]
    ones = jnp.ones(v0.shape, BF)
    val0 = jnp.concatenate([v0[...], ones], 1)
    val1 = jnp.concatenate([v1[...], ones], 1)
    outs, logs = [], []
    for head in range(2):
        qm = of_head(q, head)
        s0 = mm(qm, k0[...], NT)
        s1 = mm(qm, k1[...], NT)
        top = jnp.max(jnp.maximum(s0, s1), axis=1, keepdims=True)
        p0 = jnp.exp2(s0 - top).astype(BF)
        p1 = jnp.exp2(s1 - top).astype(BF)
        both = mm(p0, val0) + mm(p1, val1)
        total = both[:, 128:]
        outs.append(both[:, :128] / total)
        logs.append(top + jnp.log2(total))
    lane = lax.broadcasted_iota(jnp.int32, outs[0].shape, 1)
    both = jnp.where(lane < 64, outs[0], outs[1])
    o_ref[...] = both.astype(BF)
    full_ref[...] = both
    turned = jnp.where(lane < 64, logs[0], logs[1]).T
    lse_ref[0:4, :] = turned[0:4]
    lse_ref[4:8, :] = turned[64:68]


def attend(q, kv_own, kv_peer, frames):
    tokens, width = q.shape
    pairs = width // 128
    n = tokens // frames
    bq = min(512, n)
    nb = n // bq
    qs = pl.BlockSpec((bq, 128), lambda f, p, j: (f * nb + j, p))
    ks = pl.BlockSpec((n, 128), lambda f, p, j: (f, p))
    vs = pl.BlockSpec((n, 128), lambda f, p, j: (f, pairs + p))
    ls = pl.BlockSpec((8, bq), lambda f, p, j: (p, f * nb + j))
    return call(
        attend_kernel,
        "attend",
        (frames, pairs, nb),
        [(q, qs), (kv_own, ks), (kv_peer, ks), (kv_own, vs), (kv_peer, vs)],
        [
            (sds((tokens, width), BF), qs),
            (sds((tokens, width), F32), qs),
            (sds((pairs * 8, tokens), F32), ls),
        ],
        flops=50_000_000_000,
    )


def attend_back_kernel(
    q_ref, k0, k1, v0, v1, go_ref, o_ref, lse_ref, dq_ref, dk0, dk1, dv0, dv1, dka, dva
):
    j = pl.program_id(2)
    q = q_ref[...]
    go = go_ref[...]
    prod = (go.astype(F32) * o_ref[...]).T
    dq = None
    for part, (k, v) in enumerate(((k0, v0), (k1, v1))):
        keys = k[...]
        vals = v[...]
        turned = keys.T
        acc_v = acc_k = None
        for head in range(2):
            qm = of_head(q, head)
            gom = of_head(go, head)
            lse = lse_ref[4 * head : 4 * head + 1, :]
            delta = jnp.sum(prod[64 * head : 64 * head + 64], axis=0, keepdims=True)
            probs = jnp.exp2(mm(keys, qm, NT) - lse)
            ds = (probs * (mm(vals, gom, NT) - delta)).astype(BF)
            probs = probs.astype(BF)
            a = mm(probs, gom)
            b = mm(ds, qm)
            c = mm(of_head(turned, head, 0), ds)
            dq = c if dq is None else dq + c
            acc_v = a if acc_v is None else acc_v + a
            acc_k = b if acc_k is None else acc_k + b

        @pl.when(j == 0)
        def _():
            dva[part] = acc_v
            dka[part] = acc_k

        @pl.when(j > 0)
        def _():
            dva[part] += acc_v
            dka[part] += acc_k

    dq_ref[...] = (dq * SCALING).T.astype(BF)

    @pl.when(j == pl.num_programs(2) - 1)
    def _():
        back = SCALING / (SCALING * LOG2E)
        dk0[...] = (dka[0] * back).astype(BF)
        dk1[...] = (dka[1] * back).astype(BF)
        dv0[...] = dva[0].astype(BF)
        dv1[...] = dva[1].astype(BF)


def attend_back(q, kv_own, kv_peer, go, att, lse, frames, first, count, deps):
    tokens, width = q.shape
    pairs = width // 128
    n = tokens // frames
    bq = min(512, n)
    nb = n // bq
    qs = pl.BlockSpec((bq, 128), lambda f, p, j: (f * nb + j, first + p))
    ks = pl.BlockSpec((n, 128), lambda f, p, j: (f, first + p))
    vs = pl.BlockSpec((n, 128), lambda f, p, j: (f, pairs + first + p))
    ls = pl.BlockSpec((8, bq), lambda f, p, j: (first + p, f * nb + j))
    qo = pl.BlockSpec((bq, 128), lambda f, p, j: (f * nb + j, p))
    ko = pl.BlockSpec((n, 128), lambda f, p, j: (f, p))
    shape = jax.ShapeDtypeStruct((tokens, 128 * count), BF)
    return call(
        attend_back_kernel,
        "attend_back",
        (frames, count, nb),
        [(q, qs), (kv_own, ks), (kv_peer, ks), (kv_own, vs), (kv_peer, vs), (go, qs), (att, qs), (lse, ls)],
        [(shape, qo)] + [(shape, ko)] * 4,
        [pltpu.VMEM((2, n, 128), F32)] * 2,
        14_000_000_000 * count,
        deps,
    )


def normed_of(value):
    row_mean = jnp.mean(value, axis=-1, keepdims=True)
    centered = value - row_mean
    inverse = lax.rsqrt(jnp.mean(centered * centered, axis=-1, keepdims=True) + EPSILON)
    return centered * inverse, inverse


def norm_back(grad_hat, normed, inverse):
    first = jnp.mean(grad_hat, axis=-1, keepdims=True)
    second = jnp.mean(grad_hat * normed, axis=-1, keepdims=True)
    return inverse * (grad_hat - first - normed * second)


def rows_of(block, width):
    return pl.BlockSpec((block, width), lambda i: (i, 0))


def whole_of(shape):
    return pl.BlockSpec(shape, lambda i: (0,) * len(shape))


SMALL = pl.BlockSpec(memory_space=pltpu.SMEM)


def key_kernel(x_ref, chan_ref, shift_ref, gain_ref, wk, wv, h_ref, kv_ref):
    width = x_ref.shape[1]
    normed, inverse = normed_of(x_ref[...].astype(F32) + chan_ref[0])
    hidden = (normed * gain_ref[...] + shift_ref[0]).astype(BF)
    h_ref[...] = hidden
    kv_ref[:, :width] = mm(hidden, wk[...]).astype(BF)
    kv_ref[:, width:] = mm(hidden, wv[...]).astype(BF)


def keys_of(x, chan_add, shift, gain, weight, frames):
    count, width = x.shape
    block = 256
    per = count // frames // block
    frame = pl.BlockSpec((1, 1, width), lambda i: (i // per, 0, 0))
    return call(
        key_kernel,
        "keys",
        (count // block,),
        [
            (x, rows_of(block, width)),
            (chan_add, frame),
            (shift, frame),
            (gain, whole_of((1, width))),
            (weight, pl.BlockSpec((width, width), lambda i: (0, 1))),
            (weight, pl.BlockSpec((width, width), lambda i: (0, 2))),
        ],
        [
            (sds((count, width), BF), rows_of(block, width)),
            (sds((count, 2 * width), BF), rows_of(block, 2 * width)),
        ],
        flops=2_400_000_000,
    )


def query_kernel(h_ref, w, q_ref):
    q_ref[...] = (mm(h_ref[...], w[...]) * (SCALING * LOG2E)).astype(BF)


def queries_of(hidden, weight):
    count, width = hidden.shape
    block = 256
    return call(
        query_kernel,
        "queries",
        (count // block,),
        [(hidden, rows_of(block, width)), (weight, pl.BlockSpec((width, width), lambda i: (0, 0)))],
        [(sds((count, width), BF), rows_of(block, width))],
        flops=1_200_000_000,
    )[0]


ROOT = math.sqrt(2 / math.pi)
CUBE = ROOT * 0.044715


def gelu_both(x):
    square = x * x
    t = jnp.tanh(x * (ROOT + CUBE * square))
    half = 0.5 * t + 0.5
    slope = half + (0.5 * x) * (1.0 - t * t) * (ROOT + (3.0 * CUBE) * square)
    return x * half, slope


def mlp_kernel(
    x_ref,
    chan_ref,
    att_ref,
    g_ref,
    rows_ref,
    up_bias_ref,
    wo_any,
    wu_any,
    wd_any,
    res_ref,
    act_ref,
    gpre_ref,
    hid_ref,
    mid_ref,
    branch_ref,
    gatt_ref,
    sums_ref,
    wo,
    wu,
    wd,
    sems,
):
    step = pl.program_id(0)
    width = x_ref.shape[1]
    chunks = wu.shape[1] // width
    copies = [
        pltpu.make_async_copy(wo_any, wo, sems.at[0]),
        pltpu.make_async_copy(wu_any, wu, sems.at[1]),
        pltpu.make_async_copy(wd_any, wd, sems.at[2]),
    ]

    @pl.when(step == 0)
    def _():
        for c in copies:
            c.start()
        sums_ref[...] = jnp.zeros_like(sums_ref)
        copies[0].wait()

    out_bias, gain, shift, down_bias = [rows_ref[i : i + 1] for i in range(4)]
    middle = x_ref[...].astype(F32) + chan_ref[0] + mm(att_ref[...], wo[...]) + out_bias
    normed, inverse = normed_of(middle)
    hidden = (normed * gain + shift).astype(BF)
    hid_ref[...] = hidden
    g = g_ref[...]

    @pl.when(step == 0)
    def _():
        copies[1].wait()
        copies[2].wait()

    result = middle + down_bias
    grad_hidden = None
    for c in range(chunks):
        cols = pl.ds(c * width, width)
        act, slope = gelu_both(mm(hidden, wu[:, cols]) + up_bias_ref[:, cols])
        act = act.astype(BF)
        act_ref[:, cols] = act
        grad_pre = (mm(g, wd[cols, :], NT) * slope).astype(BF)
        gpre_ref[:, cols] = grad_pre
        sums_ref[4 + c : 5 + c] += jnp.sum(grad_pre.astype(F32), axis=0, keepdims=True)
        result = result + mm(act, wd[cols, :])
        part = mm(grad_pre, wu[:, cols], NT)
        grad_hidden = part if grad_hidden is None else grad_hidden + part
    res_ref[...] = result.astype(BF)
    g = g.astype(F32)
    sums_ref[0:1] += jnp.sum(g, axis=0, keepdims=True)
    sums_ref[1:2] += jnp.sum(grad_hidden * normed, axis=0, keepdims=True)
    sums_ref[2:3] += jnp.sum(grad_hidden, axis=0, keepdims=True)
    grad_middle = g + norm_back(grad_hidden * gain, normed, inverse)
    mid_ref[...] = grad_middle
    branch = grad_middle.astype(BF)
    branch_ref[...] = branch
    sums_ref[3:4] += jnp.sum(branch.astype(F32), axis=0, keepdims=True)
    gatt_ref[...] = mm(branch, wo[...], NT).astype(BF)


def mlp(x, chan_add, att, g, rows, up_bias, wo, wu, wd, frames):
    count, width = x.shape
    wide = wu.shape[1]
    block = 256
    per = count // frames // block
    narrow, broad = rows_of(block, width), rows_of(block, wide)
    anywhere = pl.BlockSpec(memory_space=pl.ANY)
    return call(
        mlp_kernel,
        "mlp",
        (count // block,),
        [
            (x, narrow),
            (chan_add, pl.BlockSpec((1, 1, width), lambda i: (i // per, 0, 0))),
            (att, narrow),
            (g, narrow),
            (rows, whole_of((4, width))),
            (up_bias, whole_of((1, wide))),
            (wo, anywhere),
            (wu, anywhere),
            (wd, anywhere),
        ],
        [
            (sds((count, width), BF), narrow),
            (sds((count, wide), BF), broad),
            (sds((count, wide), BF), broad),
            (sds((count, width), BF), narrow),
            (sds((count, width), F32), narrow),
            (sds((count, width), BF), narrow),
            (sds((count, width), BF), narrow),
            (sds((4 + wide // width, width), F32), whole_of((4 + wide // width, width))),
        ],
        [
            pltpu.VMEM(wo.shape, BF),
            pltpu.VMEM(wu.shape, BF),
            pltpu.VMEM(wd.shape, BF),
            pltpu.SemaphoreType.DMA((3,)),
        ],
        25_000_000_000,
    )


def down_grad_kernel(core_ref, act_ref, g_ref, send_ref, keep_ref, scr):
    core = core_ref[0]
    places, share, width = scr.shape[1:]
    scr[...] = mm(act_ref[...], g_ref[...], TN).reshape(scr.shape)
    keep_ref[...] = scr[:, core].astype(BF)
    send_ref[...] = scr[:, 1 - core].astype(BF)


def down_grad(core, act, g, lon):
    count, wide = act.shape
    width = g.shape[1]
    share = wide // lon
    tile = 384
    chips = tile // (2 * share)
    out = sds((lon // 2, share, width), BF)
    spec = pl.BlockSpec((chips, share, width), lambda i: (i, 0, 0))
    return call(
        down_grad_kernel,
        "down_grad",
        (wide // tile,),
        [(core, SMALL), (act, pl.BlockSpec((count, tile), lambda i: (0, i))), (g, whole_of((count, width)))],
        [(out, spec), (out, spec)],
        [pltpu.VMEM((chips, 2, share, width), F32)],
        4_800_000_000,
    )


def up_grad_kernel(core_ref, hid_ref, gpre_ref, att_ref, branch_ref, send_ref, keep_ref, turned, scr):
    core = core_ref[0]
    step = pl.program_id(0)
    last = pl.num_programs(0) - 1

    @pl.when(step == 0)
    def _():
        turned[...] = hid_ref[...].T

    @pl.when(step < last)
    def _():
        scr[...] = mm(turned[...], gpre_ref[...]).reshape(scr.shape)

    @pl.when(step == last)
    def _():
        scr[...] = mm(att_ref[...], branch_ref[...], TN).reshape(scr.shape)

    keep_ref[...] = scr[:, core].astype(BF)
    send_ref[...] = scr[:, 1 - core].astype(BF)


def up_grad(core, hidden, gpre, att, branch, lon):
    count, width = hidden.shape
    wide = gpre.shape[1]
    share = width // lon
    last = wide // width - 1
    out = sds((lon // 2, share, wide + width), BF)
    spec = pl.BlockSpec((lon // 2, share, width), lambda i: (0, 0, i))
    full = whole_of((count, width))
    return call(
        up_grad_kernel,
        "up_grad",
        (last + 2,),
        [
            (core, SMALL),
            (hidden, full),
            (gpre, pl.BlockSpec((count, width), lambda i: (0, jnp.minimum(i, last)))),
            (att, full),
            (branch, full),
        ],
        [(out, spec), (out, spec)],
        [pltpu.VMEM((width, count), BF), pltpu.VMEM((lon // 2, 2, share, width), F32)],
        6_000_000_000,
    )


def qkv_grad_kernel_of(start, stop):
    def kernel(core_ref, hid_ref, grad_ref, send_ref, keep_ref, scr):
        core = core_ref[0]
        scr[...] = mm(hid_ref[...], grad_ref[:, start:stop], TN).reshape(scr.shape)
        keep_ref[...] = scr[:, core].astype(BF)
        send_ref[...] = scr[:, 1 - core].astype(BF)

    return kernel


def qkv_grad(core, hidden, grad, start, stop, lon, deps=()):
    count, width = hidden.shape
    cols = stop - start
    share = width // lon
    out = sds((lon // 2, share, cols), BF)
    spec = whole_of((lon // 2, share, cols))
    return call(
        qkv_grad_kernel_of(start, stop),
        "qkv_grad",
        (1,),
        [(core, SMALL), (hidden, whole_of((count, width))), (grad, whole_of(grad.shape))],
        [(out, spec), (out, spec)],
        [pltpu.VMEM((lon // 2, 2, share, cols), F32)],
        1_800_000_000,
        deps,
    )


def first_back_kernel_of(groups, frame_blocks):
    def kernel(*refs):
        ins = refs[: 5 * groups]
        x_ref, chan_ref, gain_ref, mid_ref, w, patch_ref, qkv_ref, frame_ref, gain_sum = refs[5 * groups :]
        step = pl.program_id(0)
        width = x_ref.shape[1]
        at = 0
        for c in range(groups):
            dq, dk0, dv0, got_k, got_v = ins[5 * c : 5 * c + 5]
            size = dq.shape[1]
            qkv_ref[:, pl.ds(at, size)] = dq[...]
            qkv_ref[:, pl.ds(width + at, size)] = dk0[...] + got_k[...]
            qkv_ref[:, pl.ds(2 * width + at, size)] = dv0[...] + got_v[...]
            at += size
        grad_hidden = mm(qkv_ref[...], w[...], NT)
        normed, inverse = normed_of(x_ref[...].astype(F32) + chan_ref[0])
        grad_start = mid_ref[...] + norm_back(grad_hidden * gain_ref[...], normed, inverse)
        patch_ref[...] = grad_start.astype(BF)

        @pl.when(step == 0)
        def _():
            gain_sum[...] = jnp.zeros_like(gain_sum)

        @pl.when(lax.rem(step, frame_blocks) == 0)
        def _():
            frame_ref[...] = jnp.zeros_like(frame_ref)

        gain_sum[...] += jnp.sum(grad_hidden * normed, axis=0, keepdims=True)
        frame_ref[0, 0:1] += jnp.sum(grad_hidden, axis=0, keepdims=True)
        frame_ref[0, 1:2] += jnp.sum(grad_start, axis=0, keepdims=True)

    return kernel


def first_back(pieces, x, chan_add, gain, grad_middle, weight, frames):
    count, width = x.shape
    block = 256
    per = count // frames // block
    ins = [(a, rows_of(block, a.shape[1])) for group in pieces for a in group]
    return call(
        first_back_kernel_of(len(pieces), per),
        "first_back",
        (count // block,),
        ins
        + [
            (x, rows_of(block, width)),
            (chan_add, pl.BlockSpec((1, 1, width), lambda i: (i // per, 0, 0))),
            (gain, whole_of((1, width))),
            (grad_middle, rows_of(block, width)),
            (weight, whole_of(weight.shape)),
        ],
        [
            (sds((count, width), BF), rows_of(block, width)),
            (sds((count, 3 * width), BF), rows_of(block, 3 * width)),
            (sds((frames, 2, width), F32), pl.BlockSpec((1, 2, width), lambda i: (i // per, 0, 0))),
            (sds((1, width), F32), whole_of((1, width))),
        ],
        flops=3_600_000_000,
    )


def swap_pairs(size, bit):
    return [(i, i ^ (1 << bit)) for i in range(size)]


def bits_of(size):
    return size.bit_length() - 1


def my_bit(axis, bit):
    return ((lax.axis_index(axis) >> bit) & 1).astype(jnp.int32).reshape(1)


def swap(value, axis, bit):
    return lax.ppermute(value, axis, swap_pairs(lax.axis_size(axis), bit))


def add_kernel_of(kind):
    def kernel(mine_ref, kept_ref, got_ref, *outs):
        mine = mine_ref[0]

        def total(*at):
            return (kept_ref[at].astype(F32) + got_ref[at].astype(F32)).astype(BF)

        for which, ref in zip((1 - mine, mine), outs):
            if kind == "lead":
                ref[0] = total(which)
            elif kind == "rows":
                half = ref.shape[1]
                ref[...] = total(slice(None), pl.ds(pl.multiple_of(which * half, half), half))
            else:
                half = ref.shape[2]
                ref[...] = total(
                    slice(None), slice(None), pl.ds(pl.multiple_of(which * half, half), half)
                )

    return kernel


def add_split(kept, got, kind, mine, deps=()):
    lead, rows, cols = kept.shape
    size = 2 if lead > 1 else 1
    spec = pl.BlockSpec((size, rows, cols), lambda i: (i, 0, 0))
    if kind == "lead":
        part, half = (1, rows, cols), (lead // 2, rows, cols)
    elif kind == "rows":
        part, half = (size, rows // 2, cols), (lead, rows // 2, cols)
    else:
        part, half = (size, rows, cols // 2), (lead, rows, cols // 2)
    out = pl.BlockSpec(part, lambda i: (i, 0, 0))
    return call(
        add_kernel_of(kind),
        "add_" + kind,
        (lead // size,),
        [(mine, SMALL), (kept, spec), (got, spec)],
        [(sds(half, BF), out)] * 2,
        deps=deps,
    )


class Sum:
    def __init__(self, send, kept, stages, cut):
        self.kept, self.stages, self.cut = kept, list(stages), cut
        self.got = swap(send, "core", 0)
        self.final = None

    def advance(self, deps=()):
        if not self.stages:
            return ()
        axis, bit = self.stages.pop(0)
        kind = "lead" if axis == "chip" else self.cut
        send, self.kept = add_split(self.kept, self.got, kind, my_bit(axis, bit), deps)
        self.got = swap(send, axis, bit)
        return (self.kept,)

    def finish(self):
        while self.stages:
            self.advance()
        total = (self.kept.astype(F32) + self.got.astype(F32)).astype(BF)
        total = total.reshape(total.shape[-2:])
        lat = lax.axis_size("lat")
        if lat == 2:
            other = swap(total, "lat", 0)
            dim = 0 if self.cut == "rows" else 1
            total = jnp.where(
                lax.axis_index("lat") == 1,
                jnp.concatenate([other, total], dim),
                jnp.concatenate([total, other], dim),
            ).astype(F32)
        elif lat > 1:
            total = lax.psum(total.astype(F32), "lat")
        return total.astype(F32)


def stages_of(lat_at):
    chip = [("chip", bit) for bit in range(bits_of(lax.axis_size("chip")))]
    if lax.axis_size("lat") == 2:
        chip.insert(lat_at, ("lat", 0))
    return chip


def to_frames(value, chips):
    frames_all, patches, width = value.shape
    frames = frames_all // chips
    value = lax.all_to_all(value, ("lat", "chip"), 0, 0, tiled=True)
    if frames > 1:
        value = value.reshape(chips, frames, patches, width).swapaxes(0, 1)
    return value.reshape(-1, width)


def to_places(value, chips, frames_all):
    width = value.shape[-1]
    frames = frames_all // chips
    if frames > 1:
        value = value.reshape(frames, chips, -1, width).swapaxes(0, 1)
    value = value.reshape(frames_all, -1, width)
    return lax.all_to_all(value, ("lat", "chip"), 0, 0, tiled=True)


def on_device(
    tokens,
    channel_mask,
    lead_index,
    chan_embed,
    lead_embed,
    norm1_gain,
    norm1_bias,
    qkv_weight,
    out_weight,
    out_bias,
    norm2_gain,
    norm2_bias,
    up_weight,
    up_bias,
    down_weight,
    down_bias,
    cotangent,
):
    lat = lax.axis_size("lat")
    chips = lat * lax.axis_size("chip")
    lon = 2 * lax.axis_size("chip")
    frames_all, rows_here, cols_here, width = tokens.shape
    frames = frames_all // chips
    leads = lead_embed.shape[0]
    wide = up_weight.shape[1]
    share = width // lon
    place = (lax.axis_index("chip") * 2) + lax.axis_index("core")
    core = my_bit("core", 0)

    x = to_frames(tokens.reshape(frames_all, -1, width), chips)
    g = to_frames(cotangent.reshape(frames_all, -1, width), chips)
    count = x.shape[0]

    first = lax.axis_index(("lat", "chip")) * frames
    mask_here = lax.dynamic_slice_in_dim(channel_mask, first, frames, 0).astype(BF)
    lead_here = lax.dynamic_slice_in_dim(lead_index, first, frames, 0)
    lead_onehot = (lead_here[:, None] == jnp.arange(leads, dtype=jnp.int32)[None, :]).astype(BF)
    chan_add = mm(mask_here, chan_embed)[:, None, :]
    shift1 = (mm(lead_onehot, lead_embed) + norm1_bias.astype(F32))[:, None, :]
    gain1 = norm1_gain.astype(F32)[None]
    rows2 = jnp.stack([out_bias, norm2_gain, norm2_bias, down_bias]).astype(F32)

    hidden1, kv_own = keys_of(x, chan_add, shift1, gain1, qkv_weight, frames)
    kv_peer = swap(kv_own, "core", 0)
    queries = queries_of(hidden1, qkv_weight)
    attended, attended32, lse = attend(queries, kv_own, kv_peer, frames)

    result, activ, grad_pre, hidden2, grad_middle, grad_branch, grad_att, early = mlp(
        x,
        chan_add,
        attended,
        g,
        rows2,
        up_bias.astype(F32)[None],
        out_weight,
        up_weight,
        down_weight,
        frames,
    )
    out_patch = to_places(result, chips, frames_all)
    down_sum = Sum(*down_grad(core, activ, g, lon), stages_of(0), "rows")
    up_sum = Sum(*up_grad(core, hidden2, grad_pre, attended, grad_branch, lon), stages_of(1), "cols")

    pairs = width // 128
    plan = [2] + [1] * (pairs - 2)
    pieces, pair = [], 0
    marks = ()
    for size in plan:
        deps = down_sum.advance(marks) + up_sum.advance(marks)
        dq, dk0, dk1, dv0, dv1 = attend_back(
            queries, kv_own, kv_peer, grad_att, attended32, lse, frames, pair, size, deps
        )
        pieces.append((dq, dk0, dv0, swap(dk1, "core", 0), swap(dv1, "core", 0)))
        pair += size
        marks = (dq,)

    grad_start, grad_qkv, frame_sums, gain_sum = first_back(
        pieces, x, chan_add, gain1, grad_middle, qkv_weight, frames
    )
    grad_patch = to_places(grad_start, chips, frames_all)
    middle = 3 * width // 512 * 256
    first_half = qkv_grad(core, hidden1, grad_qkv, 0, middle, lon)
    other_half = qkv_grad(core, hidden1, grad_qkv, middle, 3 * width, lon)
    qkv_a = Sum(*first_half, stages_of(0), "cols")
    qkv_b = Sum(*other_half, stages_of(1), "cols")

    parts = wide // width
    early_up = early[4:].reshape(lon, parts, share).swapaxes(0, 1).reshape(parts, width)
    late = jnp.concatenate(
        [frame_sums.reshape(2 * frames, width), gain_sum, early[:4], early_up], 0
    )
    late = late.reshape(-1, lon // 2, 2, share)
    mine = core[0]
    late = lax.dynamic_index_in_dim(late, mine, 2, keepdims=False) + swap(
        lax.dynamic_index_in_dim(late, 1 - mine, 2, keepdims=False), "core", 0
    )
    late = late.reshape(1, late.shape[0], -1)
    for axis in ("chip", "lat"):
        for bit in range(bits_of(lax.axis_size(axis))):
            other = swap(late, axis, bit)
            high = my_bit(axis, bit)[0] == 1
            late = jnp.where(
                high, jnp.concatenate([other, late], 0), jnp.concatenate([late, other], 0)
            )
    late = lax.dynamic_slice_in_dim(late, lax.axis_index("chip") * share, share, 2)
    bias_of = late[:, 0 : 2 * frames : 2].reshape(frames_all, share)
    start_of = late[:, 1 : 2 * frames : 2].reshape(frames_all, share)
    rest = late[:, 2 * frames :].sum(0)
    hot = (lead_index[:, None] == jnp.arange(leads, dtype=jnp.int32)[None, :]).astype(F32)
    exact = lax.Precision.HIGHEST
    sum_lead = jnp.dot(hot.T, bias_of, precision=exact)
    sum_chan = jnp.dot(channel_mask.astype(F32).T, start_of, precision=exact)

    sum_down = down_sum.finish()
    sum_up = up_sum.finish()
    sum_qkv = jnp.concatenate([qkv_a.finish(), qkv_b.finish()], 1)
    shape = (frames_all, rows_here, cols_here, width)
    return (
        out_patch.reshape(shape),
        grad_patch.reshape(shape),
        sum_chan,
        sum_lead,
        rest[0],
        bias_of.sum(0),
        sum_qkv,
        sum_up[:, wide:],
        rest[4],
        rest[2],
        rest[3],
        sum_up[:, :wide],
        rest[5:].reshape(-1),
        sum_down,
        rest[1],
    )


def solution(mesh):
    lat, lon = mesh.shape["lat"], mesh.shape["lon"]
    fine = Mesh(mesh.devices.reshape(lat, lon // 2, 2), ("lat", "chip", "core"))
    places = P(None, "lat", ("chip", "core"), None)
    wide = ("chip", "core")
    return jax.shard_map(
        on_device,
        mesh=fine,
        in_specs=(places,) + (P(),) * 15 + (places,),
        out_specs=(
            places,
            places,
            P(None, wide),
            P(None, wide),
            P(wide),
            P(wide),
            P(wide, None),
            P(wide, None),
            P(wide),
            P(wide),
            P(wide),
            P(wide, None),
            P(wide),
            P(wide, None),
            P(wide),
        ),
        check_vma=False,
    )
```

```python
import functools
import math

import jax
import jax.numpy as jnp
from jax import lax
from jax.experimental import pallas as pl
from jax.experimental.pallas import tpu as pltpu
from jax.sharding import Mesh, PartitionSpec as P

HEADS = 12
EPSILON = 1e-06
SCALING = 0.125
LOG2E = math.log2(math.e)
F32 = jnp.float32
BF = jnp.bfloat16
NN = (((1,), (0,)), ((), ()))
NT = (((1,), (1,)), ((), ()))
TN = (((0,), (0,)), ((), ()))
KEY_CHUNK = 512
SMALLEST = 2.0**-90
VM_ATTEND = 48
VM_BACK = 56
VM_MLP = 48
VM_SUM = 56
COST = 50
DOWN_TILE = 768
MLP_BLOCK = 256


def mm(a, b, dims=NN):
    return lax.dot_general(a, b, dims, preferred_element_type=F32)


def of_head(value, head, axis=1):
    lane = lax.broadcasted_iota(jnp.int32, value.shape, axis)
    return jnp.where((lane // 64) == head, value, jnp.zeros_like(value))


def sds(shape, dtype):
    return jax.ShapeDtypeStruct(shape, dtype)


def call(kernel, name, grid, ins, outs, scratch=(), flops=0, deps=(), vmem=32):
    given, skipped = len(ins), len(deps)

    def body(*refs):
        kernel(*refs[:given], *refs[given + skipped :])

    anywhere = pl.BlockSpec(memory_space=pl.ANY)
    moved = sum(math.prod(a.shape) * a.dtype.itemsize for a, spec in list(ins) + list(outs))
    return pl.pallas_call(
        body,
        grid=grid,
        in_specs=[spec for a, spec in ins] + [anywhere] * skipped,
        out_specs=[spec for a, spec in outs],
        out_shape=[a for a, spec in outs],
        scratch_shapes=list(scratch),
        compiler_params=pltpu.CompilerParams(vmem_limit_bytes=vmem << 20),
        cost_estimate=pl.CostEstimate(flops=flops // COST, bytes_accessed=moved // COST, transcendentals=0),
        name=name,
    )(*[a for a, spec in ins], *deps)


def attend_kernel(q_ref, k0, k1, v0, v1, o_ref, full_ref, lse_ref):
    count = q_ref.shape[0]
    n = k0.shape[0]
    q = q_ref[...]
    wide_q = q.astype(F32)
    square_q = (wide_q * wide_q).astype(BF)
    turned, squares = [v0[...].T, v1[...].T], []
    for k in (k0, k1):
        wide_k = k[...].astype(F32)
        squares.append((wide_k * wide_k).astype(BF))
    chunk = min(KEY_CHUNK, n)

    def one_head(head, exact):
        qm = of_head(q, head)
        top = None
        if exact:
            for k in (k0, k1):
                for i in range(0, n, chunk):
                    part = jnp.max(mm(k[i : i + chunk], qm, NT), axis=0, keepdims=True)
                    top = part if top is None else jnp.maximum(top, part)
        else:
            pick = of_head(jnp.ones((8, 128), BF), head)
            for square in squares:
                part = jnp.max(mm(pick, square, NT))
                top = part if top is None else jnp.maximum(top, part)
            top = jnp.sqrt(mm(pick, square_q, NT)[0:1] * (top * 1.05))
        out = total = None
        for k, values in ((k0, turned[0]), (k1, turned[1])):
            for i in range(0, n, chunk):
                probs = jnp.exp2(mm(k[i : i + chunk], qm, NT) - top)
                part = jnp.sum(probs, axis=0, keepdims=True)
                total = part if total is None else total + part
                part = mm(values[64 * head : 64 * head + 64, i : i + chunk], probs.astype(BF))
                out = part if out is None else out + part
        lse = jnp.broadcast_to(top + jnp.log2(total), (64, count))
        return out / total, lse, jnp.min(total)

    def run(exact):
        first, second = one_head(0, exact), one_head(1, exact)
        out = jnp.concatenate([first[0], second[0]], 0).T
        o_ref[...] = out.astype(BF)
        full_ref[...] = out
        lse_ref[...] = jnp.concatenate([first[1], second[1]], 0).T
        return jnp.minimum(first[2], second[2])

    least = run(False)

    @pl.when(jnp.logical_not(least >= SMALLEST))
    def _():
        run(True)


def attend(q, kv_own, kv_peer, frames):
    tokens, width = q.shape
    pairs = width // 128
    n = tokens // frames
    qs = pl.BlockSpec((n, 128), lambda f, p: (f, p))
    vs = pl.BlockSpec((n, 128), lambda f, p: (f, pairs + p))
    return call(
        attend_kernel,
        "attend",
        (frames, pairs),
        [(q, qs), (kv_own, qs), (kv_peer, qs), (kv_own, vs), (kv_peer, vs)],
        [
            (sds((tokens, width), BF), qs),
            (sds((tokens, width), F32), qs),
            (sds((tokens, width), F32), qs),
        ],
        flops=30_000_000_000,
        vmem=VM_ATTEND,
    )


def attend_back_kernel(
    q_ref, k0, k1, v0, v1, go_ref, o_ref, lse_ref, dq_ref, dk0, dk1, dv0, dv1, dka, dva
):
    n = k0.shape[0]
    q = q_ref[...]
    go = go_ref[...]
    turned_q, turned_go = q.T, go.T
    prod = go.astype(F32) * o_ref[...]
    qms = [of_head(q, head) for head in range(2)]
    goms = [of_head(go, head) for head in range(2)]
    lses = [lse_ref[:, 64 * head : 64 * head + 1] for head in range(2)]
    deltas = [jnp.sum(of_head(prod, head), axis=1, keepdims=True) for head in range(2)]
    chunk = min(KEY_CHUNK, n)
    dq = None
    for part, (k, v) in enumerate(((k0, v0), (k1, v1))):
        for i in range(0, n, chunk):
            keys = k[i : i + chunk]
            vals = v[i : i + chunk]
            for head in range(2):
                lanes = slice(64 * head, 64 * head + 64)
                probs = jnp.exp2(mm(qms[head], keys, NT) - lses[head])
                ds = (probs * (mm(goms[head], vals, NT) - deltas[head])).astype(BF)
                dva[part, lanes, i : i + chunk] = mm(turned_go[lanes], probs.astype(BF))
                dka[part, lanes, i : i + chunk] = mm(turned_q[lanes], ds)
                term = mm(ds, of_head(keys, head))
                dq = term if dq is None else dq + term
    dq_ref[...] = (dq * SCALING).astype(BF)
    back = 1.0 / LOG2E
    for part, (dk, dv) in enumerate(((dk0, dv0), (dk1, dv1))):
        dk[...] = (dka[part].T * back).astype(BF)
        dv[...] = dva[part].T.astype(BF)


def attend_back(q, kv_own, kv_peer, go, att, lse, frames, first, count, deps):
    tokens, width = q.shape
    pairs = width // 128
    n = tokens // frames
    qs = pl.BlockSpec((n, 128), lambda f, p: (f, first + p))
    vs = pl.BlockSpec((n, 128), lambda f, p: (f, pairs + first + p))
    out = pl.BlockSpec((n, 128), lambda f, p: (f, p))
    shape = sds((tokens, 128 * count), BF)
    return call(
        attend_back_kernel,
        "attend_back",
        (frames, count),
        [(q, qs), (kv_own, qs), (kv_peer, qs), (kv_own, vs), (kv_peer, vs), (go, qs), (att, qs), (lse, qs)],
        [(shape, out)] * 5,
        [pltpu.VMEM((2, 128, n), F32)] * 2,
        11_000_000_000 * count,
        deps,
        VM_BACK,
    )


def normed_of(value):
    row_mean = jnp.mean(value, axis=-1, keepdims=True)
    centered = value - row_mean
    inverse = lax.rsqrt(jnp.mean(centered * centered, axis=-1, keepdims=True) + EPSILON)
    return centered * inverse, inverse


def norm_back(grad_hat, normed, inverse):
    first = jnp.mean(grad_hat, axis=-1, keepdims=True)
    second = jnp.mean(grad_hat * normed, axis=-1, keepdims=True)
    return inverse * (grad_hat - first - normed * second)


def rows_of(block, width):
    return pl.BlockSpec((block, width), lambda i: (i, 0))


def whole_of(shape):
    return pl.BlockSpec(shape, lambda i: (0,) * len(shape))


SMALL = pl.BlockSpec(memory_space=pltpu.SMEM)


def key_kernel(x_ref, chan_ref, shift_ref, gain_ref, wk, wv, h_ref, kv_ref):
    width = x_ref.shape[1]
    normed, inverse = normed_of(x_ref[...].astype(F32) + chan_ref[0])
    hidden = (normed * gain_ref[...] + shift_ref[0]).astype(BF)
    h_ref[...] = hidden
    kv_ref[:, :width] = mm(hidden, wk[...]).astype(BF)
    kv_ref[:, width:] = mm(hidden, wv[...]).astype(BF)


def keys_of(x, chan_add, shift, gain, weight, frames, deps):
    count, width = x.shape
    block = 256
    per = count // frames // block
    frame = pl.BlockSpec((1, 1, width), lambda i: (i // per, 0, 0))
    return call(
        key_kernel,
        "keys",
        (count // block,),
        [
            (x, rows_of(block, width)),
            (chan_add, frame),
            (shift, frame),
            (gain, whole_of((1, width))),
            (weight, pl.BlockSpec((width, width), lambda i: (0, 1))),
            (weight, pl.BlockSpec((width, width), lambda i: (0, 2))),
        ],
        [
            (sds((count, width), BF), rows_of(block, width)),
            (sds((count, 2 * width), BF), rows_of(block, 2 * width)),
        ],
        flops=2_400_000_000,
        deps=deps,
    )


def query_kernel(h_ref, w, q_ref):
    q_ref[...] = (mm(h_ref[...], w[...]) * (SCALING * LOG2E)).astype(BF)


def queries_of(hidden, weight):
    count, width = hidden.shape
    block = 256
    return call(
        query_kernel,
        "queries",
        (count // block,),
        [(hidden, rows_of(block, width)), (weight, pl.BlockSpec((width, width), lambda i: (0, 0)))],
        [(sds((count, width), BF), rows_of(block, width))],
        flops=1_200_000_000,
    )[0]


ROOT = math.sqrt(2 / math.pi)
CUBE = ROOT * 0.044715


def gelu_both(x):
    square = x * x
    t = jnp.tanh(x * (ROOT + CUBE * square))
    half = 0.5 * t + 0.5
    slope = half + (0.5 * x) * (1.0 - t * t) * (ROOT + (3.0 * CUBE) * square)
    return x * half, slope


def mlp_kernel(
    x_ref,
    chan_ref,
    att_ref,
    g_ref,
    rows_ref,
    up_bias_ref,
    wo_any,
    wu_any,
    wd_any,
    res_ref,
    act_ref,
    gpre_ref,
    hid_ref,
    mid_ref,
    branch_ref,
    gatt_ref,
    sums_ref,
    wo,
    wu,
    wd,
    sems,
):
    step = pl.program_id(0)
    width = x_ref.shape[1]
    chunks = wu.shape[1] // width
    copies = [
        pltpu.make_async_copy(wo_any, wo, sems.at[0]),
        pltpu.make_async_copy(wu_any, wu, sems.at[1]),
        pltpu.make_async_copy(wd_any, wd, sems.at[2]),
    ]

    @pl.when(step == 0)
    def _():
        for c in copies:
            c.start()
        sums_ref[...] = jnp.zeros_like(sums_ref)
        copies[0].wait()

    out_bias, gain, shift, down_bias = [rows_ref[i : i + 1] for i in range(4)]
    middle = x_ref[...].astype(F32) + chan_ref[0] + mm(att_ref[...], wo[...]) + out_bias
    normed, inverse = normed_of(middle)
    hidden = (normed * gain + shift).astype(BF)
    hid_ref[...] = hidden
    g = g_ref[...]

    @pl.when(step == 0)
    def _():
        copies[1].wait()
        copies[2].wait()

    result = middle + down_bias
    grad_hidden = None
    for c in range(chunks):
        cols = pl.ds(c * width, width)
        act, slope = gelu_both(mm(hidden, wu[:, cols]) + up_bias_ref[:, cols])
        act = act.astype(BF)
        act_ref[:, cols] = act
        grad_pre = (mm(g, wd[cols, :], NT) * slope).astype(BF)
        gpre_ref[:, cols] = grad_pre
        sums_ref[4 + c : 5 + c] += jnp.sum(grad_pre.astype(F32), axis=0, keepdims=True)
        result = result + mm(act, wd[cols, :])
        part = mm(grad_pre, wu[:, cols], NT)
        grad_hidden = part if grad_hidden is None else grad_hidden + part
    res_ref[...] = result.astype(BF)
    g = g.astype(F32)
    sums_ref[0:1] += jnp.sum(g, axis=0, keepdims=True)
    sums_ref[1:2] += jnp.sum(grad_hidden * normed, axis=0, keepdims=True)
    sums_ref[2:3] += jnp.sum(grad_hidden, axis=0, keepdims=True)
    grad_middle = g + norm_back(grad_hidden * gain, normed, inverse)
    mid_ref[...] = grad_middle
    branch = grad_middle.astype(BF)
    branch_ref[...] = branch
    sums_ref[3:4] += jnp.sum(branch.astype(F32), axis=0, keepdims=True)
    gatt_ref[...] = mm(branch, wo[...], NT).astype(BF)


def mlp(x, chan_add, att, g, rows, up_bias, wo, wu, wd, frames):
    count, width = x.shape
    wide = wu.shape[1]
    block = MLP_BLOCK
    per = count // frames // block
    narrow, broad = rows_of(block, width), rows_of(block, wide)
    anywhere = pl.BlockSpec(memory_space=pl.ANY)
    return call(
        mlp_kernel,
        "mlp",
        (count // block,),
        [
            (x, narrow),
            (chan_add, pl.BlockSpec((1, 1, width), lambda i: (i // per, 0, 0))),
            (att, narrow),
            (g, narrow),
            (rows, whole_of((4, width))),
            (up_bias, whole_of((1, wide))),
            (wo, anywhere),
            (wu, anywhere),
            (wd, anywhere),
        ],
        [
            (sds((count, width), BF), narrow),
            (sds((count, wide), BF), broad),
            (sds((count, wide), BF), broad),
            (sds((count, width), BF), narrow),
            (sds((count, width), F32), narrow),
            (sds((count, width), BF), narrow),
            (sds((count, width), BF), narrow),
            (sds((4 + wide // width, width), F32), whole_of((4 + wide // width, width))),
        ],
        [
            pltpu.VMEM(wo.shape, BF),
            pltpu.VMEM(wu.shape, BF),
            pltpu.VMEM(wd.shape, BF),
            pltpu.SemaphoreType.DMA((3,)),
        ],
        25_000_000_000,
        vmem=VM_MLP,
    )


def down_grad_kernel(core_ref, act_ref, g_ref, send_ref, keep_ref, scr):
    core = core_ref[0]
    places, share, width = scr.shape[1:]
    scr[...] = mm(act_ref[...], g_ref[...], TN).reshape(scr.shape)
    keep_ref[...] = scr[:, core].astype(BF)
    send_ref[...] = scr[:, 1 - core].astype(BF)


def down_grad(core, act, g, lon, deps):
    count, wide = act.shape
    width = g.shape[1]
    share = wide // lon
    tile = DOWN_TILE
    chips = tile // (2 * share)
    out = sds((lon // 2, share, width), BF)
    spec = pl.BlockSpec((chips, share, width), lambda i: (i, 0, 0))
    return call(
        down_grad_kernel,
        "down_grad",
        (wide // tile,),
        [(core, SMALL), (act, pl.BlockSpec((count, tile), lambda i: (0, i))), (g, whole_of((count, width)))],
        [(out, spec), (out, spec)],
        [pltpu.VMEM((chips, 2, share, width), F32)],
        4_800_000_000,
        deps,
        VM_SUM,
    )


def up_grad_kernel(core_ref, hid_ref, gpre_ref, att_ref, branch_ref, send_ref, keep_ref, turned, scr):
    core = core_ref[0]
    step = pl.program_id(0)
    last = pl.num_programs(0) - 1

    @pl.when(step == 0)
    def _():
        turned[...] = hid_ref[...].T

    @pl.when(step < last)
    def _():
        scr[...] = mm(turned[...], gpre_ref[...]).reshape(scr.shape)

    @pl.when(step == last)
    def _():
        scr[...] = mm(att_ref[...], branch_ref[...], TN).reshape(scr.shape)

    keep_ref[...] = scr[:, core].astype(BF)
    send_ref[...] = scr[:, 1 - core].astype(BF)


def up_grad(core, hidden, gpre, att, branch, lon):
    count, width = hidden.shape
    wide = gpre.shape[1]
    share = width // lon
    last = wide // width - 1
    out = sds((lon // 2, share, wide + width), BF)
    spec = pl.BlockSpec((lon // 2, share, width), lambda i: (0, 0, i))
    full = whole_of((count, width))
    return call(
        up_grad_kernel,
        "up_grad",
        (last + 2,),
        [
            (core, SMALL),
            (hidden, full),
            (gpre, pl.BlockSpec((count, width), lambda i: (0, jnp.minimum(i, last)))),
            (att, full),
            (branch, full),
        ],
        [(out, spec), (out, spec)],
        [pltpu.VMEM((width, count), BF), pltpu.VMEM((lon // 2, 2, share, width), F32)],
        6_000_000_000,
        vmem=VM_SUM,
    )


def qkv_grad_kernel(core_ref, hid_ref, grad_ref, send_ref, keep_ref, turned, scr):
    core = core_ref[0]

    @pl.when(pl.program_id(0) == 0)
    def _():
        turned[...] = hid_ref[...].T

    scr[...] = mm(turned[...], grad_ref[...]).reshape(scr.shape)
    keep_ref[...] = scr[:, core].astype(BF)
    send_ref[...] = scr[:, 1 - core].astype(BF)


def qkv_grad(core, hidden, grad, lon, deps):
    count, width = hidden.shape
    share = width // lon
    out = sds((lon // 2, share, grad.shape[1]), BF)
    spec = pl.BlockSpec((lon // 2, share, width), lambda i: (0, 0, i))
    return call(
        qkv_grad_kernel,
        "qkv_grad",
        (grad.shape[1] // width,),
        [
            (core, SMALL),
            (hidden, whole_of((count, width))),
            (grad, pl.BlockSpec((count, width), lambda i: (0, i))),
        ],
        [(out, spec), (out, spec)],
        [pltpu.VMEM((width, count), BF), pltpu.VMEM((lon // 2, 2, share, width), F32)],
        3_600_000_000,
        deps,
        VM_SUM,
    )


def first_back_kernel_of(groups, frame_blocks):
    def kernel(*refs):
        ins = refs[: 5 * groups]
        x_ref, chan_ref, gain_ref, mid_ref, w, patch_ref, qkv_ref, frame_ref, gain_sum = refs[5 * groups :]
        step = pl.program_id(0)
        width = x_ref.shape[1]
        at = 0
        for c in range(groups):
            dq, dk0, dv0, got_k, got_v = ins[5 * c : 5 * c + 5]
            size = dq.shape[1]
            qkv_ref[:, pl.ds(at, size)] = dq[...]
            qkv_ref[:, pl.ds(width + at, size)] = dk0[...] + got_k[...]
            qkv_ref[:, pl.ds(2 * width + at, size)] = dv0[...] + got_v[...]
            at += size
        grad_hidden = mm(qkv_ref[...], w[...], NT)
        normed, inverse = normed_of(x_ref[...].astype(F32) + chan_ref[0])
        grad_start = mid_ref[...] + norm_back(grad_hidden * gain_ref[...], normed, inverse)
        patch_ref[...] = grad_start.astype(BF)

        @pl.when(step == 0)
        def _():
            gain_sum[...] = jnp.zeros_like(gain_sum)

        @pl.when(lax.rem(step, frame_blocks) == 0)
        def _():
            frame_ref[...] = jnp.zeros_like(frame_ref)

        gain_sum[...] += jnp.sum(grad_hidden * normed, axis=0, keepdims=True)
        frame_ref[0, 0:1] += jnp.sum(grad_hidden, axis=0, keepdims=True)
        frame_ref[0, 1:2] += jnp.sum(grad_start, axis=0, keepdims=True)

    return kernel


def first_back(pieces, x, chan_add, gain, grad_middle, weight, frames, deps):
    count, width = x.shape
    block = 256
    per = count // frames // block
    ins = [(a, rows_of(block, a.shape[1])) for group in pieces for a in group]
    return call(
        first_back_kernel_of(len(pieces), per),
        "first_back",
        (count // block,),
        ins
        + [
            (x, rows_of(block, width)),
            (chan_add, pl.BlockSpec((1, 1, width), lambda i: (i // per, 0, 0))),
            (gain, whole_of((1, width))),
            (grad_middle, rows_of(block, width)),
            (weight, whole_of(weight.shape)),
        ],
        [
            (sds((count, width), BF), rows_of(block, width)),
            (sds((count, 3 * width), BF), rows_of(block, 3 * width)),
            (sds((frames, 2, width), F32), pl.BlockSpec((1, 2, width), lambda i: (i // per, 0, 0))),
            (sds((1, width), F32), whole_of((1, width))),
        ],
        flops=3_600_000_000,
        deps=deps,
        vmem=VM_SUM,
    )


def swap_pairs(size, bit):
    return [(i, i ^ (1 << bit)) for i in range(size)]


def bits_of(size):
    return size.bit_length() - 1


def my_bit(axis, bit):
    return ((lax.axis_index(axis) >> bit) & 1).astype(jnp.int32).reshape(1)


def swap(value, axis, bit):
    return lax.ppermute(value, axis, swap_pairs(lax.axis_size(axis), bit))


def cross(value, turn):
    pairs = []
    for i in range(8):
        lat_next = (i & 1) == turn
        pairs.append((i, i ^ (4 if lat_next else 2)))
    return lax.ppermute(value, ("lat", "yy", "core"), pairs)


def both(kept_ref, got_ref, *at):
    return (kept_ref[at].astype(F32) + got_ref[at].astype(F32)).astype(BF)


def mlp_part(ins, out, at, yy, half):
    kept_d, got_d, kept_u, got_u = ins
    rows, width = kept_d.shape[1:]
    share = kept_u.shape[1]
    wide = kept_u.shape[2] - width

    @pl.when(half == 0)
    def _():
        out[0, at, :rows] = both(kept_d, got_d, yy)
        out[0, at, rows:] = both(kept_u, got_u, yy, slice(None), slice(wide, None))

    @pl.when(half == 1)
    def _():
        for c in range(wide // width):
            out[0, at, c * share : (c + 1) * share] = both(
                kept_u, got_u, yy, slice(None), slice(c * width, (c + 1) * width)
            )
        out[0, at, rows:] = jnp.zeros((share, width), BF)


def qkv_part(ins, out, at, yy, half):
    kept, got = ins
    cols = kept.shape[2] // 2
    for side in range(2):

        @pl.when(half == side)
        def _():
            out[0, at] = both(kept, got, yy, slice(None), slice(side * cols, (side + 1) * cols))


def first_add(part, ins, rows, cols, deps=()):
    zed = ins[0].shape[0] // 2

    def kernel(where_ref, *refs):
        core, mine = where_ref[0], where_ref[1]
        for which, out in zip((1 - mine, mine), refs[len(ins) :]):
            for at in range(2):
                yy = jnp.where(core == 0, at, which)
                half = jnp.where(core == 0, which, at)
                part(refs[: len(ins)], out, at, yy, half)

    core = my_bit("core", 0)
    mine = jnp.where(core == 0, my_bit("lat", 0), my_bit("yy", 0))
    out = sds((zed, 2, rows, cols), BF)
    spec = pl.BlockSpec((1, 2, rows, cols), lambda i: (i, 0, 0, 0))
    return call(
        kernel,
        "first_add",
        (zed,),
        [(jnp.concatenate([core, mine]), SMALL)]
        + [(a, pl.BlockSpec((2,) + a.shape[1:], lambda i: (i, 0, 0))) for a in ins],
        [(out, spec)] * 2,
        deps=deps,
        vmem=VM_SUM,
    )


def second_add(kept, got, deps=()):
    zed, two, rows, cols = kept.shape

    def kernel(mine_ref, kept_ref, got_ref, send_ref, keep_ref):
        mine = mine_ref[0]
        send_ref[0] = both(kept_ref, got_ref, 0, 1 - mine)
        keep_ref[0] = both(kept_ref, got_ref, 0, mine)

    mine = jnp.where(my_bit("core", 0) == 0, my_bit("yy", 0), my_bit("lat", 0))
    spec = pl.BlockSpec((1, 2, rows, cols), lambda i: (i, 0, 0, 0))
    out = pl.BlockSpec((1, rows, cols), lambda i: (i, 0, 0))
    return call(
        kernel,
        "second_add",
        (zed,),
        [(mine, SMALL), (kept, spec), (got, spec)],
        [(sds((zed, rows, cols), BF), out)] * 2,
        deps=deps,
        vmem=VM_SUM,
    )


def third_add(kept, got, deps=()):
    zed, rows, cols = kept.shape

    def kernel(me_ref, kept_ref, got_ref, *outs):
        for up, out in enumerate(outs):
            out[...] = both(kept_ref, got_ref, lax.rem(me_ref[0] + up, zed))

    me = lax.axis_index("zed").astype(jnp.int32).reshape(1)
    return call(
        kernel,
        "third_add",
        (1,),
        [(me, SMALL), (kept, whole_of(kept.shape)), (got, whole_of(kept.shape))],
        [(sds((rows, cols), BF), whole_of((rows, cols)))] * zed,
        deps=deps,
        vmem=VM_SUM,
    )


def cut_lead(kept, got, bit, deps=()):
    zed, rows, cols = kept.shape

    def kernel(mine_ref, kept_ref, got_ref, send_ref, keep_ref):
        mine = mine_ref[0]
        send_ref[0] = both(kept_ref, got_ref, 1 - mine)
        keep_ref[0] = both(kept_ref, got_ref, mine)

    spec = pl.BlockSpec((2, rows, cols), lambda i: (i, 0, 0))
    out = pl.BlockSpec((1, rows, cols), lambda i: (i, 0, 0))
    return call(
        kernel,
        "cut_lead",
        (zed // 2,),
        [(my_bit("zed", bit), SMALL), (kept, spec), (got, spec)],
        [(sds((zed // 2, rows, cols), BF), out)] * 2,
        deps=deps,
        vmem=VM_SUM,
    )


def up_zed(value, up):
    zed = lax.axis_size("zed")
    return lax.ppermute(value, "zed", [(i, (i + up) % zed) for i in range(zed)])


def last_add(parts, deps=()):
    rows, cols = parts[0].shape

    def kernel(*refs):
        total = refs[0][...].astype(F32)
        for ref in refs[1:-1]:
            total = total + ref[...].astype(F32)
        refs[-1][...] = total.astype(BF)

    spec = whole_of((rows, cols))
    return call(
        kernel,
        "last_add",
        (1,),
        [(a, spec) for a in parts],
        [(sds((rows, cols), BF), spec)],
        deps=deps,
        vmem=VM_SUM,
    )[0]


def halves_of(mine):
    other = swap(mine, "lat", 0)
    high = lax.axis_index("lat") == 1
    return jnp.where(high, other, mine).astype(F32), jnp.where(high, mine, other).astype(F32)


def held(value, deps):
    def kernel(value_ref, out_ref):
        out_ref[...] = value_ref[...]

    spec = whole_of(value.shape)
    return call(
        kernel, "held", (1,), [(value, spec)], [(sds(value.shape, value.dtype), spec)], deps=deps
    )[0]


def plain_sum(kept, got):
    value = lax.psum_scatter(kept + got, ("zed", "yy"), scatter_dimension=0, tiled=True)[0]
    return lax.psum(value.astype(F32), "lat")


def to_frames(value, chips):
    frames_all, patches, width = value.shape
    frames = frames_all // chips
    value = lax.all_to_all(value, ("lat", "zed", "yy"), 0, 0, tiled=True)
    if frames > 1:
        value = value.reshape(chips, frames, patches, width).swapaxes(0, 1)
    return value.reshape(-1, width)


def to_places(value, chips, frames_all):
    width = value.shape[-1]
    frames = frames_all // chips
    if frames > 1:
        value = value.reshape(frames, chips, -1, width).swapaxes(0, 1)
    value = value.reshape(frames_all, -1, width)
    return lax.all_to_all(value, ("lat", "zed", "yy"), 0, 0, tiled=True)


def on_device(
    tokens,
    channel_mask,
    lead_index,
    chan_embed,
    lead_embed,
    norm1_gain,
    norm1_bias,
    qkv_weight,
    out_weight,
    out_bias,
    norm2_gain,
    norm2_bias,
    up_weight,
    up_bias,
    down_weight,
    down_bias,
    cotangent,
):
    lat = lax.axis_size("lat")
    lon = 4 * lax.axis_size("zed")
    chips = lat * (lon // 2)
    frames_all, rows_here, cols_here, width = tokens.shape
    frames = frames_all // chips
    leads = lead_embed.shape[0]
    wide = up_weight.shape[1]
    share = width // lon
    core = my_bit("core", 0)

    x = to_frames(tokens.reshape(frames_all, -1, width), chips)
    flat = cotangent.reshape(frames_all, -1, width)
    g = to_frames(flat, chips)
    count = x.shape[0]

    first = lax.axis_index(("lat", "zed", "yy")) * frames
    mask_here = lax.dynamic_slice_in_dim(channel_mask, first, frames, 0).astype(BF)
    lead_here = lax.dynamic_slice_in_dim(lead_index, first, frames, 0)
    lead_onehot = (lead_here[:, None] == jnp.arange(leads, dtype=jnp.int32)[None, :]).astype(BF)
    chan_add = mm(mask_here, chan_embed)[:, None, :]
    shift1 = (mm(lead_onehot, lead_embed) + norm1_bias.astype(F32))[:, None, :]
    gain1 = norm1_gain.astype(F32)[None]
    rows2 = jnp.stack([out_bias, norm2_gain, norm2_bias, down_bias]).astype(F32)

    hidden1, kv_own = keys_of(x, chan_add, shift1, gain1, qkv_weight, frames, (flat,))
    kv_peer = swap(kv_own, "core", 0)
    queries = queries_of(hidden1, qkv_weight)
    attended, attended32, lse = attend(queries, kv_own, kv_peer, frames)

    result, activ, grad_pre, hidden2, grad_middle, grad_branch, grad_att, early = mlp(
        x,
        chan_add,
        attended,
        g,
        rows2,
        up_bias.astype(F32)[None],
        out_weight,
        up_weight,
        down_weight,
        frames,
    )
    out_patch = to_places(result, chips, frames_all)
    up_send, up_kept = up_grad(core, hidden2, grad_pre, attended, grad_branch, lon)
    up_got = swap(up_send, "core", 0)
    down_send, down_kept = down_grad(core, activ, g, lon, (up_send,))
    down_got = swap(down_send, "core", 0)

    staged = lat == 2
    rows = down_kept.shape[1] + share
    pieces, pair = [], 0
    deps = (down_kept,)
    if staged:
        sent, kept = first_add(mlp_part, [down_kept, down_got, up_kept, up_got], rows, width)
        got = cross(sent, 0)
        deps = (sent,)
    pairs = width // 128
    plan = [pairs // 2, (pairs + 1) // 3, pairs - pairs // 2 - (pairs + 1) // 3]
    for at, size in enumerate(plan):
        dq, dk0, dk1, dv0, dv1 = attend_back(
            queries, kv_own, kv_peer, grad_att, attended32, lse, frames, pair, size, deps
        )
        pieces.append((dq, dk0, dv0, swap(dk1, "core", 0), swap(dv1, "core", 0)))
        pair += size
        deps = (dq,)
        if staged and at == 0:
            sent, kept = second_add(kept, got, deps)
            got = cross(sent, 1)
            deps = (sent, dq)
        if staged and at == 1:
            sent, kept = cut_lead(kept, got, 0, deps)
            got = swap(sent, "zed", 0)
            deps = (sent, dq)
        if at == 1:
            deps = deps + (out_patch,)

    if staged:
        for bit in range(1, bits_of(lax.axis_size("zed"))):
            sent, kept = cut_lead(kept, got, bit, deps)
            got = swap(sent, "zed", bit)
            deps = (sent,)
        mlp_parts = [kept[0], got[0]]
    grad_start, grad_qkv, frame_sums, gain_sum = first_back(
        pieces, x, chan_add, gain1, grad_middle, qkv_weight, frames, deps
    )
    grad_patch = to_places(grad_start, chips, frames_all)

    ups = wide // width
    early_up = early[4:].reshape(lon, ups, share).swapaxes(0, 1).reshape(ups, width)
    late = jnp.concatenate(
        [frame_sums.reshape(2 * frames, width), gain_sum, early[:4], early_up], 0
    )
    late = late.reshape(-1, lon // 2, 2, share)
    mine = core[0]
    late_got = swap(lax.dynamic_index_in_dim(late, 1 - mine, 2, keepdims=False), "core", 0)
    late = lax.dynamic_index_in_dim(late, mine, 2, keepdims=False) + late_got

    deps = (late_got,)
    qkv_send, qkv_kept = qkv_grad(core, hidden1, grad_qkv, lon, deps)
    qkv_got = swap(qkv_send, "core", 0)

    zed = lax.axis_size("zed")

    if staged:
        sent, kept = first_add(qkv_part, [qkv_kept, qkv_got], share, 3 * width // 2)
        got = cross(sent, 0)
        sent, kept = second_add(kept, got, (grad_patch, mlp_parts[1]))
        got = cross(sent, 1)
        parts = third_add(kept, got)
        late = held(late, (parts[0],))
        parts = [parts[0]] + [up_zed(part, up) for up, part in enumerate(parts) if up]
        halves = halves_of(last_add(mlp_parts, (parts[0],)))
        sum_down, sum_out = halves[0][: rows - share], halves[0][rows - share :]
        sum_up = jnp.concatenate(
            [halves[1][c * share : (c + 1) * share] for c in range(wide // width)], 1
        )
        sum_qkv = jnp.concatenate(halves_of(last_add(parts)), 1)
    else:
        sum_down = plain_sum(down_kept, down_got)
        sum_up = plain_sum(up_kept, up_got)
        sum_up, sum_out = sum_up[:, :wide], sum_up[:, wide:]
        sum_qkv = plain_sum(qkv_kept, qkv_got)

    late = late.reshape(1, late.shape[0], -1)
    for axis in ("yy", "lat"):
        for bit in range(bits_of(lax.axis_size(axis))):
            other = swap(late, axis, bit)
            high = my_bit(axis, bit)[0] == 1
            late = jnp.where(
                high, jnp.concatenate([other, late], 0), jnp.concatenate([late, other], 0)
            )
    late = jnp.stack([late] + [up_zed(late, up) for up in range(1, zed)])
    late = jnp.take(late, (lax.axis_index("zed") - jnp.arange(zed)) % zed, axis=0)
    late = lax.dynamic_slice_in_dim(late, lax.axis_index(("zed", "yy")) * share, share, 3)
    late = late.reshape(zed, lat, 2, -1, share).swapaxes(0, 1).reshape(chips, -1, share)
    bias_of = late[:, 0 : 2 * frames : 2].reshape(frames_all, share)
    start_of = late[:, 1 : 2 * frames : 2].reshape(frames_all, share)
    rest = late[:, 2 * frames :].sum(0)
    hot = (lead_index[:, None] == jnp.arange(leads, dtype=jnp.int32)[None, :]).astype(F32)
    exact = lax.Precision.HIGHEST
    sum_lead = jnp.dot(hot.T, bias_of, precision=exact)
    sum_chan = jnp.dot(channel_mask.astype(F32).T, start_of, precision=exact)

    shape = (frames_all, rows_here, cols_here, width)
    return (
        out_patch.reshape(shape),
        grad_patch.reshape(shape),
        sum_chan,
        sum_lead,
        rest[0],
        bias_of.sum(0),
        sum_qkv,
        sum_out,
        rest[4],
        rest[2],
        rest[3],
        sum_up,
        rest[5:].reshape(-1),
        sum_down,
        rest[1],
    )


def solution(mesh):
    lat, lon = mesh.shape["lat"], mesh.shape["lon"]
    fine = Mesh(mesh.devices.reshape(lat, lon // 4, 2, 2), ("lat", "zed", "yy", "core"))
    wide = ("zed", "yy", "core")
    places = P(None, "lat", wide, None)
    return jax.shard_map(
        on_device,
        mesh=fine,
        in_specs=(places,) + (P(),) * 15 + (places,),
        out_specs=(
            places,
            places,
            P(None, wide),
            P(None, wide),
            P(wide),
            P(wide),
            P(wide, None),
            P(wide, None),
            P(wide),
            P(wide),
            P(wide),
            P(wide, None),
            P(wide),
            P(wide, None),
            P(wide),
        ),
        check_vma=False,
    )
```

```python
import functools
import math

import jax
import jax.numpy as jnp
from jax import lax
from jax.experimental import pallas as pl
from jax.experimental.pallas import tpu as pltpu
from jax.sharding import Mesh, PartitionSpec as P

HEADS = 12
EPSILON = 1e-06
SCALING = 0.125
LOG2E = math.log2(math.e)
F32 = jnp.float32
BF = jnp.bfloat16
NN = (((1,), (0,)), ((), ()))
NT = (((1,), (1,)), ((), ()))
TN = (((0,), (0,)), ((), ()))
KEY_CHUNK = 512
SMALLEST = 2.0**-90
VM_ATTEND = 48
VM_BACK = 56
VM_MLP = 62
VM_SUM = 56
VM_QKV = 32
COST = 50
DOWN_TILE = 768
MLP_BLOCK = 512
MLP_SPLIT = 1


def mm(a, b, dims=NN):
    return lax.dot_general(a, b, dims, preferred_element_type=F32)


def of_head(value, head, axis=1):
    lane = lax.broadcasted_iota(jnp.int32, value.shape, axis)
    return jnp.where((lane // 64) == head, value, jnp.zeros_like(value))


def sds(shape, dtype):
    return jax.ShapeDtypeStruct(shape, dtype)


def call(kernel, name, grid, ins, outs, scratch=(), flops=0, deps=(), vmem=32):
    given, skipped = len(ins), len(deps)

    def body(*refs):
        kernel(*refs[:given], *refs[given + skipped :])

    anywhere = pl.BlockSpec(memory_space=pl.ANY)
    moved = sum(math.prod(a.shape) * a.dtype.itemsize for a, spec in list(ins) + list(outs))
    return pl.pallas_call(
        body,
        grid=grid,
        in_specs=[spec for a, spec in ins] + [anywhere] * skipped,
        out_specs=[spec for a, spec in outs],
        out_shape=[a for a, spec in outs],
        scratch_shapes=list(scratch),
        compiler_params=pltpu.CompilerParams(vmem_limit_bytes=vmem << 20),
        cost_estimate=pl.CostEstimate(flops=flops // COST, bytes_accessed=moved // COST, transcendentals=0),
        name=name,
    )(*[a for a, spec in ins], *deps)


def attend_kernel(q_ref, k0, k1, v0, v1, o_ref, full_ref, lse_ref):
    count = q_ref.shape[0]
    n = k0.shape[0]
    q = q_ref[...]
    wide_q = q.astype(F32)
    square_q = (wide_q * wide_q).astype(BF)
    turned, squares = [v0[...].T, v1[...].T], []
    for k in (k0, k1):
        wide_k = k[...].astype(F32)
        squares.append((wide_k * wide_k).astype(BF))
    chunk = min(KEY_CHUNK, n)

    def one_head(head, exact):
        qm = of_head(q, head)
        top = None
        if exact:
            for k in (k0, k1):
                for i in range(0, n, chunk):
                    part = jnp.max(mm(k[i : i + chunk], qm, NT), axis=0, keepdims=True)
                    top = part if top is None else jnp.maximum(top, part)
        else:
            pick = of_head(jnp.ones((8, 128), BF), head)
            for square in squares:
                part = jnp.max(mm(pick, square, NT))
                top = part if top is None else jnp.maximum(top, part)
            top = jnp.sqrt(mm(pick, square_q, NT)[0:1] * (top * 1.05))
        out = total = None
        for k, values in ((k0, turned[0]), (k1, turned[1])):
            for i in range(0, n, chunk):
                probs = jnp.exp2(mm(k[i : i + chunk], qm, NT) - top)
                part = jnp.sum(probs, axis=0, keepdims=True)
                total = part if total is None else total + part
                part = mm(values[64 * head : 64 * head + 64, i : i + chunk], probs.astype(BF))
                out = part if out is None else out + part
        lse = jnp.broadcast_to(top + jnp.log2(total), (64, count))
        return out / total, lse, jnp.min(total)

    def run(exact):
        first, second = one_head(0, exact), one_head(1, exact)
        out = jnp.concatenate([first[0], second[0]], 0).T
        o_ref[...] = out.astype(BF)
        full_ref[...] = out
        lse_ref[...] = jnp.concatenate([first[1], second[1]], 0).T
        return jnp.minimum(first[2], second[2])

    least = run(False)

    @pl.when(jnp.logical_not(least >= SMALLEST))
    def _():
        run(True)


def attend(q, kv_own, kv_peer, frames):
    tokens, width = q.shape
    pairs = width // 128
    n = tokens // frames
    qs = pl.BlockSpec((n, 128), lambda f, p: (f, p))
    vs = pl.BlockSpec((n, 128), lambda f, p: (f, pairs + p))
    return call(
        attend_kernel,
        "attend",
        (frames, pairs),
        [(q, qs), (kv_own, qs), (kv_peer, qs), (kv_own, vs), (kv_peer, vs)],
        [
            (sds((tokens, width), BF), qs),
            (sds((tokens, width), F32), qs),
            (sds((tokens, width), F32), qs),
        ],
        flops=30_000_000_000,
        vmem=VM_ATTEND,
    )


def attend_back_kernel(
    q_ref, k0, k1, v0, v1, go_ref, o_ref, lse_ref, dq_ref, dk0, dk1, dv0, dv1, dka, dva
):
    n = k0.shape[0]
    q = q_ref[...]
    go = go_ref[...]
    turned_q, turned_go = q.T, go.T
    prod = go.astype(F32) * o_ref[...]
    qms = [of_head(q, head) for head in range(2)]
    goms = [of_head(go, head) for head in range(2)]
    lses = [lse_ref[:, 64 * head : 64 * head + 1] for head in range(2)]
    deltas = [jnp.sum(of_head(prod, head), axis=1, keepdims=True) for head in range(2)]
    chunk = min(KEY_CHUNK, n)
    dq = None
    for part, (k, v) in enumerate(((k0, v0), (k1, v1))):
        for i in range(0, n, chunk):
            keys = k[i : i + chunk]
            vals = v[i : i + chunk]
            for head in range(2):
                lanes = slice(64 * head, 64 * head + 64)
                probs = jnp.exp2(mm(qms[head], keys, NT) - lses[head])
                ds = (probs * (mm(goms[head], vals, NT) - deltas[head])).astype(BF)
                dva[part, lanes, i : i + chunk] = mm(turned_go[lanes], probs.astype(BF))
                dka[part, lanes, i : i + chunk] = mm(turned_q[lanes], ds)
                term = mm(ds, of_head(keys, head))
                dq = term if dq is None else dq + term
    dq_ref[...] = (dq * SCALING).astype(BF)
    back = 1.0 / LOG2E
    for part, (dk, dv) in enumerate(((dk0, dv0), (dk1, dv1))):
        dk[...] = (dka[part].T * back).astype(BF)
        dv[...] = dva[part].T.astype(BF)


def attend_back(q, kv_own, kv_peer, go, att, lse, frames, first, count, deps):
    tokens, width = q.shape
    pairs = width // 128
    n = tokens // frames
    qs = pl.BlockSpec((n, 128), lambda f, p: (f, first + p))
    vs = pl.BlockSpec((n, 128), lambda f, p: (f, pairs + first + p))
    out = pl.BlockSpec((n, 128), lambda f, p: (f, p))
    shape = sds((tokens, 128 * count), BF)
    return call(
        attend_back_kernel,
        "attend_back",
        (frames, count),
        [(q, qs), (kv_own, qs), (kv_peer, qs), (kv_own, vs), (kv_peer, vs), (go, qs), (att, qs), (lse, qs)],
        [(shape, out)] * 5,
        [pltpu.VMEM((2, 128, n), F32)] * 2,
        11_000_000_000 * count,
        deps,
        VM_BACK,
    )


def normed_of(value):
    row_mean = jnp.mean(value, axis=-1, keepdims=True)
    centered = value - row_mean
    inverse = lax.rsqrt(jnp.mean(centered * centered, axis=-1, keepdims=True) + EPSILON)
    return centered * inverse, inverse


def norm_back(grad_hat, normed, inverse):
    first = jnp.mean(grad_hat, axis=-1, keepdims=True)
    second = jnp.mean(grad_hat * normed, axis=-1, keepdims=True)
    return inverse * (grad_hat - first - normed * second)


def rows_of(block, width):
    return pl.BlockSpec((block, width), lambda i: (i, 0))


def whole_of(shape):
    return pl.BlockSpec(shape, lambda i: (0,) * len(shape))


SMALL = pl.BlockSpec(memory_space=pltpu.SMEM)


def qkv_kernel(x_ref, chan_ref, shift_ref, gain_ref, w, h_ref, kv_ref, q_ref):
    width = x_ref.shape[1]
    normed, inverse = normed_of(x_ref[...].astype(F32) + chan_ref[0])
    hidden = (normed * gain_ref[...] + shift_ref[0]).astype(BF)
    h_ref[...] = hidden
    kv_ref[...] = mm(hidden, w[:, width:]).astype(BF)
    q_ref[...] = (mm(hidden, w[:, :width]) * (SCALING * LOG2E)).astype(BF)


def qkv_of(x, chan_add, shift, gain, weight, frames, deps):
    count, width = x.shape
    block = 256
    per = count // frames // block
    frame = pl.BlockSpec((1, 1, width), lambda i: (i // per, 0, 0))
    narrow = rows_of(block, width)
    return call(
        qkv_kernel,
        "qkv",
        (count // block,),
        [
            (x, narrow),
            (chan_add, frame),
            (shift, frame),
            (gain, whole_of((1, width))),
            (weight, whole_of(weight.shape)),
        ],
        [
            (sds((count, width), BF), narrow),
            (sds((count, 2 * width), BF), rows_of(block, 2 * width)),
            (sds((count, width), BF), narrow),
        ],
        flops=3_600_000_000,
        deps=deps,
        vmem=VM_QKV,
    )


ROOT = math.sqrt(2 / math.pi)
CUBE = ROOT * 0.044715


def gelu_both(x):
    square = x * x
    t = jnp.tanh(x * (ROOT + CUBE * square))
    half = 0.5 * t + 0.5
    slope = half + (0.5 * x) * (1.0 - t * t) * (ROOT + (3.0 * CUBE) * square)
    return x * half, slope


def mlp_kernel(
    x_ref,
    chan_ref,
    att_ref,
    g_ref,
    rows_ref,
    up_bias_ref,
    wo_any,
    wu_any,
    wd_any,
    res_ref,
    act_ref,
    gpre_ref,
    hid_ref,
    mid_ref,
    branch_ref,
    gatt_ref,
    sums_ref,
    wo,
    wu,
    wd,
    sems,
):
    step = pl.program_id(0)
    width = x_ref.shape[1]
    copies = [
        pltpu.make_async_copy(wo_any, wo, sems.at[0]),
        pltpu.make_async_copy(wu_any, wu, sems.at[1]),
        pltpu.make_async_copy(wd_any, wd, sems.at[2]),
    ]

    @pl.when(step == 0)
    def _():
        for c in copies:
            c.start()
        sums_ref[...] = jnp.zeros_like(sums_ref)
        copies[0].wait()

    out_bias, gain, shift, down_bias = [rows_ref[i : i + 1] for i in range(4)]
    middle = x_ref[...].astype(F32) + chan_ref[0] + mm(att_ref[...], wo[...]) + out_bias
    normed, inverse = normed_of(middle)
    hidden = (normed * gain + shift).astype(BF)
    hid_ref[...] = hidden
    g = g_ref[...]

    @pl.when(step == 0)
    def _():
        copies[1].wait()
        copies[2].wait()

    result = middle + down_bias
    grad_hidden = None
    part = width // MLP_SPLIT
    spans = [pl.ds(i * part, part) for i in range(wu.shape[1] // part)]

    def products(cols):
        return mm(hidden, wu[:, cols]), mm(g, wd[cols, :], NT)

    ready = products(spans[0])
    for i, cols in enumerate(spans):
        pre, back = ready
        if i + 1 < len(spans):
            ready = products(spans[i + 1])
        act, slope = gelu_both(pre + up_bias_ref[:, cols])
        act = act.astype(BF)
        act_ref[:, cols] = act
        grad_pre = (back * slope).astype(BF)
        gpre_ref[:, cols] = grad_pre
        at = i % MLP_SPLIT * part
        row = 4 + i // MLP_SPLIT
        sums_ref[row : row + 1, at : at + part] += jnp.sum(
            grad_pre.astype(F32), axis=0, keepdims=True
        )
        result = result + mm(act, wd[cols, :])
        term = mm(grad_pre, wu[:, cols], NT)
        grad_hidden = term if grad_hidden is None else grad_hidden + term
    res_ref[...] = result.astype(BF)
    g = g.astype(F32)
    sums_ref[0:1] += jnp.sum(g, axis=0, keepdims=True)
    sums_ref[1:2] += jnp.sum(grad_hidden * normed, axis=0, keepdims=True)
    sums_ref[2:3] += jnp.sum(grad_hidden, axis=0, keepdims=True)
    grad_middle = g + norm_back(grad_hidden * gain, normed, inverse)
    mid_ref[...] = grad_middle
    branch = grad_middle.astype(BF)
    branch_ref[...] = branch
    sums_ref[3:4] += jnp.sum(branch.astype(F32), axis=0, keepdims=True)
    gatt_ref[...] = mm(branch, wo[...], NT).astype(BF)


def mlp(x, chan_add, att, g, rows, up_bias, wo, wu, wd, frames):
    count, width = x.shape
    wide = wu.shape[1]
    block = MLP_BLOCK
    per = count // frames // block
    narrow, broad = rows_of(block, width), rows_of(block, wide)
    anywhere = pl.BlockSpec(memory_space=pl.ANY)
    return call(
        mlp_kernel,
        "mlp",
        (count // block,),
        [
            (x, narrow),
            (chan_add, pl.BlockSpec((1, 1, width), lambda i: (i // per, 0, 0))),
            (att, narrow),
            (g, narrow),
            (rows, whole_of((4, width))),
            (up_bias, whole_of((1, wide))),
            (wo, anywhere),
            (wu, anywhere),
            (wd, anywhere),
        ],
        [
            (sds((count, width), BF), narrow),
            (sds((count, wide), BF), broad),
            (sds((count, wide), BF), broad),
            (sds((count, width), BF), narrow),
            (sds((count, width), F32), narrow),
            (sds((count, width), BF), narrow),
            (sds((count, width), BF), narrow),
            (sds((4 + wide // width, width), F32), whole_of((4 + wide // width, width))),
        ],
        [
            pltpu.VMEM(wo.shape, BF),
            pltpu.VMEM(wu.shape, BF),
            pltpu.VMEM(wd.shape, BF),
            pltpu.SemaphoreType.DMA((3,)),
        ],
        25_000_000_000,
        vmem=VM_MLP,
    )


def down_grad_kernel(core_ref, act_ref, g_ref, send_ref, keep_ref, scr):
    core = core_ref[0]
    places, share, width = scr.shape[1:]
    scr[...] = mm(act_ref[...], g_ref[...], TN).reshape(scr.shape)
    keep_ref[...] = scr[:, core].astype(BF)
    send_ref[...] = scr[:, 1 - core].astype(BF)


def down_grad(core, act, g, lon, deps):
    count, wide = act.shape
    width = g.shape[1]
    share = wide // lon
    tile = DOWN_TILE
    chips = tile // (2 * share)
    out = sds((lon // 2, share, width), BF)
    spec = pl.BlockSpec((chips, share, width), lambda i: (i, 0, 0))
    return call(
        down_grad_kernel,
        "down_grad",
        (wide // tile,),
        [(core, SMALL), (act, pl.BlockSpec((count, tile), lambda i: (0, i))), (g, whole_of((count, width)))],
        [(out, spec), (out, spec)],
        [pltpu.VMEM((chips, 2, share, width), F32)],
        4_800_000_000,
        deps,
        VM_SUM,
    )


def up_grad_kernel(core_ref, hid_ref, gpre_ref, att_ref, branch_ref, send_ref, keep_ref, turned, scr):
    core = core_ref[0]
    step = pl.program_id(0)
    last = pl.num_programs(0) - 1

    @pl.when(step == 0)
    def _():
        turned[...] = hid_ref[...].T

    @pl.when(step < last)
    def _():
        scr[...] = mm(turned[...], gpre_ref[...]).reshape(scr.shape)

    @pl.when(step == last)
    def _():
        scr[...] = mm(att_ref[...], branch_ref[...], TN).reshape(scr.shape)

    keep_ref[...] = scr[:, core].astype(BF)
    send_ref[...] = scr[:, 1 - core].astype(BF)


def up_grad(core, hidden, gpre, att, branch, lon):
    count, width = hidden.shape
    wide = gpre.shape[1]
    share = width // lon
    last = wide // width - 1
    out = sds((lon // 2, share, wide + width), BF)
    spec = pl.BlockSpec((lon // 2, share, width), lambda i: (0, 0, i))
    full = whole_of((count, width))
    return call(
        up_grad_kernel,
        "up_grad",
        (last + 2,),
        [
            (core, SMALL),
            (hidden, full),
            (gpre, pl.BlockSpec((count, width), lambda i: (0, jnp.minimum(i, last)))),
            (att, full),
            (branch, full),
        ],
        [(out, spec), (out, spec)],
        [pltpu.VMEM((width, count), BF), pltpu.VMEM((lon // 2, 2, share, width), F32)],
        6_000_000_000,
        vmem=VM_SUM,
    )


def fill_part(out, pieces, part):
    at = 0
    for dq, dk0, dv0, got_k, got_v in pieces:
        size = dq.shape[1]
        if part == 0:
            out[:, at : at + size] = dq[...]
        elif part == 1:
            out[:, at : at + size] = dk0[...] + got_k[...]
        else:
            out[:, at : at + size] = dv0[...] + got_v[...]
        at += size


def groups_of(refs):
    return [refs[i : i + 5] for i in range(0, len(refs), 5)]


def qkv_grad_kernel(core_ref, hid_ref, *refs):
    pieces = groups_of(refs[:-5])
    send_ref, keep_ref, turned, grad, scr = refs[-5:]
    core = core_ref[0]
    step = pl.program_id(0)

    @pl.when(step == 0)
    def _():
        turned[...] = hid_ref[...].T

    for part in range(3):

        @pl.when(step == part)
        def _():
            fill_part(grad, pieces, part)

    scr[...] = mm(turned[...], grad[...]).reshape(scr.shape)
    keep_ref[...] = scr[:, core].astype(BF)
    send_ref[...] = scr[:, 1 - core].astype(BF)


def qkv_grad(core, hidden, pieces, lon, deps):
    count, width = hidden.shape
    share = width // lon
    out = sds((lon // 2, share, 3 * width), BF)
    spec = pl.BlockSpec((lon // 2, share, width), lambda i: (0, 0, i))
    return call(
        qkv_grad_kernel,
        "qkv_grad",
        (3,),
        [(core, SMALL), (hidden, whole_of((count, width)))]
        + [(a, whole_of(a.shape)) for group in pieces for a in group],
        [(out, spec), (out, spec)],
        [
            pltpu.VMEM((width, count), BF),
            pltpu.VMEM((count, width), BF),
            pltpu.VMEM((lon // 2, 2, share, width), F32),
        ],
        3_600_000_000,
        deps,
        VM_SUM,
    )


def first_back_kernel_of(groups, frame_blocks):
    def kernel(*refs):
        pieces = groups_of(refs[: 5 * groups])
        x_ref, chan_ref, gain_ref, mid_ref, w, patch_ref, frame_ref, gain_sum, qkv_ref = refs[5 * groups :]
        step = pl.program_id(0)
        width = x_ref.shape[1]
        for part in range(3):
            fill_part(qkv_ref.at[:, part * width : (part + 1) * width], pieces, part)
        grad_hidden = mm(qkv_ref[...], w[...], NT)
        normed, inverse = normed_of(x_ref[...].astype(F32) + chan_ref[0])
        grad_start = mid_ref[...] + norm_back(grad_hidden * gain_ref[...], normed, inverse)
        patch_ref[...] = grad_start.astype(BF)

        @pl.when(step == 0)
        def _():
            gain_sum[...] = jnp.zeros_like(gain_sum)

        @pl.when(lax.rem(step, frame_blocks) == 0)
        def _():
            frame_ref[...] = jnp.zeros_like(frame_ref)

        gain_sum[...] += jnp.sum(grad_hidden * normed, axis=0, keepdims=True)
        frame_ref[0, 0:1] += jnp.sum(grad_hidden, axis=0, keepdims=True)
        frame_ref[0, 1:2] += jnp.sum(grad_start, axis=0, keepdims=True)

    return kernel


def first_back(pieces, x, chan_add, gain, grad_middle, weight, frames, deps):
    count, width = x.shape
    block = 256
    per = count // frames // block
    ins = [(a, rows_of(block, a.shape[1])) for group in pieces for a in group]
    return call(
        first_back_kernel_of(len(pieces), per),
        "first_back",
        (count // block,),
        ins
        + [
            (x, rows_of(block, width)),
            (chan_add, pl.BlockSpec((1, 1, width), lambda i: (i // per, 0, 0))),
            (gain, whole_of((1, width))),
            (grad_middle, rows_of(block, width)),
            (weight, whole_of(weight.shape)),
        ],
        [
            (sds((count, width), BF), rows_of(block, width)),
            (sds((frames, 2, width), F32), pl.BlockSpec((1, 2, width), lambda i: (i // per, 0, 0))),
            (sds((1, width), F32), whole_of((1, width))),
        ],
        [pltpu.VMEM((block, 3 * width), BF)],
        3_600_000_000,
        deps,
        VM_SUM,
    )


def swap_pairs(size, bit):
    return [(i, i ^ (1 << bit)) for i in range(size)]


def bits_of(size):
    return size.bit_length() - 1


def my_bit(axis, bit):
    return ((lax.axis_index(axis) >> bit) & 1).astype(jnp.int32).reshape(1)


def swap(value, axis, bit):
    return lax.ppermute(value, axis, swap_pairs(lax.axis_size(axis), bit))


def cross(value, turn):
    pairs = []
    for i in range(8):
        lat_next = (i & 1) == turn
        pairs.append((i, i ^ (4 if lat_next else 2)))
    return lax.ppermute(value, ("lat", "yy", "core"), pairs)


EVERY = slice(None)


def both(kept_ref, got_ref, *at):
    return (kept_ref[at].astype(F32) + got_ref[at].astype(F32)).astype(BF)


def mlp_part(ins, out, at, yy, half):
    kept_d, got_d, kept_u, got_u = ins
    rows, width = kept_d.shape[1:]
    share = kept_u.shape[1]
    wide = kept_u.shape[2] - width

    @pl.when(half == 0)
    def _():
        out[0, at, :rows] = both(kept_d, got_d, yy)
        out[0, at, rows:] = both(kept_u, got_u, yy, slice(0, share // 2), slice(wide, None))

    @pl.when(half == 1)
    def _():
        for c in range(wide // width):
            out[0, at, c * share : (c + 1) * share] = both(
                kept_u, got_u, yy, EVERY, slice(c * width, (c + 1) * width)
            )
        out[0, at, rows:] = both(kept_u, got_u, yy, slice(share // 2, None), slice(wide, None))


def qkv_part(ins, out, at, yy, half):
    kept, got = ins
    cols = kept.shape[2] // 2
    for side in range(2):

        @pl.when(half == side)
        def _():
            out[0, at] = both(kept, got, yy, slice(None), slice(side * cols, (side + 1) * cols))


def first_add(part, ins, rows, cols, deps=()):
    zed = ins[0].shape[0] // 2

    def kernel(where_ref, *refs):
        core, mine = where_ref[0], where_ref[1]
        for which, out in zip((1 - mine, mine), refs[len(ins) :]):
            for at in range(2):
                yy = jnp.where(core == 0, at, which)
                half = jnp.where(core == 0, which, at)
                part(refs[: len(ins)], out, at, yy, half)

    core = my_bit("core", 0)
    mine = jnp.where(core == 0, my_bit("lat", 0), my_bit("yy", 0))
    out = sds((zed, 2, rows, cols), BF)
    spec = pl.BlockSpec((1, 2, rows, cols), lambda i: (i, 0, 0, 0))
    return call(
        kernel,
        "first_add",
        (zed,),
        [(jnp.concatenate([core, mine]), SMALL)]
        + [(a, pl.BlockSpec((2,) + a.shape[1:], lambda i: (i, 0, 0))) for a in ins],
        [(out, spec)] * 2,
        deps=deps,
        vmem=VM_SUM,
    )


def second_add(kept, got, deps=()):
    zed, two, rows, cols = kept.shape

    def kernel(mine_ref, kept_ref, got_ref, send_ref, keep_ref):
        mine = mine_ref[0]
        send_ref[0] = both(kept_ref, got_ref, 0, 1 - mine)
        keep_ref[0] = both(kept_ref, got_ref, 0, mine)

    mine = jnp.where(my_bit("core", 0) == 0, my_bit("yy", 0), my_bit("lat", 0))
    spec = pl.BlockSpec((1, 2, rows, cols), lambda i: (i, 0, 0, 0))
    out = pl.BlockSpec((1, rows, cols), lambda i: (i, 0, 0))
    return call(
        kernel,
        "second_add",
        (zed,),
        [(mine, SMALL), (kept, spec), (got, spec)],
        [(sds((zed, rows, cols), BF), out)] * 2,
        deps=deps,
        vmem=VM_SUM,
    )


def third_add(kept, got, deps=()):
    zed, rows, cols = kept.shape

    def kernel(me_ref, kept_ref, got_ref, *outs):
        for up, out in enumerate(outs):
            out[...] = both(kept_ref, got_ref, lax.rem(me_ref[0] + up, zed))

    me = lax.axis_index("zed").astype(jnp.int32).reshape(1)
    return call(
        kernel,
        "third_add",
        (1,),
        [(me, SMALL), (kept, whole_of(kept.shape)), (got, whole_of(kept.shape))],
        [(sds((rows, cols), BF), whole_of((rows, cols)))] * zed,
        deps=deps,
        vmem=VM_SUM,
    )


def cut_lead(kept, got, bit, deps=()):
    zed, rows, cols = kept.shape

    def kernel(mine_ref, kept_ref, got_ref, send_ref, keep_ref):
        mine = mine_ref[0]
        send_ref[0] = both(kept_ref, got_ref, 1 - mine)
        keep_ref[0] = both(kept_ref, got_ref, mine)

    spec = pl.BlockSpec((2, rows, cols), lambda i: (i, 0, 0))
    out = pl.BlockSpec((1, rows, cols), lambda i: (i, 0, 0))
    return call(
        kernel,
        "cut_lead",
        (zed // 2,),
        [(my_bit("zed", bit), SMALL), (kept, spec), (got, spec)],
        [(sds((zed // 2, rows, cols), BF), out)] * 2,
        deps=deps,
        vmem=VM_SUM,
    )


def up_zed(value, up):
    zed = lax.axis_size("zed")
    return lax.ppermute(value, "zed", [(i, (i + up) % zed) for i in range(zed)])


def last_add(parts, deps=()):
    rows, cols = parts[0].shape

    def kernel(*refs):
        total = refs[0][...].astype(F32)
        for ref in refs[1:-1]:
            total = total + ref[...].astype(F32)
        refs[-1][...] = total.astype(BF)

    spec = whole_of((rows, cols))
    return call(
        kernel,
        "last_add",
        (1,),
        [(a, spec) for a in parts],
        [(sds((rows, cols), BF), spec)],
        deps=deps,
        vmem=VM_SUM,
    )[0]


def add_and_pass(kept, got, passed):
    rows, cols = kept.shape

    def kernel(kept_ref, got_ref, passed_ref, out_ref, same_ref):
        out_ref[...] = both(kept_ref, got_ref, Ellipsis)

    spec = whole_of((rows, cols))
    anywhere = pl.BlockSpec(memory_space=pl.ANY)
    return pl.pallas_call(
        kernel,
        grid=(1,),
        in_specs=[spec, spec, anywhere],
        out_specs=[spec, anywhere],
        out_shape=[sds((rows, cols), BF), sds(passed.shape, passed.dtype)],
        input_output_aliases={2: 1},
        compiler_params=pltpu.CompilerParams(vmem_limit_bytes=VM_SUM << 20),
        name="add_and_pass",
    )(kept, got, passed)


def halves_of(mine):
    other = swap(mine, "lat", 0)
    high = lax.axis_index("lat") == 1
    return jnp.where(high, other, mine).astype(F32), jnp.where(high, mine, other).astype(F32)


def held(value, deps):
    def kernel(value_ref, out_ref):
        out_ref[...] = value_ref[...]

    spec = whole_of(value.shape)
    return call(
        kernel, "held", (1,), [(value, spec)], [(sds(value.shape, value.dtype), spec)], deps=deps
    )[0]


def plain_sum(kept, got):
    value = lax.psum_scatter(kept + got, ("zed", "yy"), scatter_dimension=0, tiled=True)[0]
    return lax.psum(value.astype(F32), "lat")


def to_frames(value, chips):
    frames_all, patches, width = value.shape
    frames = frames_all // chips
    value = lax.all_to_all(value, ("lat", "zed", "yy"), 0, 0, tiled=True)
    if frames > 1:
        value = value.reshape(chips, frames, patches, width).swapaxes(0, 1)
    return value.reshape(-1, width)


def to_places(value, chips, frames_all):
    width = value.shape[-1]
    frames = frames_all // chips
    if frames > 1:
        value = value.reshape(frames, chips, -1, width).swapaxes(0, 1)
    value = value.reshape(frames_all, -1, width)
    return lax.all_to_all(value, ("lat", "zed", "yy"), 0, 0, tiled=True)


def on_device(
    tokens,
    channel_mask,
    lead_index,
    chan_embed,
    lead_embed,
    norm1_gain,
    norm1_bias,
    qkv_weight,
    out_weight,
    out_bias,
    norm2_gain,
    norm2_bias,
    up_weight,
    up_bias,
    down_weight,
    down_bias,
    cotangent,
):
    lat = lax.axis_size("lat")
    lon = 4 * lax.axis_size("zed")
    chips = lat * (lon // 2)
    frames_all, rows_here, cols_here, width = tokens.shape
    frames = frames_all // chips
    leads = lead_embed.shape[0]
    wide = up_weight.shape[1]
    share = width // lon
    core = my_bit("core", 0)

    x = to_frames(tokens.reshape(frames_all, -1, width), chips)
    flat = cotangent.reshape(frames_all, -1, width)
    g = to_frames(flat, chips)
    count = x.shape[0]

    first = lax.axis_index(("lat", "zed", "yy")) * frames
    mask_here = lax.dynamic_slice_in_dim(channel_mask, first, frames, 0).astype(BF)
    lead_here = lax.dynamic_slice_in_dim(lead_index, first, frames, 0)
    lead_onehot = (lead_here[:, None] == jnp.arange(leads, dtype=jnp.int32)[None, :]).astype(BF)
    chan_add = mm(mask_here, chan_embed)[:, None, :]
    shift1 = (mm(lead_onehot, lead_embed) + norm1_bias.astype(F32))[:, None, :]
    gain1 = norm1_gain.astype(F32)[None]
    rows2 = jnp.stack([out_bias, norm2_gain, norm2_bias, down_bias]).astype(F32)

    hidden1, kv_own, queries = qkv_of(x, chan_add, shift1, gain1, qkv_weight, frames, (flat,))
    kv_peer = swap(kv_own, "core", 0)
    attended, attended32, lse = attend(queries, kv_own, kv_peer, frames)

    result, activ, grad_pre, hidden2, grad_middle, grad_branch, grad_att, early = mlp(
        x,
        chan_add,
        attended,
        g,
        rows2,
        up_bias.astype(F32)[None],
        out_weight,
        up_weight,
        down_weight,
        frames,
    )
    out_patch = to_places(result, chips, frames_all)
    up_send, up_kept = up_grad(core, hidden2, grad_pre, attended, grad_branch, lon)
    up_got = swap(up_send, "core", 0)
    down_send, down_kept = down_grad(core, activ, g, lon, (up_send,))
    down_got = swap(down_send, "core", 0)

    staged = lat == 2
    rows = down_kept.shape[1] + share // 2
    pieces, pair = [], 0
    deps = (down_kept,)
    if staged:
        sent, kept = first_add(mlp_part, [down_kept, down_got, up_kept, up_got], rows, width)
        got = cross(sent, 0)
        deps = (sent,)
    pairs = width // 128
    plan = [pairs // 2, (pairs + 1) // 3, pairs - pairs // 2 - (pairs + 1) // 3]
    for at, size in enumerate(plan):
        dq, dk0, dk1, dv0, dv1 = attend_back(
            queries, kv_own, kv_peer, grad_att, attended32, lse, frames, pair, size, deps
        )
        pieces.append((dq, dk0, dv0, swap(dk1, "core", 0), swap(dv1, "core", 0)))
        pair += size
        deps = (dq,)
        if staged and at == 0:
            sent, kept = second_add(kept, got, deps)
            got = cross(sent, 1)
            deps = (sent, dq)
        if staged and at == 1:
            sent, kept = cut_lead(kept, got, 0, deps)
            got = swap(sent, "zed", 0)
            deps = (sent, dq)
        if at == 1:
            deps = deps + (out_patch,)

    if staged:
        for bit in range(1, bits_of(lax.axis_size("zed"))):
            sent, kept = cut_lead(kept, got, bit, deps)
            got = swap(sent, "zed", bit)
            deps = (sent,)
        mlp_parts = [kept[0], got[0]]
    grad_start, frame_sums, gain_sum = first_back(
        pieces, x, chan_add, gain1, grad_middle, qkv_weight, frames, deps
    )
    if staged:
        mlp_sum, grad_start = add_and_pass(*mlp_parts, grad_start)
    grad_patch = to_places(grad_start, chips, frames_all)

    ups = wide // width
    early_up = early[4:].reshape(lon, ups, share).swapaxes(0, 1).reshape(ups, width)
    late = jnp.concatenate(
        [frame_sums.reshape(2 * frames, width), gain_sum, early[:4], early_up], 0
    )
    late = late.reshape(-1, lon // 2, 2, share)
    mine = core[0]
    late_got = swap(lax.dynamic_index_in_dim(late, 1 - mine, 2, keepdims=False), "core", 0)
    late = lax.dynamic_index_in_dim(late, mine, 2, keepdims=False) + late_got

    deps = (late_got,)
    qkv_send, qkv_kept = qkv_grad(core, hidden1, pieces, lon, deps)
    qkv_got = swap(qkv_send, "core", 0)

    zed = lax.axis_size("zed")

    if staged:
        sent, kept = first_add(qkv_part, [qkv_kept, qkv_got], share, 3 * width // 2)
        got = cross(sent, 0)
        sent, kept = second_add(kept, got, (grad_patch,))
        got = cross(sent, 1)
        parts = third_add(kept, got)
        late = held(late.reshape(late.shape[0], -1), (sent,))
        deps = (parts[0],)
        parts = [parts[0]] + [up_zed(part, up) for up, part in enumerate(parts) if up]
        halves = halves_of(held(mlp_sum, (parts[0],)))
        tall = wide // lon
        sum_down = halves[0][:tall]
        sum_out = jnp.concatenate([half[tall:] for half in halves], 0)
        sum_up = jnp.concatenate(
            [halves[1][c * share : (c + 1) * share] for c in range(wide // width)], 1
        )
        sum_qkv = jnp.concatenate(halves_of(last_add(parts)), 1)
    else:
        sum_down = plain_sum(down_kept, down_got)
        sum_up = plain_sum(up_kept, up_got)
        sum_up, sum_out = sum_up[:, :wide], sum_up[:, wide:]
        sum_qkv = plain_sum(qkv_kept, qkv_got)

    late = late.reshape(1, late.shape[0], -1)
    for axis in ("yy", "lat"):
        for bit in range(bits_of(lax.axis_size(axis))):
            other = swap(late, axis, bit)
            high = my_bit(axis, bit)[0] == 1
            late = jnp.where(
                high, jnp.concatenate([other, late], 0), jnp.concatenate([late, other], 0)
            )
    if staged:
        late = held(late, deps)
    late = jnp.stack([late] + [up_zed(late, up) for up in range(1, zed)])
    late = jnp.take(late, (lax.axis_index("zed") - jnp.arange(zed)) % zed, axis=0)
    late = lax.dynamic_slice_in_dim(late, lax.axis_index(("zed", "yy")) * share, share, 3)
    late = late.reshape(zed, lat, 2, -1, share).swapaxes(0, 1).reshape(chips, -1, share)
    bias_of = late[:, 0 : 2 * frames : 2].reshape(frames_all, share)
    start_of = late[:, 1 : 2 * frames : 2].reshape(frames_all, share)
    rest = late[:, 2 * frames :].sum(0)
    hot = (lead_index[:, None] == jnp.arange(leads, dtype=jnp.int32)[None, :]).astype(F32)
    exact = lax.Precision.HIGHEST
    sum_lead = jnp.dot(hot.T, bias_of, precision=exact)
    sum_chan = jnp.dot(channel_mask.astype(F32).T, start_of, precision=exact)

    shape = (frames_all, rows_here, cols_here, width)
    return (
        out_patch.reshape(shape),
        grad_patch.reshape(shape),
        sum_chan,
        sum_lead,
        rest[0],
        bias_of.sum(0),
        sum_qkv,
        sum_out,
        rest[4],
        rest[2],
        rest[3],
        sum_up,
        rest[5:].reshape(-1),
        sum_down,
        rest[1],
    )


def solution(mesh):
    lat, lon = mesh.shape["lat"], mesh.shape["lon"]
    fine = Mesh(mesh.devices.reshape(lat, lon // 4, 2, 2), ("lat", "zed", "yy", "core"))
    wide = ("zed", "yy", "core")
    places = P(None, "lat", wide, None)
    return jax.shard_map(
        on_device,
        mesh=fine,
        in_specs=(places,) + (P(),) * 15 + (places,),
        out_specs=(
            places,
            places,
            P(None, wide),
            P(None, wide),
            P(wide),
            P(wide),
            P(wide, None),
            P(wide, None),
            P(wide),
            P(wide),
            P(wide),
            P(wide, None),
            P(wide),
            P(wide, None),
            P(wide),
        ),
        check_vma=False,
    )
```

```python
import functools
import math

import jax
import jax.numpy as jnp
from jax import lax
from jax.experimental import pallas as pl
from jax.experimental.pallas import tpu as pltpu
from jax.sharding import Mesh, PartitionSpec as P

HEADS = 12
EPSILON = 1e-06
SCALING = 0.125
LOG2E = math.log2(math.e)
F32 = jnp.float32
BF = jnp.bfloat16
NN = (((1,), (0,)), ((), ()))
NT = (((1,), (1,)), ((), ()))
TN = (((0,), (0,)), ((), ()))
KEY_CHUNK = 512
SMALLEST = 2.0**-90
VM_ATTEND = 62
VM_BACK = 62
VM_MLP = 62
VM_SUM = 62
VM_QKV = 62
COST = 50
DOWN_TILE = 768
MLP_BLOCK = 256
MLP_SPLIT = 1


def mm(a, b, dims=NN):
    return lax.dot_general(a, b, dims, preferred_element_type=F32)


def of_head(value, head, axis=1):
    lane = lax.broadcasted_iota(jnp.int32, value.shape, axis)
    return jnp.where((lane // 64) == head, value, jnp.zeros_like(value))


def sds(shape, dtype):
    return jax.ShapeDtypeStruct(shape, dtype)


def call(kernel, name, grid, ins, outs, scratch=(), flops=0, deps=(), vmem=32):
    given, skipped = len(ins), len(deps)

    def body(*refs):
        kernel(*refs[:given], *refs[given + skipped :])

    anywhere = pl.BlockSpec(memory_space=pl.ANY)
    moved = sum(math.prod(a.shape) * a.dtype.itemsize for a, spec in list(ins) + list(outs))
    return pl.pallas_call(
        body,
        grid=grid,
        in_specs=[spec for a, spec in ins] + [anywhere] * skipped,
        out_specs=[spec for a, spec in outs],
        out_shape=[a for a, spec in outs],
        scratch_shapes=list(scratch),
        compiler_params=pltpu.CompilerParams(vmem_limit_bytes=vmem << 20),
        cost_estimate=pl.CostEstimate(flops=flops // COST, bytes_accessed=moved // COST, transcendentals=0),
        name=name,
    )(*[a for a, spec in ins], *deps)


def attend_kernel(q_ref, k0, k1, v0, v1, o_ref, full_ref, lse_ref):
    count = q_ref.shape[0]
    n = k0.shape[0]
    q = q_ref[...]
    wide_q = q.astype(F32)
    square_q = (wide_q * wide_q).astype(BF)
    turned, squares = [v0[...].T, v1[...].T], []
    for k in (k0, k1):
        wide_k = k[...].astype(F32)
        squares.append((wide_k * wide_k).astype(BF))
    chunk = min(KEY_CHUNK, n)

    def one_head(head, exact):
        qm = of_head(q, head)
        top = None
        if exact:
            for k in (k0, k1):
                for i in range(0, n, chunk):
                    part = jnp.max(mm(k[i : i + chunk], qm, NT), axis=0, keepdims=True)
                    top = part if top is None else jnp.maximum(top, part)
        else:
            pick = of_head(jnp.ones((8, 128), BF), head)
            for square in squares:
                part = jnp.max(mm(pick, square, NT))
                top = part if top is None else jnp.maximum(top, part)
            top = jnp.sqrt(mm(pick, square_q, NT)[0:1] * (top * 1.05))
        out = total = None
        for k, values in ((k0, turned[0]), (k1, turned[1])):
            for i in range(0, n, chunk):
                probs = jnp.exp2(mm(k[i : i + chunk], qm, NT) - top)
                part = jnp.sum(probs, axis=0, keepdims=True)
                total = part if total is None else total + part
                part = mm(values[:, i : i + chunk], probs.astype(BF))
                out = part if out is None else out + part
        lse = jnp.broadcast_to(top + jnp.log2(total), (64, count))
        return out[64 * head : 64 * head + 64] / total, lse, jnp.min(total)

    def run(exact):
        first, second = one_head(0, exact), one_head(1, exact)
        out = jnp.concatenate([first[0], second[0]], 0).T
        o_ref[...] = out.astype(BF)
        full_ref[...] = out
        lse_ref[...] = jnp.concatenate([first[1], second[1]], 0).T
        return jnp.minimum(first[2], second[2])

    least = run(False)

    @pl.when(jnp.logical_not(least >= SMALLEST))
    def _():
        run(True)


def attend(q, kv_own, kv_peer, frames):
    tokens, width = q.shape
    pairs = width // 128
    n = tokens // frames
    qs = pl.BlockSpec((n, 128), lambda f, p: (f, p))
    vs = pl.BlockSpec((n, 128), lambda f, p: (f, pairs + p))
    return call(
        attend_kernel,
        "attend",
        (frames, pairs),
        [(q, qs), (kv_own, qs), (kv_peer, qs), (kv_own, vs), (kv_peer, vs)],
        [
            (sds((tokens, width), BF), qs),
            (sds((tokens, width), F32), qs),
            (sds((tokens, width), F32), qs),
        ],
        flops=30_000_000_000,
        vmem=VM_ATTEND,
    )


def attend_back_kernel(
    q_ref, k0, k1, v0, v1, go_ref, o_ref, lse_ref, dq_ref, dk0, dk1, dv0, dv1, dka, dva
):
    n = k0.shape[0]
    q = q_ref[...]
    go = go_ref[...]
    turned_q, turned_go = q.T, go.T
    prod = go.astype(F32) * o_ref[...]
    qms = [of_head(q, head) for head in range(2)]
    goms = [of_head(go, head) for head in range(2)]
    lses = [lse_ref[:, 64 * head : 64 * head + 1] for head in range(2)]
    deltas = [jnp.sum(of_head(prod, head), axis=1, keepdims=True) for head in range(2)]
    chunk = min(KEY_CHUNK, n)
    dq = None
    for part, (k, v) in enumerate(((k0, v0), (k1, v1))):
        for i in range(0, n, chunk):
            keys = k[i : i + chunk]
            vals = v[i : i + chunk]
            for head in range(2):
                lanes = slice(64 * head, 64 * head + 64)
                probs = jnp.exp2(mm(qms[head], keys, NT) - lses[head])
                ds = (probs * (mm(goms[head], vals, NT) - deltas[head])).astype(BF)
                dva[part, lanes, i : i + chunk] = mm(turned_go, probs.astype(BF))[lanes]
                dka[part, lanes, i : i + chunk] = mm(turned_q, ds)[lanes]
                term = mm(ds, of_head(keys, head))
                dq = term if dq is None else dq + term
    dq_ref[...] = (dq * SCALING).astype(BF)
    back = 1.0 / LOG2E
    for part, (dk, dv) in enumerate(((dk0, dv0), (dk1, dv1))):
        dk[...] = (dka[part].T * back).astype(BF)
        dv[...] = dva[part].T.astype(BF)


def attend_back(q, kv_own, kv_peer, go, att, lse, frames, first, count, deps):
    tokens, width = q.shape
    pairs = width // 128
    n = tokens // frames
    qs = pl.BlockSpec((n, 128), lambda f, p: (f, first + p))
    vs = pl.BlockSpec((n, 128), lambda f, p: (f, pairs + first + p))
    out = pl.BlockSpec((n, 128), lambda f, p: (f, p))
    shape = sds((tokens, 128 * count), BF)
    return call(
        attend_back_kernel,
        "attend_back",
        (frames, count),
        [(q, qs), (kv_own, qs), (kv_peer, qs), (kv_own, vs), (kv_peer, vs), (go, qs), (att, qs), (lse, qs)],
        [(shape, out)] * 5,
        [pltpu.VMEM((2, 128, n), F32)] * 2,
        11_000_000_000 * count,
        deps,
        VM_BACK,
    )


def normed_of(value):
    row_mean = jnp.mean(value, axis=-1, keepdims=True)
    centered = value - row_mean
    inverse = lax.rsqrt(jnp.mean(centered * centered, axis=-1, keepdims=True) + EPSILON)
    return centered * inverse, inverse


def norm_back(grad_hat, normed, inverse):
    first = jnp.mean(grad_hat, axis=-1, keepdims=True)
    second = jnp.mean(grad_hat * normed, axis=-1, keepdims=True)
    return inverse * (grad_hat - first - normed * second)


def rows_of(block, width):
    return pl.BlockSpec((block, width), lambda i: (i, 0))


def whole_of(shape):
    return pl.BlockSpec(shape, lambda i: (0,) * len(shape))


SMALL = pl.BlockSpec(memory_space=pltpu.SMEM)


def qkv_kernel(x_ref, chan_ref, shift_ref, gain_ref, w, h_ref, kv_ref, q_ref):
    width = x_ref.shape[1]
    normed, inverse = normed_of(x_ref[...].astype(F32) + chan_ref[0])
    hidden = (normed * gain_ref[...] + shift_ref[0]).astype(BF)
    h_ref[...] = hidden
    kv_ref[...] = mm(hidden, w[:, width:]).astype(BF)
    q_ref[...] = (mm(hidden, w[:, :width]) * (SCALING * LOG2E)).astype(BF)


def qkv_of(x, chan_add, shift, gain, weight, frames, deps):
    count, width = x.shape
    block = 256
    per = count // frames // block
    frame = pl.BlockSpec((1, 1, width), lambda i: (i // per, 0, 0))
    narrow = rows_of(block, width)
    return call(
        qkv_kernel,
        "qkv",
        (count // block,),
        [
            (x, narrow),
            (chan_add, frame),
            (shift, frame),
            (gain, whole_of((1, width))),
            (weight, whole_of(weight.shape)),
        ],
        [
            (sds((count, width), BF), narrow),
            (sds((count, 2 * width), BF), rows_of(block, 2 * width)),
            (sds((count, width), BF), narrow),
        ],
        flops=3_600_000_000,
        deps=deps,
        vmem=VM_QKV,
    )


ROOT = math.sqrt(2 / math.pi)
CUBE = ROOT * 0.044715


def gelu_both(x):
    square = x * x
    t = jnp.tanh(x * (ROOT + CUBE * square))
    half = 0.5 * t + 0.5
    slope = half + (0.5 * x) * (1.0 - t * t) * (ROOT + (3.0 * CUBE) * square)
    return x * half, slope


def mlp_kernel(
    x_ref,
    chan_ref,
    att_ref,
    g_ref,
    rows_ref,
    up_bias_ref,
    wo_any,
    wu_any,
    wd_any,
    res_ref,
    act_ref,
    gpre_ref,
    hid_ref,
    mid_ref,
    branch_ref,
    gatt_ref,
    sums_ref,
    wo,
    wu,
    wd,
    sems,
):
    step = pl.program_id(0)
    width = x_ref.shape[1]
    copies = [
        pltpu.make_async_copy(wo_any, wo, sems.at[0]),
        pltpu.make_async_copy(wu_any, wu, sems.at[1]),
        pltpu.make_async_copy(wd_any, wd, sems.at[2]),
    ]

    @pl.when(step == 0)
    def _():
        for c in copies:
            c.start()
        sums_ref[...] = jnp.zeros_like(sums_ref)
        copies[0].wait()

    out_bias, gain, shift, down_bias = [rows_ref[i : i + 1] for i in range(4)]
    middle = x_ref[...].astype(F32) + chan_ref[0] + mm(att_ref[...], wo[...]) + out_bias
    normed, inverse = normed_of(middle)
    hidden = (normed * gain + shift).astype(BF)
    hid_ref[...] = hidden
    g = g_ref[...]

    @pl.when(step == 0)
    def _():
        copies[1].wait()
        copies[2].wait()

    result = middle + down_bias
    grad_hidden = None
    part = width // MLP_SPLIT
    spans = [pl.ds(i * part, part) for i in range(wu.shape[1] // part)]

    def products(cols):
        return mm(hidden, wu[:, cols]), mm(g, wd[cols, :], NT)

    ready = products(spans[0])
    for i, cols in enumerate(spans):
        pre, back = ready
        if i + 1 < len(spans):
            ready = products(spans[i + 1])
        act, slope = gelu_both(pre + up_bias_ref[:, cols])
        act = act.astype(BF)
        act_ref[:, cols] = act
        grad_pre = (back * slope).astype(BF)
        gpre_ref[:, cols] = grad_pre
        at = i % MLP_SPLIT * part
        row = 4 + i // MLP_SPLIT
        sums_ref[row : row + 1, at : at + part] += jnp.sum(
            grad_pre.astype(F32), axis=0, keepdims=True
        )
        result = result + mm(act, wd[cols, :])
        term = mm(grad_pre, wu[:, cols], NT)
        grad_hidden = term if grad_hidden is None else grad_hidden + term
    res_ref[...] = result.astype(BF)
    g = g.astype(F32)
    sums_ref[0:1] += jnp.sum(g, axis=0, keepdims=True)
    sums_ref[1:2] += jnp.sum(grad_hidden * normed, axis=0, keepdims=True)
    sums_ref[2:3] += jnp.sum(grad_hidden, axis=0, keepdims=True)
    grad_middle = g + norm_back(grad_hidden * gain, normed, inverse)
    mid_ref[...] = grad_middle
    branch = grad_middle.astype(BF)
    branch_ref[...] = branch
    sums_ref[3:4] += jnp.sum(branch.astype(F32), axis=0, keepdims=True)
    gatt_ref[...] = mm(branch, wo[...], NT).astype(BF)


def mlp(x, chan_add, att, g, rows, up_bias, wo, wu, wd, frames):
    count, width = x.shape
    wide = wu.shape[1]
    block = MLP_BLOCK
    per = count // frames // block
    narrow, broad = rows_of(block, width), rows_of(block, wide)
    anywhere = pl.BlockSpec(memory_space=pl.ANY)
    return call(
        mlp_kernel,
        "mlp",
        (count // block,),
        [
            (x, narrow),
            (chan_add, pl.BlockSpec((1, 1, width), lambda i: (i // per, 0, 0))),
            (att, narrow),
            (g, narrow),
            (rows, whole_of((4, width))),
            (up_bias, whole_of((1, wide))),
            (wo, anywhere),
            (wu, anywhere),
            (wd, anywhere),
        ],
        [
            (sds((count, width), BF), narrow),
            (sds((count, wide), BF), broad),
            (sds((count, wide), BF), broad),
            (sds((count, width), BF), narrow),
            (sds((count, width), F32), narrow),
            (sds((count, width), BF), narrow),
            (sds((count, width), BF), narrow),
            (sds((4 + wide // width, width), F32), whole_of((4 + wide // width, width))),
        ],
        [
            pltpu.VMEM(wo.shape, BF),
            pltpu.VMEM(wu.shape, BF),
            pltpu.VMEM(wd.shape, BF),
            pltpu.SemaphoreType.DMA((3,)),
        ],
        25_000_000_000,
        vmem=VM_MLP,
    )


def down_grad_kernel(core_ref, act_ref, g_ref, send_ref, keep_ref, scr):
    core = core_ref[0]
    places, share, width = scr.shape[1:]
    scr[...] = mm(act_ref[...], g_ref[...], TN).reshape(scr.shape)
    keep_ref[...] = scr[:, core].astype(BF)
    send_ref[...] = scr[:, 1 - core].astype(BF)


def down_grad(core, act, g, lon, deps):
    count, wide = act.shape
    width = g.shape[1]
    share = wide // lon
    tile = DOWN_TILE
    chips = tile // (2 * share)
    out = sds((lon // 2, share, width), BF)
    spec = pl.BlockSpec((chips, share, width), lambda i: (i, 0, 0))
    return call(
        down_grad_kernel,
        "down_grad",
        (wide // tile,),
        [(core, SMALL), (act, pl.BlockSpec((count, tile), lambda i: (0, i))), (g, whole_of((count, width)))],
        [(out, spec), (out, spec)],
        [pltpu.VMEM((chips, 2, share, width), F32)],
        4_800_000_000,
        deps,
        VM_SUM,
    )


def up_grad_kernel(core_ref, hid_ref, gpre_ref, att_ref, branch_ref, send_ref, keep_ref, turned, scr):
    core = core_ref[0]
    step = pl.program_id(0)
    last = pl.num_programs(0) - 1

    @pl.when(step == 0)
    def _():
        turned[...] = hid_ref[...].T

    @pl.when(step < last)
    def _():
        scr[...] = mm(turned[...], gpre_ref[...]).reshape(scr.shape)

    @pl.when(step == last)
    def _():
        scr[...] = mm(att_ref[...], branch_ref[...], TN).reshape(scr.shape)

    keep_ref[...] = scr[:, core].astype(BF)
    send_ref[...] = scr[:, 1 - core].astype(BF)


def up_grad(core, hidden, gpre, att, branch, lon):
    count, width = hidden.shape
    wide = gpre.shape[1]
    share = width // lon
    last = wide // width - 1
    out = sds((lon // 2, share, wide + width), BF)
    spec = pl.BlockSpec((lon // 2, share, width), lambda i: (0, 0, i))
    full = whole_of((count, width))
    return call(
        up_grad_kernel,
        "up_grad",
        (last + 2,),
        [
            (core, SMALL),
            (hidden, full),
            (gpre, pl.BlockSpec((count, width), lambda i: (0, jnp.minimum(i, last)))),
            (att, full),
            (branch, full),
        ],
        [(out, spec), (out, spec)],
        [pltpu.VMEM((width, count), BF), pltpu.VMEM((lon // 2, 2, share, width), F32)],
        6_000_000_000,
        vmem=VM_SUM,
    )


def fill_part(out, pieces, part):
    at = 0
    for dq, dk0, dv0, got_k, got_v in pieces:
        size = dq.shape[1]
        if part == 0:
            out[:, at : at + size] = dq[...]
        elif part == 1:
            out[:, at : at + size] = dk0[...] + got_k[...]
        else:
            out[:, at : at + size] = dv0[...] + got_v[...]
        at += size


def groups_of(refs):
    return [refs[i : i + 5] for i in range(0, len(refs), 5)]


def qkv_grad_kernel(core_ref, hid_ref, *refs):
    pieces = groups_of(refs[:-5])
    send_ref, keep_ref, turned, grad, scr = refs[-5:]
    core = core_ref[0]
    step = pl.program_id(0)

    @pl.when(step == 0)
    def _():
        turned[...] = hid_ref[...].T

    for part in range(3):

        @pl.when(step == part)
        def _():
            fill_part(grad, pieces, part)

    scr[...] = mm(turned[...], grad[...]).reshape(scr.shape)
    keep_ref[...] = scr[:, core].astype(BF)
    send_ref[...] = scr[:, 1 - core].astype(BF)


def qkv_grad(core, hidden, pieces, lon, deps):
    count, width = hidden.shape
    share = width // lon
    out = sds((lon // 2, share, 3 * width), BF)
    spec = pl.BlockSpec((lon // 2, share, width), lambda i: (0, 0, i))
    return call(
        qkv_grad_kernel,
        "qkv_grad",
        (3,),
        [(core, SMALL), (hidden, whole_of((count, width)))]
        + [(a, whole_of(a.shape)) for group in pieces for a in group],
        [(out, spec), (out, spec)],
        [
            pltpu.VMEM((width, count), BF),
            pltpu.VMEM((count, width), BF),
            pltpu.VMEM((lon // 2, 2, share, width), F32),
        ],
        3_600_000_000,
        deps,
        VM_SUM,
    )


def first_back_kernel_of(groups, frame_blocks):
    def kernel(*refs):
        pieces = groups_of(refs[: 5 * groups])
        x_ref, chan_ref, gain_ref, mid_ref, w, patch_ref, frame_ref, gain_sum, qkv_ref = refs[5 * groups :]
        step = pl.program_id(0)
        width = x_ref.shape[1]
        for part in range(3):
            fill_part(qkv_ref.at[:, part * width : (part + 1) * width], pieces, part)
        grad_hidden = mm(qkv_ref[...], w[...], NT)
        normed, inverse = normed_of(x_ref[...].astype(F32) + chan_ref[0])
        grad_start = mid_ref[...] + norm_back(grad_hidden * gain_ref[...], normed, inverse)
        patch_ref[...] = grad_start.astype(BF)

        @pl.when(step == 0)
        def _():
            gain_sum[...] = jnp.zeros_like(gain_sum)

        @pl.when(lax.rem(step, frame_blocks) == 0)
        def _():
            frame_ref[...] = jnp.zeros_like(frame_ref)

        gain_sum[...] += jnp.sum(grad_hidden * normed, axis=0, keepdims=True)
        frame_ref[0, 0:1] += jnp.sum(grad_hidden, axis=0, keepdims=True)
        frame_ref[0, 1:2] += jnp.sum(grad_start, axis=0, keepdims=True)

    return kernel


def first_back(pieces, x, chan_add, gain, grad_middle, weight, frames, deps):
    count, width = x.shape
    block = 256
    per = count // frames // block
    ins = [(a, rows_of(block, a.shape[1])) for group in pieces for a in group]
    return call(
        first_back_kernel_of(len(pieces), per),
        "first_back",
        (count // block,),
        ins
        + [
            (x, rows_of(block, width)),
            (chan_add, pl.BlockSpec((1, 1, width), lambda i: (i // per, 0, 0))),
            (gain, whole_of((1, width))),
            (grad_middle, rows_of(block, width)),
            (weight, whole_of(weight.shape)),
        ],
        [
            (sds((count, width), BF), rows_of(block, width)),
            (sds((frames, 2, width), F32), pl.BlockSpec((1, 2, width), lambda i: (i // per, 0, 0))),
            (sds((1, width), F32), whole_of((1, width))),
        ],
        [pltpu.VMEM((block, 3 * width), BF)],
        3_600_000_000,
        deps,
        VM_SUM,
    )


def swap_pairs(size, bit):
    return [(i, i ^ (1 << bit)) for i in range(size)]


def bits_of(size):
    return size.bit_length() - 1


def my_bit(axis, bit):
    return ((lax.axis_index(axis) >> bit) & 1).astype(jnp.int32).reshape(1)


def swap(value, axis, bit):
    return lax.ppermute(value, axis, swap_pairs(lax.axis_size(axis), bit))


def cross(value, turn):
    pairs = []
    for i in range(8):
        lat_next = (i & 1) == turn
        pairs.append((i, i ^ (4 if lat_next else 2)))
    return lax.ppermute(value, ("lat", "yy", "core"), pairs)


EVERY = slice(None)


def both(kept_ref, got_ref, *at):
    return (kept_ref[at].astype(F32) + got_ref[at].astype(F32)).astype(BF)


def mlp_part(ins, out, at, yy, half):
    kept_d, got_d, kept_u, got_u = ins
    rows, width = kept_d.shape[1:]
    share = kept_u.shape[1]
    wide = kept_u.shape[2] - width

    @pl.when(half == 0)
    def _():
        out[0, at, :rows] = both(kept_d, got_d, yy)
        out[0, at, rows:] = both(kept_u, got_u, yy, slice(0, share // 2), slice(wide, None))

    @pl.when(half == 1)
    def _():
        for c in range(wide // width):
            out[0, at, c * share : (c + 1) * share] = both(
                kept_u, got_u, yy, EVERY, slice(c * width, (c + 1) * width)
            )
        out[0, at, rows:] = both(kept_u, got_u, yy, slice(share // 2, None), slice(wide, None))


def qkv_part(ins, out, at, yy, half):
    kept, got = ins
    cols = kept.shape[2] // 2
    for side in range(2):

        @pl.when(half == side)
        def _():
            out[0, at] = both(kept, got, yy, slice(None), slice(side * cols, (side + 1) * cols))


def first_add(part, ins, rows, cols, deps=()):
    zed = ins[0].shape[0] // 2

    def kernel(where_ref, *refs):
        core, mine = where_ref[0], where_ref[1]
        for which, out in zip((1 - mine, mine), refs[len(ins) :]):
            for at in range(2):
                yy = jnp.where(core == 0, at, which)
                half = jnp.where(core == 0, which, at)
                part(refs[: len(ins)], out, at, yy, half)

    core = my_bit("core", 0)
    mine = jnp.where(core == 0, my_bit("lat", 0), my_bit("yy", 0))
    out = sds((zed, 2, rows, cols), BF)
    spec = pl.BlockSpec((1, 2, rows, cols), lambda i: (i, 0, 0, 0))
    return call(
        kernel,
        "first_add",
        (zed,),
        [(jnp.concatenate([core, mine]), SMALL)]
        + [(a, pl.BlockSpec((2,) + a.shape[1:], lambda i: (i, 0, 0))) for a in ins],
        [(out, spec)] * 2,
        deps=deps,
        vmem=VM_SUM,
    )


def second_add(kept, got, deps=()):
    zed, two, rows, cols = kept.shape

    def kernel(mine_ref, kept_ref, got_ref, send_ref, keep_ref):
        mine = mine_ref[0]
        send_ref[0] = both(kept_ref, got_ref, 0, 1 - mine)
        keep_ref[0] = both(kept_ref, got_ref, 0, mine)

    mine = jnp.where(my_bit("core", 0) == 0, my_bit("yy", 0), my_bit("lat", 0))
    spec = pl.BlockSpec((1, 2, rows, cols), lambda i: (i, 0, 0, 0))
    out = pl.BlockSpec((1, rows, cols), lambda i: (i, 0, 0))
    return call(
        kernel,
        "second_add",
        (zed,),
        [(mine, SMALL), (kept, spec), (got, spec)],
        [(sds((zed, rows, cols), BF), out)] * 2,
        deps=deps,
        vmem=VM_SUM,
    )


def third_add(kept, got, deps=()):
    zed, rows, cols = kept.shape

    def kernel(me_ref, kept_ref, got_ref, *outs):
        for up, out in enumerate(outs):
            out[...] = both(kept_ref, got_ref, lax.rem(me_ref[0] + up, zed))

    me = lax.axis_index("zed").astype(jnp.int32).reshape(1)
    return call(
        kernel,
        "third_add",
        (1,),
        [(me, SMALL), (kept, whole_of(kept.shape)), (got, whole_of(kept.shape))],
        [(sds((rows, cols), BF), whole_of((rows, cols)))] * zed,
        deps=deps,
        vmem=VM_SUM,
    )


def cut_lead(kept, got, bit, deps=()):
    zed, rows, cols = kept.shape

    def kernel(mine_ref, kept_ref, got_ref, send_ref, keep_ref):
        mine = mine_ref[0]
        send_ref[0] = both(kept_ref, got_ref, 1 - mine)
        keep_ref[0] = both(kept_ref, got_ref, mine)

    spec = pl.BlockSpec((2, rows, cols), lambda i: (i, 0, 0))
    out = pl.BlockSpec((1, rows, cols), lambda i: (i, 0, 0))
    return call(
        kernel,
        "cut_lead",
        (zed // 2,),
        [(my_bit("zed", bit), SMALL), (kept, spec), (got, spec)],
        [(sds((zed // 2, rows, cols), BF), out)] * 2,
        deps=deps,
        vmem=VM_SUM,
    )


def up_zed(value, up):
    zed = lax.axis_size("zed")
    return lax.ppermute(value, "zed", [(i, (i + up) % zed) for i in range(zed)])


def last_add(parts, deps=()):
    rows, cols = parts[0].shape

    def kernel(*refs):
        total = refs[0][...].astype(F32)
        for ref in refs[1:-1]:
            total = total + ref[...].astype(F32)
        refs[-1][...] = total.astype(BF)

    spec = whole_of((rows, cols))
    return call(
        kernel,
        "last_add",
        (1,),
        [(a, spec) for a in parts],
        [(sds((rows, cols), BF), spec)],
        deps=deps,
        vmem=VM_SUM,
    )[0]


def add_and_pass(kept, got, passed):
    rows, cols = kept.shape

    def kernel(kept_ref, got_ref, passed_ref, out_ref, same_ref):
        out_ref[...] = both(kept_ref, got_ref, Ellipsis)

    spec = whole_of((rows, cols))
    anywhere = pl.BlockSpec(memory_space=pl.ANY)
    return pl.pallas_call(
        kernel,
        grid=(1,),
        in_specs=[spec, spec, anywhere],
        out_specs=[spec, anywhere],
        out_shape=[sds((rows, cols), BF), sds(passed.shape, passed.dtype)],
        input_output_aliases={2: 1},
        compiler_params=pltpu.CompilerParams(vmem_limit_bytes=VM_SUM << 20),
        name="add_and_pass",
    )(kept, got, passed)


def spread(mine, other, shapes, fill, deps=()):
    def kernel(high_ref, mine_ref, other_ref, *outs):
        @pl.when(high_ref[0] == 0)
        def _():
            fill(mine_ref, other_ref, outs)

        @pl.when(high_ref[0] == 1)
        def _():
            fill(other_ref, mine_ref, outs)

    spec = whole_of(mine.shape)
    return call(
        kernel,
        "spread",
        (1,),
        [(my_bit("lat", 0), SMALL), (mine, spec), (other, spec)],
        [(sds(shape, F32), whole_of(shape)) for shape in shapes],
        deps=deps,
        vmem=VM_SUM,
    )


def fill_qkv(low, high, outs):
    cols = low.shape[1]
    outs[0][:, :cols] = low[...].astype(F32)
    outs[0][:, cols:] = high[...].astype(F32)


def fill_mlp(low, high, outs):
    down, up, out = outs
    tall, share, width = down.shape[0], up.shape[0], down.shape[1]
    down[...] = low[:tall].astype(F32)
    for c in range(up.shape[1] // width):
        up[:, c * width : (c + 1) * width] = high[c * share : (c + 1) * share].astype(F32)
    out[: share // 2] = low[tall:].astype(F32)
    out[share // 2 :] = high[tall:].astype(F32)


def beside(value):
    value = value[None]
    for axis in ("yy", "lat"):
        for bit in range(bits_of(lax.axis_size(axis))):
            other = swap(value, axis, bit)
            high = my_bit(axis, bit)[0] == 1
            value = jnp.where(
                high, jnp.concatenate([other, value], 0), jnp.concatenate([value, other], 0)
            )
    return value


def held(value, deps):
    def kernel(value_ref, out_ref):
        out_ref[...] = value_ref[...]

    spec = whole_of(value.shape)
    return call(
        kernel, "held", (1,), [(value, spec)], [(sds(value.shape, value.dtype), spec)], deps=deps
    )[0]


def plain_sum(kept, got):
    value = lax.psum_scatter(kept + got, ("zed", "yy"), scatter_dimension=0, tiled=True)[0]
    return lax.psum(value.astype(F32), "lat")


def to_frames(value, chips):
    frames_all, patches, width = value.shape
    frames = frames_all // chips
    value = lax.all_to_all(value, ("lat", "zed", "yy"), 0, 0, tiled=True)
    if frames > 1:
        value = value.reshape(chips, frames, patches, width).swapaxes(0, 1)
    return value.reshape(-1, width)


def to_places(value, chips, frames_all):
    width = value.shape[-1]
    frames = frames_all // chips
    if frames > 1:
        value = value.reshape(frames, chips, -1, width).swapaxes(0, 1)
    value = value.reshape(frames_all, -1, width)
    return lax.all_to_all(value, ("lat", "zed", "yy"), 0, 0, tiled=True)


def on_device(
    tokens,
    channel_mask,
    lead_index,
    chan_embed,
    lead_embed,
    norm1_gain,
    norm1_bias,
    qkv_weight,
    out_weight,
    out_bias,
    norm2_gain,
    norm2_bias,
    up_weight,
    up_bias,
    down_weight,
    down_bias,
    cotangent,
):
    lat = lax.axis_size("lat")
    lon = 4 * lax.axis_size("zed")
    chips = lat * (lon // 2)
    frames_all, rows_here, cols_here, width = tokens.shape
    frames = frames_all // chips
    leads = lead_embed.shape[0]
    wide = up_weight.shape[1]
    share = width // lon
    core = my_bit("core", 0)

    x = to_frames(tokens.reshape(frames_all, -1, width), chips)
    flat = cotangent.reshape(frames_all, -1, width)
    g = to_frames(flat, chips)
    count = x.shape[0]

    first = lax.axis_index(("lat", "zed", "yy")) * frames
    mask_here = lax.dynamic_slice_in_dim(channel_mask, first, frames, 0).astype(BF)
    lead_here = lax.dynamic_slice_in_dim(lead_index, first, frames, 0)
    lead_onehot = (lead_here[:, None] == jnp.arange(leads, dtype=jnp.int32)[None, :]).astype(BF)
    chan_add = mm(mask_here, chan_embed)[:, None, :]
    shift1 = (mm(lead_onehot, lead_embed) + norm1_bias.astype(F32))[:, None, :]
    gain1 = norm1_gain.astype(F32)[None]
    rows2 = jnp.stack([out_bias, norm2_gain, norm2_bias, down_bias]).astype(F32)

    hidden1, kv_own, queries = qkv_of(x, chan_add, shift1, gain1, qkv_weight, frames, (flat,))
    kv_peer = swap(kv_own, "core", 0)
    attended, attended32, lse = attend(queries, kv_own, kv_peer, frames)

    result, activ, grad_pre, hidden2, grad_middle, grad_branch, grad_att, early = mlp(
        x,
        chan_add,
        attended,
        g,
        rows2,
        up_bias.astype(F32)[None],
        out_weight,
        up_weight,
        down_weight,
        frames,
    )
    out_patch = to_places(result, chips, frames_all)
    up_send, up_kept = up_grad(core, hidden2, grad_pre, attended, grad_branch, lon)
    up_got = swap(up_send, "core", 0)
    down_send, down_kept = down_grad(core, activ, g, lon, (up_send,))
    down_got = swap(down_send, "core", 0)

    staged = lat == 2
    rows = down_kept.shape[1] + share // 2
    pieces, pair = [], 0
    deps = (down_kept,)
    if staged:
        sent, kept = first_add(mlp_part, [down_kept, down_got, up_kept, up_got], rows, width)
        got = cross(sent, 0)
        deps = (sent,)
    pairs = width // 128
    plan = [pairs // 2, (pairs + 1) // 3, pairs - pairs // 2 - (pairs + 1) // 3]
    for at, size in enumerate(plan):
        dq, dk0, dk1, dv0, dv1 = attend_back(
            queries, kv_own, kv_peer, grad_att, attended32, lse, frames, pair, size, deps
        )
        pieces.append((dq, dk0, dv0, swap(dk1, "core", 0), swap(dv1, "core", 0)))
        pair += size
        deps = (dq,)
        if staged and at == 0:
            sent, kept = second_add(kept, got, deps)
            got = cross(sent, 1)
            deps = (sent, dq)
        if staged and at == 1:
            sent, kept = cut_lead(kept, got, 0, deps)
            got = swap(sent, "zed", 0)
            deps = (sent, dq)
        if at == 1:
            deps = deps + (out_patch,)

    if staged:
        for bit in range(1, bits_of(lax.axis_size("zed"))):
            sent, kept = cut_lead(kept, got, bit, deps)
            got = swap(sent, "zed", bit)
            deps = (sent,)
        mlp_parts = [kept[0], got[0]]
    grad_start, frame_sums, gain_sum = first_back(
        pieces, x, chan_add, gain1, grad_middle, qkv_weight, frames, deps
    )
    if staged:
        mlp_sum, grad_start = add_and_pass(*mlp_parts, grad_start)
    grad_patch = to_places(grad_start, chips, frames_all)

    ups = wide // width
    early_up = early[4:].reshape(lon, ups, share).swapaxes(0, 1).reshape(ups, width)
    late = jnp.concatenate(
        [frame_sums.reshape(2 * frames, width), gain_sum, early[:4], early_up], 0
    )
    late = late.reshape(-1, lon // 2, 2, share)
    mine = core[0]
    late_got = swap(lax.dynamic_index_in_dim(late, 1 - mine, 2, keepdims=False), "core", 0)
    late = lax.dynamic_index_in_dim(late, mine, 2, keepdims=False) + late_got

    deps = (late_got,)
    qkv_send, qkv_kept = qkv_grad(core, hidden1, pieces, lon, deps)
    qkv_got = swap(qkv_send, "core", 0)

    zed = lax.axis_size("zed")

    if staged:
        sent, kept = first_add(qkv_part, [qkv_kept, qkv_got], share, 3 * width // 2)
        got = cross(sent, 0)
        late = beside(held(late.reshape(late.shape[0], -1), (sent,)))
        sent, kept = second_add(kept, got, (grad_patch, late))
        got = cross(sent, 1)
        parts = third_add(kept, got)
        deps = (parts[0],)
        parts = [parts[0]] + [up_zed(part, up) for up, part in enumerate(parts) if up]
        mlp_sum = held(mlp_sum, deps)
        late = held(late, deps)
        tall = wide // lon
        sum_down, sum_up, sum_out = spread(
            mlp_sum, swap(mlp_sum, "lat", 0), [(tall, width), (share, wide), (share, width)], fill_mlp
        )
        total = last_add(parts)
        sum_qkv = spread(total, swap(total, "lat", 0), [(share, 3 * width)], fill_qkv)[0]
    else:
        sum_down = plain_sum(down_kept, down_got)
        sum_up = plain_sum(up_kept, up_got)
        sum_up, sum_out = sum_up[:, :wide], sum_up[:, wide:]
        sum_qkv = plain_sum(qkv_kept, qkv_got)
        late = beside(late.reshape(late.shape[0], -1))

    late = jnp.stack([late] + [up_zed(late, up) for up in range(1, zed)])
    late = jnp.take(late, (lax.axis_index("zed") - jnp.arange(zed)) % zed, axis=0)
    late = lax.dynamic_slice_in_dim(late, lax.axis_index(("zed", "yy")) * share, share, 3)
    late = late.reshape(zed, lat, 2, -1, share).swapaxes(0, 1).reshape(chips, -1, share)
    bias_of = late[:, 0 : 2 * frames : 2].reshape(frames_all, share)
    start_of = late[:, 1 : 2 * frames : 2].reshape(frames_all, share)
    rest = late[:, 2 * frames :].sum(0)
    hot = (lead_index[:, None] == jnp.arange(leads, dtype=jnp.int32)[None, :]).astype(F32)
    exact = lax.Precision.HIGHEST
    sum_lead = jnp.dot(hot.T, bias_of, precision=exact)
    sum_chan = jnp.dot(channel_mask.astype(F32).T, start_of, precision=exact)

    shape = (frames_all, rows_here, cols_here, width)
    return (
        out_patch.reshape(shape),
        grad_patch.reshape(shape),
        sum_chan,
        sum_lead,
        rest[0],
        bias_of.sum(0),
        sum_qkv,
        sum_out,
        rest[4],
        rest[2],
        rest[3],
        sum_up,
        rest[5:].reshape(-1),
        sum_down,
        rest[1],
    )


def solution(mesh):
    lat, lon = mesh.shape["lat"], mesh.shape["lon"]
    fine = Mesh(mesh.devices.reshape(lat, lon // 4, 2, 2), ("lat", "zed", "yy", "core"))
    wide = ("zed", "yy", "core")
    places = P(None, "lat", wide, None)
    return jax.shard_map(
        on_device,
        mesh=fine,
        in_specs=(places,) + (P(),) * 15 + (places,),
        out_specs=(
            places,
            places,
            P(None, wide),
            P(None, wide),
            P(wide),
            P(wide),
            P(wide, None),
            P(wide, None),
            P(wide),
            P(wide),
            P(wide),
            P(wide, None),
            P(wide),
            P(wide, None),
            P(wide),
        ),
        check_vma=False,
    )
```

```python
import functools
import math

import jax
import jax.numpy as jnp
from jax import lax
from jax.experimental import pallas as pl
from jax.experimental.pallas import tpu as pltpu
from jax.sharding import Mesh, PartitionSpec as P

HEADS = 12
EPSILON = 1e-06
SCALING = 0.125
LOG2E = math.log2(math.e)
F32 = jnp.float32
BF = jnp.bfloat16
NN = (((1,), (0,)), ((), ()))
NT = (((1,), (1,)), ((), ()))
TN = (((0,), (0,)), ((), ()))
KEY_CHUNK = 512
SMALLEST = 2.0**-90
VM_ATTEND = 62
VM_BACK = 62
VM_MLP = 62
VM_SUM = 62
VM_QKV = 62
COST = 50
DOWN_TILE = 768
MLP_BLOCK = 256
MLP_SPLIT = 1


def mm(a, b, dims=NN):
    return lax.dot_general(a, b, dims, preferred_element_type=F32)


def of_head(value, head, axis=1):
    lane = lax.broadcasted_iota(jnp.int32, value.shape, axis)
    return jnp.where((lane // 64) == head, value, jnp.zeros_like(value))


def sds(shape, dtype):
    return jax.ShapeDtypeStruct(shape, dtype)


def call(kernel, name, grid, ins, outs, scratch=(), flops=0, deps=(), vmem=32):
    given, skipped = len(ins), len(deps)

    def body(*refs):
        kernel(*refs[:given], *refs[given + skipped :])

    anywhere = pl.BlockSpec(memory_space=pl.ANY)
    moved = sum(math.prod(a.shape) * a.dtype.itemsize for a, spec in list(ins) + list(outs))
    return pl.pallas_call(
        body,
        grid=grid,
        in_specs=[spec for a, spec in ins] + [anywhere] * skipped,
        out_specs=[spec for a, spec in outs],
        out_shape=[a for a, spec in outs],
        scratch_shapes=list(scratch),
        compiler_params=pltpu.CompilerParams(vmem_limit_bytes=vmem << 20),
        cost_estimate=pl.CostEstimate(flops=flops // COST, bytes_accessed=moved // COST, transcendentals=0),
        name=name,
    )(*[a for a, spec in ins], *deps)


def attend_kernel(q_ref, k0, k1, v0, v1, o_ref, full_ref, lse_ref):
    count = q_ref.shape[0]
    n = k0.shape[0]
    q = q_ref[...]
    wide_q = q.astype(F32)
    square_q = (wide_q * wide_q).astype(BF)
    turned, squares = [v0[...].T, v1[...].T], []
    for k in (k0, k1):
        wide_k = k[...].astype(F32)
        squares.append((wide_k * wide_k).astype(BF))
    chunk = min(KEY_CHUNK, n)

    def one_head(head, exact):
        qm = of_head(q, head)
        top = None
        if exact:
            for k in (k0, k1):
                for i in range(0, n, chunk):
                    part = jnp.max(mm(k[i : i + chunk], qm, NT), axis=0, keepdims=True)
                    top = part if top is None else jnp.maximum(top, part)
        else:
            pick = of_head(jnp.ones((8, 128), BF), head)
            for square in squares:
                part = jnp.max(mm(pick, square, NT))
                top = part if top is None else jnp.maximum(top, part)
            top = jnp.sqrt(mm(pick, square_q, NT)[0:1] * (top * 1.05))
        out = total = None
        for k, values in ((k0, turned[0]), (k1, turned[1])):
            for i in range(0, n, chunk):
                probs = jnp.exp2(mm(k[i : i + chunk], qm, NT) - top)
                part = jnp.sum(probs, axis=0, keepdims=True)
                total = part if total is None else total + part
                part = mm(values[:, i : i + chunk], probs.astype(BF))
                out = part if out is None else out + part
        lse = jnp.broadcast_to(top + jnp.log2(total), (64, count))
        return out[64 * head : 64 * head + 64] / total, lse, jnp.min(total)

    def run(exact):
        first, second = one_head(0, exact), one_head(1, exact)
        out = jnp.concatenate([first[0], second[0]], 0).T
        o_ref[...] = out.astype(BF)
        full_ref[...] = out
        lse_ref[...] = jnp.concatenate([first[1], second[1]], 0).T
        return jnp.minimum(first[2], second[2])

    least = run(False)

    @pl.when(jnp.logical_not(least >= SMALLEST))
    def _():
        run(True)


def attend(q, kv_own, kv_peer, frames):
    tokens, width = q.shape
    pairs = width // 128
    n = tokens // frames
    qs = pl.BlockSpec((n, 128), lambda f, p: (f, p))
    vs = pl.BlockSpec((n, 128), lambda f, p: (f, pairs + p))
    return call(
        attend_kernel,
        "attend",
        (frames, pairs),
        [(q, qs), (kv_own, qs), (kv_peer, qs), (kv_own, vs), (kv_peer, vs)],
        [
            (sds((tokens, width), BF), qs),
            (sds((tokens, width), F32), qs),
            (sds((tokens, width), F32), qs),
        ],
        flops=30_000_000_000,
        vmem=VM_ATTEND,
    )


def attend_back_kernel(
    q_ref, k0, k1, v0, v1, go_ref, o_ref, lse_ref, dq_ref, dk0, dk1, dv0, dv1, dka, dva
):
    n = k0.shape[0]
    q = q_ref[...]
    go = go_ref[...]
    turned_q, turned_go = q.T, go.T
    prod = go.astype(F32) * o_ref[...]
    qms = [of_head(q, head) for head in range(2)]
    goms = [of_head(go, head) for head in range(2)]
    lses = [lse_ref[:, 64 * head : 64 * head + 1] for head in range(2)]
    deltas = [jnp.sum(of_head(prod, head), axis=1, keepdims=True) for head in range(2)]
    chunk = min(KEY_CHUNK, n)
    dq = None
    for part, (k, v) in enumerate(((k0, v0), (k1, v1))):
        for i in range(0, n, chunk):
            keys = k[i : i + chunk]
            vals = v[i : i + chunk]
            for head in range(2):
                lanes = slice(64 * head, 64 * head + 64)
                probs = jnp.exp2(mm(qms[head], keys, NT) - lses[head])
                ds = (probs * (mm(goms[head], vals, NT) - deltas[head])).astype(BF)
                dva[part, lanes, i : i + chunk] = mm(turned_go, probs.astype(BF))[lanes]
                dka[part, lanes, i : i + chunk] = mm(turned_q, ds)[lanes]
                term = mm(ds, of_head(keys, head))
                dq = term if dq is None else dq + term
    dq_ref[...] = (dq * SCALING).astype(BF)
    back = 1.0 / LOG2E
    for part, (dk, dv) in enumerate(((dk0, dv0), (dk1, dv1))):
        dk[...] = (dka[part].T * back).astype(BF)
        dv[...] = dva[part].T.astype(BF)


def attend_back(q, kv_own, kv_peer, go, att, lse, frames, first, count, deps):
    tokens, width = q.shape
    pairs = width // 128
    n = tokens // frames
    qs = pl.BlockSpec((n, 128), lambda f, p: (f, first + p))
    vs = pl.BlockSpec((n, 128), lambda f, p: (f, pairs + first + p))
    out = pl.BlockSpec((n, 128), lambda f, p: (f, p))
    shape = sds((tokens, 128 * count), BF)
    return call(
        attend_back_kernel,
        "attend_back",
        (frames, count),
        [(q, qs), (kv_own, qs), (kv_peer, qs), (kv_own, vs), (kv_peer, vs), (go, qs), (att, qs), (lse, qs)],
        [(shape, out)] * 5,
        [pltpu.VMEM((2, 128, n), F32)] * 2,
        11_000_000_000 * count,
        deps,
        VM_BACK,
    )


def normed_of(value):
    row_mean = jnp.mean(value, axis=-1, keepdims=True)
    centered = value - row_mean
    inverse = lax.rsqrt(jnp.mean(centered * centered, axis=-1, keepdims=True) + EPSILON)
    return centered * inverse, inverse


def norm_back(grad_hat, normed, inverse):
    first = jnp.mean(grad_hat, axis=-1, keepdims=True)
    second = jnp.mean(grad_hat * normed, axis=-1, keepdims=True)
    return inverse * (grad_hat - first - normed * second)


def rows_of(block, width):
    return pl.BlockSpec((block, width), lambda i: (i, 0))


def whole_of(shape):
    return pl.BlockSpec(shape, lambda i: (0,) * len(shape))


SMALL = pl.BlockSpec(memory_space=pltpu.SMEM)


def qkv_kernel(x_ref, chan_ref, shift_ref, gain_ref, w, h_ref, kv_ref, q_ref):
    width = x_ref.shape[1]
    normed, inverse = normed_of(x_ref[...].astype(F32) + chan_ref[0])
    hidden = (normed * gain_ref[...] + shift_ref[0]).astype(BF)
    h_ref[...] = hidden
    kv_ref[...] = mm(hidden, w[:, width:]).astype(BF)
    q_ref[...] = (mm(hidden, w[:, :width]) * (SCALING * LOG2E)).astype(BF)


def qkv_of(x, chan_add, shift, gain, weight, frames, deps):
    count, width = x.shape
    block = 256
    per = count // frames // block
    frame = pl.BlockSpec((1, 1, width), lambda i: (i // per, 0, 0))
    narrow = rows_of(block, width)
    return call(
        qkv_kernel,
        "qkv",
        (count // block,),
        [
            (x, narrow),
            (chan_add, frame),
            (shift, frame),
            (gain, whole_of((1, width))),
            (weight, whole_of(weight.shape)),
        ],
        [
            (sds((count, width), BF), narrow),
            (sds((count, 2 * width), BF), rows_of(block, 2 * width)),
            (sds((count, width), BF), narrow),
        ],
        flops=3_600_000_000,
        deps=deps,
        vmem=VM_QKV,
    )


ROOT = math.sqrt(2 / math.pi)
CUBE = ROOT * 0.044715


def gelu_both(x):
    square = x * x
    t = jnp.tanh(x * (ROOT + CUBE * square))
    half = 0.5 * t + 0.5
    slope = half + (0.5 * x) * (1.0 - t * t) * (ROOT + (3.0 * CUBE) * square)
    return x * half, slope


def mlp_kernel(
    x_ref,
    chan_ref,
    att_ref,
    g_ref,
    rows_ref,
    up_bias_ref,
    wo_any,
    wu_any,
    wd_any,
    res_ref,
    act_ref,
    gpre_ref,
    hid_ref,
    mid_ref,
    branch_ref,
    gatt_ref,
    sums_ref,
    wo,
    wu,
    wd,
    sems,
):
    step = pl.program_id(0)
    width = x_ref.shape[1]
    copies = [
        pltpu.make_async_copy(wo_any, wo, sems.at[0]),
        pltpu.make_async_copy(wu_any, wu, sems.at[1]),
        pltpu.make_async_copy(wd_any, wd, sems.at[2]),
    ]

    @pl.when(step == 0)
    def _():
        for c in copies:
            c.start()
        sums_ref[...] = jnp.zeros_like(sums_ref)
        copies[0].wait()

    out_bias, gain, shift, down_bias = [rows_ref[i : i + 1] for i in range(4)]
    middle = x_ref[...].astype(F32) + chan_ref[0] + mm(att_ref[...], wo[...]) + out_bias
    normed, inverse = normed_of(middle)
    hidden = (normed * gain + shift).astype(BF)
    hid_ref[...] = hidden
    g = g_ref[...]

    @pl.when(step == 0)
    def _():
        copies[1].wait()
        copies[2].wait()

    result = middle + down_bias
    grad_hidden = None
    part = width // MLP_SPLIT
    spans = [pl.ds(i * part, part) for i in range(wu.shape[1] // part)]

    def products(cols):
        return mm(hidden, wu[:, cols]), mm(g, wd[cols, :], NT)

    ready = products(spans[0])
    for i, cols in enumerate(spans):
        pre, back = ready
        if i + 1 < len(spans):
            ready = products(spans[i + 1])
        act, slope = gelu_both(pre + up_bias_ref[:, cols])
        act = act.astype(BF)
        act_ref[:, cols] = act
        grad_pre = (back * slope).astype(BF)
        gpre_ref[:, cols] = grad_pre
        at = i % MLP_SPLIT * part
        row = 4 + i // MLP_SPLIT
        sums_ref[row : row + 1, at : at + part] += jnp.sum(
            grad_pre.astype(F32), axis=0, keepdims=True
        )
        result = result + mm(act, wd[cols, :])
        term = mm(grad_pre, wu[:, cols], NT)
        grad_hidden = term if grad_hidden is None else grad_hidden + term
    res_ref[...] = result.astype(BF)
    g = g.astype(F32)
    sums_ref[0:1] += jnp.sum(g, axis=0, keepdims=True)
    sums_ref[1:2] += jnp.sum(grad_hidden * normed, axis=0, keepdims=True)
    sums_ref[2:3] += jnp.sum(grad_hidden, axis=0, keepdims=True)
    grad_middle = g + norm_back(grad_hidden * gain, normed, inverse)
    mid_ref[...] = grad_middle
    branch = grad_middle.astype(BF)
    branch_ref[...] = branch
    sums_ref[3:4] += jnp.sum(branch.astype(F32), axis=0, keepdims=True)
    gatt_ref[...] = mm(branch, wo[...], NT).astype(BF)


def mlp(x, chan_add, att, g, rows, up_bias, wo, wu, wd, frames):
    count, width = x.shape
    wide = wu.shape[1]
    block = MLP_BLOCK
    per = count // frames // block
    narrow, broad = rows_of(block, width), rows_of(block, wide)
    anywhere = pl.BlockSpec(memory_space=pl.ANY)
    return call(
        mlp_kernel,
        "mlp",
        (count // block,),
        [
            (x, narrow),
            (chan_add, pl.BlockSpec((1, 1, width), lambda i: (i // per, 0, 0))),
            (att, narrow),
            (g, narrow),
            (rows, whole_of((4, width))),
            (up_bias, whole_of((1, wide))),
            (wo, anywhere),
            (wu, anywhere),
            (wd, anywhere),
        ],
        [
            (sds((count, width), BF), narrow),
            (sds((count, wide), BF), broad),
            (sds((count, wide), BF), broad),
            (sds((count, width), BF), narrow),
            (sds((count, width), F32), narrow),
            (sds((count, width), BF), narrow),
            (sds((count, width), BF), narrow),
            (sds((4 + wide // width, width), F32), whole_of((4 + wide // width, width))),
        ],
        [
            pltpu.VMEM(wo.shape, BF),
            pltpu.VMEM(wu.shape, BF),
            pltpu.VMEM(wd.shape, BF),
            pltpu.SemaphoreType.DMA((3,)),
        ],
        25_000_000_000,
        vmem=VM_MLP,
    )


def down_grad_kernel(core_ref, act_ref, g_ref, send_ref, keep_ref, scr):
    core = core_ref[0]
    places, share, width = scr.shape[1:]
    scr[...] = mm(act_ref[...], g_ref[...], TN).reshape(scr.shape)
    keep_ref[...] = scr[:, core].astype(BF)
    send_ref[...] = scr[:, 1 - core].astype(BF)


def down_grad(core, act, g, lon, deps):
    count, wide = act.shape
    width = g.shape[1]
    share = wide // lon
    tile = DOWN_TILE
    chips = tile // (2 * share)
    out = sds((lon // 2, share, width), BF)
    spec = pl.BlockSpec((chips, share, width), lambda i: (i, 0, 0))
    return call(
        down_grad_kernel,
        "down_grad",
        (wide // tile,),
        [(core, SMALL), (act, pl.BlockSpec((count, tile), lambda i: (0, i))), (g, whole_of((count, width)))],
        [(out, spec), (out, spec)],
        [pltpu.VMEM((chips, 2, share, width), F32)],
        4_800_000_000,
        deps,
        VM_SUM,
    )


def up_grad_kernel(core_ref, hid_ref, gpre_ref, att_ref, branch_ref, send_ref, keep_ref, turned, scr):
    core = core_ref[0]
    step = pl.program_id(0)
    last = pl.num_programs(0) - 1

    @pl.when(step == 0)
    def _():
        turned[...] = hid_ref[...].T

    @pl.when(step < last)
    def _():
        scr[...] = mm(turned[...], gpre_ref[...]).reshape(scr.shape)

    @pl.when(step == last)
    def _():
        scr[...] = mm(att_ref[...], branch_ref[...], TN).reshape(scr.shape)

    keep_ref[...] = scr[:, core].astype(BF)
    send_ref[...] = scr[:, 1 - core].astype(BF)


def up_grad(core, hidden, gpre, att, branch, lon):
    count, width = hidden.shape
    wide = gpre.shape[1]
    share = width // lon
    last = wide // width - 1
    out = sds((lon // 2, share, wide + width), BF)
    spec = pl.BlockSpec((lon // 2, share, width), lambda i: (0, 0, i))
    full = whole_of((count, width))
    return call(
        up_grad_kernel,
        "up_grad",
        (last + 2,),
        [
            (core, SMALL),
            (hidden, full),
            (gpre, pl.BlockSpec((count, width), lambda i: (0, jnp.minimum(i, last)))),
            (att, full),
            (branch, full),
        ],
        [(out, spec), (out, spec)],
        [pltpu.VMEM((width, count), BF), pltpu.VMEM((lon // 2, 2, share, width), F32)],
        6_000_000_000,
        vmem=VM_SUM,
    )


def fill_part(out, pieces, part):
    at = 0
    for dq, dk0, dv0, got_k, got_v in pieces:
        size = dq.shape[1]
        if part == 0:
            out[:, at : at + size] = dq[...]
        elif part == 1:
            out[:, at : at + size] = dk0[...] + got_k[...]
        else:
            out[:, at : at + size] = dv0[...] + got_v[...]
        at += size


def groups_of(refs):
    return [refs[i : i + 5] for i in range(0, len(refs), 5)]


def qkv_grad_kernel(core_ref, hid_ref, *refs):
    pieces = groups_of(refs[:-5])
    send_ref, keep_ref, turned, grad, scr = refs[-5:]
    core = core_ref[0]
    step = pl.program_id(0)

    @pl.when(step == 0)
    def _():
        turned[...] = hid_ref[...].T

    for part in range(3):

        @pl.when(step == part)
        def _():
            fill_part(grad, pieces, part)

    scr[...] = mm(turned[...], grad[...]).reshape(scr.shape)
    keep_ref[...] = scr[:, core].astype(BF)
    send_ref[...] = scr[:, 1 - core].astype(BF)


def qkv_grad(core, hidden, pieces, lon, deps):
    count, width = hidden.shape
    share = width // lon
    out = sds((lon // 2, share, 3 * width), BF)
    spec = pl.BlockSpec((lon // 2, share, width), lambda i: (0, 0, i))
    return call(
        qkv_grad_kernel,
        "qkv_grad",
        (3,),
        [(core, SMALL), (hidden, whole_of((count, width)))]
        + [(a, whole_of(a.shape)) for group in pieces for a in group],
        [(out, spec), (out, spec)],
        [
            pltpu.VMEM((width, count), BF),
            pltpu.VMEM((count, width), BF),
            pltpu.VMEM((lon // 2, 2, share, width), F32),
        ],
        3_600_000_000,
        deps,
        VM_SUM,
    )


def first_back_kernel_of(groups, frame_blocks):
    def kernel(*refs):
        pieces = groups_of(refs[: 5 * groups])
        x_ref, chan_ref, gain_ref, mid_ref, w, patch_ref, frame_ref, gain_sum, qkv_ref = refs[5 * groups :]
        step = pl.program_id(0)
        width = x_ref.shape[1]
        for part in range(3):
            fill_part(qkv_ref.at[:, part * width : (part + 1) * width], pieces, part)
        grad_hidden = mm(qkv_ref[...], w[...], NT)
        normed, inverse = normed_of(x_ref[...].astype(F32) + chan_ref[0])
        grad_start = mid_ref[...] + norm_back(grad_hidden * gain_ref[...], normed, inverse)
        patch_ref[...] = grad_start.astype(BF)

        @pl.when(step == 0)
        def _():
            gain_sum[...] = jnp.zeros_like(gain_sum)

        @pl.when(lax.rem(step, frame_blocks) == 0)
        def _():
            frame_ref[...] = jnp.zeros_like(frame_ref)

        gain_sum[...] += jnp.sum(grad_hidden * normed, axis=0, keepdims=True)
        frame_ref[0, 0:1] += jnp.sum(grad_hidden, axis=0, keepdims=True)
        frame_ref[0, 1:2] += jnp.sum(grad_start, axis=0, keepdims=True)

    return kernel


def first_back(pieces, x, chan_add, gain, grad_middle, weight, frames, deps):
    count, width = x.shape
    block = 256
    per = count // frames // block
    ins = [(a, rows_of(block, a.shape[1])) for group in pieces for a in group]
    return call(
        first_back_kernel_of(len(pieces), per),
        "first_back",
        (count // block,),
        ins
        + [
            (x, rows_of(block, width)),
            (chan_add, pl.BlockSpec((1, 1, width), lambda i: (i // per, 0, 0))),
            (gain, whole_of((1, width))),
            (grad_middle, rows_of(block, width)),
            (weight, whole_of(weight.shape)),
        ],
        [
            (sds((count, width), BF), rows_of(block, width)),
            (sds((frames, 2, width), F32), pl.BlockSpec((1, 2, width), lambda i: (i // per, 0, 0))),
            (sds((1, width), F32), whole_of((1, width))),
        ],
        [pltpu.VMEM((block, 3 * width), BF)],
        3_600_000_000,
        deps,
        VM_SUM,
    )


def swap_pairs(size, bit):
    return [(i, i ^ (1 << bit)) for i in range(size)]


def bits_of(size):
    return size.bit_length() - 1


def my_bit(axis, bit):
    return ((lax.axis_index(axis) >> bit) & 1).astype(jnp.int32).reshape(1)


def swap(value, axis, bit):
    return lax.ppermute(value, axis, swap_pairs(lax.axis_size(axis), bit))


def cross(value, turn):
    pairs = []
    for i in range(8):
        lat_next = (i & 1) == turn
        pairs.append((i, i ^ (4 if lat_next else 2)))
    return lax.ppermute(value, ("lat", "yy", "core"), pairs)


EVERY = slice(None)


def both(kept_ref, got_ref, *at):
    return (kept_ref[at].astype(F32) + got_ref[at].astype(F32)).astype(BF)


def mlp_part(ins, out, at, yy, half):
    kept_d, got_d, kept_u, got_u = ins
    rows, width = kept_d.shape[1:]
    share = kept_u.shape[1]
    wide = kept_u.shape[2] - width

    @pl.when(half == 0)
    def _():
        out[0, at, :rows] = both(kept_d, got_d, yy)
        out[0, at, rows:] = both(kept_u, got_u, yy, slice(0, share // 2), slice(wide, None))

    @pl.when(half == 1)
    def _():
        for c in range(wide // width):
            out[0, at, c * share : (c + 1) * share] = both(
                kept_u, got_u, yy, EVERY, slice(c * width, (c + 1) * width)
            )
        out[0, at, rows:] = both(kept_u, got_u, yy, slice(share // 2, None), slice(wide, None))


def qkv_part(ins, out, at, yy, half):
    kept, got = ins
    cols = kept.shape[2] // 2
    for side in range(2):

        @pl.when(half == side)
        def _():
            out[0, at] = both(kept, got, yy, slice(None), slice(side * cols, (side + 1) * cols))


def first_add(part, ins, rows, cols, deps=()):
    zed = ins[0].shape[0] // 2

    def kernel(where_ref, *refs):
        core, mine = where_ref[0], where_ref[1]
        for which, out in zip((1 - mine, mine), refs[len(ins) :]):
            for at in range(2):
                yy = jnp.where(core == 0, at, which)
                half = jnp.where(core == 0, which, at)
                part(refs[: len(ins)], out, at, yy, half)

    core = my_bit("core", 0)
    mine = jnp.where(core == 0, my_bit("lat", 0), my_bit("yy", 0))
    out = sds((zed, 2, rows, cols), BF)
    spec = pl.BlockSpec((1, 2, rows, cols), lambda i: (i, 0, 0, 0))
    return call(
        kernel,
        "first_add",
        (zed,),
        [(jnp.concatenate([core, mine]), SMALL)]
        + [(a, pl.BlockSpec((2,) + a.shape[1:], lambda i: (i, 0, 0))) for a in ins],
        [(out, spec)] * 2,
        deps=deps,
        vmem=VM_SUM,
    )


def second_add(kept, got, deps=()):
    zed, two, rows, cols = kept.shape

    def kernel(mine_ref, kept_ref, got_ref, send_ref, keep_ref):
        mine = mine_ref[0]
        send_ref[0] = both(kept_ref, got_ref, 0, 1 - mine)
        keep_ref[0] = both(kept_ref, got_ref, 0, mine)

    mine = jnp.where(my_bit("core", 0) == 0, my_bit("yy", 0), my_bit("lat", 0))
    spec = pl.BlockSpec((1, 2, rows, cols), lambda i: (i, 0, 0, 0))
    out = pl.BlockSpec((1, rows, cols), lambda i: (i, 0, 0))
    return call(
        kernel,
        "second_add",
        (zed,),
        [(mine, SMALL), (kept, spec), (got, spec)],
        [(sds((zed, rows, cols), BF), out)] * 2,
        deps=deps,
        vmem=VM_SUM,
    )


def third_add(kept, got, deps=()):
    zed, rows, cols = kept.shape

    def kernel(me_ref, kept_ref, got_ref, *outs):
        for up, out in enumerate(outs):
            out[...] = both(kept_ref, got_ref, lax.rem(me_ref[0] + up, zed))

    me = lax.axis_index("zed").astype(jnp.int32).reshape(1)
    return call(
        kernel,
        "third_add",
        (1,),
        [(me, SMALL), (kept, whole_of(kept.shape)), (got, whole_of(kept.shape))],
        [(sds((rows, cols), BF), whole_of((rows, cols)))] * zed,
        deps=deps,
        vmem=VM_SUM,
    )


def cut_lead(kept, got, bit, deps=()):
    zed, rows, cols = kept.shape

    def kernel(mine_ref, kept_ref, got_ref, send_ref, keep_ref):
        mine = mine_ref[0]
        send_ref[0] = both(kept_ref, got_ref, 1 - mine)
        keep_ref[0] = both(kept_ref, got_ref, mine)

    spec = pl.BlockSpec((2, rows, cols), lambda i: (i, 0, 0))
    out = pl.BlockSpec((1, rows, cols), lambda i: (i, 0, 0))
    return call(
        kernel,
        "cut_lead",
        (zed // 2,),
        [(my_bit("zed", bit), SMALL), (kept, spec), (got, spec)],
        [(sds((zed // 2, rows, cols), BF), out)] * 2,
        deps=deps,
        vmem=VM_SUM,
    )


def up_zed(value, up):
    zed = lax.axis_size("zed")
    return lax.ppermute(value, "zed", [(i, (i + up) % zed) for i in range(zed)])


def last_add(parts, deps=()):
    rows, cols = parts[0].shape

    def kernel(*refs):
        total = refs[0][...].astype(F32)
        for ref in refs[1:-1]:
            total = total + ref[...].astype(F32)
        refs[-1][...] = total.astype(BF)

    spec = whole_of((rows, cols))
    return call(
        kernel,
        "last_add",
        (1,),
        [(a, spec) for a in parts],
        [(sds((rows, cols), BF), spec)],
        deps=deps,
        vmem=VM_SUM,
    )[0]


def add_and_pass(kept, got, passed):
    rows, cols = kept.shape

    def kernel(kept_ref, got_ref, passed_ref, out_ref, same_ref):
        out_ref[...] = both(kept_ref, got_ref, Ellipsis)

    spec = whole_of((rows, cols))
    anywhere = pl.BlockSpec(memory_space=pl.ANY)
    return pl.pallas_call(
        kernel,
        grid=(1,),
        in_specs=[spec, spec, anywhere],
        out_specs=[spec, anywhere],
        out_shape=[sds((rows, cols), BF), sds(passed.shape, passed.dtype)],
        input_output_aliases={2: 1},
        compiler_params=pltpu.CompilerParams(vmem_limit_bytes=VM_SUM << 20),
        name="add_and_pass",
    )(kept, got, passed)


def spread(mine, other, shapes, fill, deps=()):
    def kernel(high_ref, mine_ref, other_ref, *outs):
        @pl.when(high_ref[0] == 0)
        def _():
            fill(mine_ref, other_ref, outs)

        @pl.when(high_ref[0] == 1)
        def _():
            fill(other_ref, mine_ref, outs)

    spec = whole_of(mine.shape)
    return call(
        kernel,
        "spread",
        (1,),
        [(my_bit("lat", 0), SMALL), (mine, spec), (other, spec)],
        [(sds(shape, F32), whole_of(shape)) for shape in shapes],
        deps=deps,
        vmem=VM_SUM,
    )


def fill_qkv(low, high, outs):
    cols = low.shape[1]
    outs[0][:, :cols] = low[...].astype(F32)
    outs[0][:, cols:] = high[...].astype(F32)


def fill_mlp(low, high, outs):
    down, up, out = outs
    tall, share, width = down.shape[0], up.shape[0], down.shape[1]
    down[...] = low[:tall].astype(F32)
    for c in range(up.shape[1] // width):
        up[:, c * width : (c + 1) * width] = high[c * share : (c + 1) * share].astype(F32)
    out[: share // 2] = low[tall:].astype(F32)
    out[share // 2 :] = high[tall:].astype(F32)


def beside(value):
    value = value[None]
    for axis in ("yy", "lat"):
        for bit in range(bits_of(lax.axis_size(axis))):
            other = swap(value, axis, bit)
            high = my_bit(axis, bit)[0] == 1
            value = jnp.where(
                high, jnp.concatenate([other, value], 0), jnp.concatenate([value, other], 0)
            )
    return value


def held(value, deps):
    def kernel(value_ref, out_ref):
        out_ref[...] = value_ref[...]

    spec = whole_of(value.shape)
    return call(
        kernel, "held", (1,), [(value, spec)], [(sds(value.shape, value.dtype), spec)], deps=deps
    )[0]


def plain_sum(kept, got):
    value = lax.psum_scatter(kept + got, ("zed", "yy"), scatter_dimension=0, tiled=True)[0]
    return lax.psum(value.astype(F32), "lat")


def to_frames(value, chips):
    frames_all, patches, width = value.shape
    frames = frames_all // chips
    value = lax.all_to_all(value, ("lat", "zed", "yy"), 0, 0, tiled=True)
    if frames > 1:
        value = value.reshape(chips, frames, patches, width).swapaxes(0, 1)
    return value.reshape(-1, width)


def to_places(value, chips, frames_all):
    width = value.shape[-1]
    frames = frames_all // chips
    if frames > 1:
        value = value.reshape(frames, chips, -1, width).swapaxes(0, 1)
    value = value.reshape(frames_all, -1, width)
    return lax.all_to_all(value, ("lat", "zed", "yy"), 0, 0, tiled=True)


def on_device(
    tokens,
    channel_mask,
    lead_index,
    chan_embed,
    lead_embed,
    norm1_gain,
    norm1_bias,
    qkv_weight,
    out_weight,
    out_bias,
    norm2_gain,
    norm2_bias,
    up_weight,
    up_bias,
    down_weight,
    down_bias,
    cotangent,
):
    lat = lax.axis_size("lat")
    lon = 4 * lax.axis_size("zed")
    chips = lat * (lon // 2)
    frames_all, rows_here, cols_here, width = tokens.shape
    frames = frames_all // chips
    leads = lead_embed.shape[0]
    wide = up_weight.shape[1]
    share = width // lon
    core = my_bit("core", 0)

    x = to_frames(tokens.reshape(frames_all, -1, width), chips)
    flat = cotangent.reshape(frames_all, -1, width)
    g = to_frames(flat, chips)
    count = x.shape[0]

    first = lax.axis_index(("lat", "zed", "yy")) * frames
    mask_here = lax.dynamic_slice_in_dim(channel_mask, first, frames, 0).astype(BF)
    lead_here = lax.dynamic_slice_in_dim(lead_index, first, frames, 0)
    lead_onehot = (lead_here[:, None] == jnp.arange(leads, dtype=jnp.int32)[None, :]).astype(BF)
    chan_add = mm(mask_here, chan_embed)[:, None, :]
    shift1 = (mm(lead_onehot, lead_embed) + norm1_bias.astype(F32))[:, None, :]
    gain1 = norm1_gain.astype(F32)[None]
    rows2 = jnp.stack([out_bias, norm2_gain, norm2_bias, down_bias]).astype(F32)

    hidden1, kv_own, queries = qkv_of(x, chan_add, shift1, gain1, qkv_weight, frames, (flat,))
    kv_peer = swap(kv_own, "core", 0)
    attended, attended32, lse = attend(queries, kv_own, kv_peer, frames)

    result, activ, grad_pre, hidden2, grad_middle, grad_branch, grad_att, early = mlp(
        x,
        chan_add,
        attended,
        g,
        rows2,
        up_bias.astype(F32)[None],
        out_weight,
        up_weight,
        down_weight,
        frames,
    )
    out_patch = to_places(result, chips, frames_all)
    up_send, up_kept = up_grad(core, hidden2, grad_pre, attended, grad_branch, lon)
    up_got = swap(up_send, "core", 0)
    down_send, down_kept = down_grad(core, activ, g, lon, (up_send,))
    down_got = swap(down_send, "core", 0)

    staged = lat == 2
    rows = down_kept.shape[1] + share // 2
    pieces, pair = [], 0
    deps = (down_kept,)
    if staged:
        sent, kept = first_add(mlp_part, [down_kept, down_got, up_kept, up_got], rows, width)
        got = cross(sent, 0)
        deps = (sent,)
    pairs = width // 128
    plan = [pairs // 2, (pairs + 1) // 3, pairs - pairs // 2 - (pairs + 1) // 3]
    for at, size in enumerate(plan):
        dq, dk0, dk1, dv0, dv1 = attend_back(
            queries, kv_own, kv_peer, grad_att, attended32, lse, frames, pair, size, deps
        )
        pieces.append((dq, dk0, dv0, swap(dk1, "core", 0), swap(dv1, "core", 0)))
        pair += size
        deps = (dq,)
        if staged and at == 0:
            sent, kept = second_add(kept, got, deps)
            got = cross(sent, 1)
            deps = (sent, dq)
        if staged and at == 1:
            sent, kept = cut_lead(kept, got, 0, deps)
            got = swap(sent, "zed", 0)
            deps = (sent, dq)

    if staged:
        for bit in range(1, bits_of(lax.axis_size("zed"))):
            sent, kept = cut_lead(kept, got, bit, deps)
            got = swap(sent, "zed", bit)
            deps = (sent, out_patch)
        mlp_parts = [kept[0], got[0]]
    grad_start, frame_sums, gain_sum = first_back(
        pieces, x, chan_add, gain1, grad_middle, qkv_weight, frames, deps
    )
    if staged:
        mlp_sum, grad_start = add_and_pass(*mlp_parts, grad_start)
    grad_patch = to_places(grad_start, chips, frames_all)

    ups = wide // width
    early_up = early[4:].reshape(lon, ups, share).swapaxes(0, 1).reshape(ups, width)
    late = jnp.concatenate(
        [frame_sums.reshape(2 * frames, width), gain_sum, early[:4], early_up], 0
    )
    late = late.reshape(-1, lon // 2, 2, share)
    mine = core[0]
    late_got = swap(lax.dynamic_index_in_dim(late, 1 - mine, 2, keepdims=False), "core", 0)
    late = lax.dynamic_index_in_dim(late, mine, 2, keepdims=False) + late_got

    deps = (late_got,)
    qkv_send, qkv_kept = qkv_grad(core, hidden1, pieces, lon, deps)
    qkv_got = swap(qkv_send, "core", 0)

    zed = lax.axis_size("zed")

    if staged:
        sent, kept = first_add(qkv_part, [qkv_kept, qkv_got], share, 3 * width // 2)
        got = cross(sent, 0)
        late = beside(held(late.reshape(late.shape[0], -1), (sent,)))
        sent, kept = second_add(kept, got, (grad_patch, late))
        got = cross(sent, 1)
        parts = third_add(kept, got)
        deps = (parts[0],)
        parts = [parts[0]] + [up_zed(part, up) for up, part in enumerate(parts) if up]
        mlp_sum = held(mlp_sum, deps)
        late = held(late, deps)
        tall = wide // lon
        sum_down, sum_up, sum_out = spread(
            mlp_sum, swap(mlp_sum, "lat", 0), [(tall, width), (share, wide), (share, width)], fill_mlp
        )
        total = last_add(parts, (sum_down,))
        sum_qkv = spread(total, swap(total, "lat", 0), [(share, 3 * width)], fill_qkv)[0]
    else:
        sum_down = plain_sum(down_kept, down_got)
        sum_up = plain_sum(up_kept, up_got)
        sum_up, sum_out = sum_up[:, :wide], sum_up[:, wide:]
        sum_qkv = plain_sum(qkv_kept, qkv_got)
        late = beside(late.reshape(late.shape[0], -1))

    late = jnp.stack([late] + [up_zed(late, up) for up in range(1, zed)])
    late = jnp.take(late, (lax.axis_index("zed") - jnp.arange(zed)) % zed, axis=0)
    late = lax.dynamic_slice_in_dim(late, lax.axis_index(("zed", "yy")) * share, share, 3)
    late = late.reshape(zed, lat, 2, -1, share).swapaxes(0, 1).reshape(chips, -1, share)
    bias_of = late[:, 0 : 2 * frames : 2].reshape(frames_all, share)
    start_of = late[:, 1 : 2 * frames : 2].reshape(frames_all, share)
    rest = late[:, 2 * frames :].sum(0)
    hot = (lead_index[:, None] == jnp.arange(leads, dtype=jnp.int32)[None, :]).astype(F32)
    exact = lax.Precision.HIGHEST
    sum_lead = jnp.dot(hot.T, bias_of, precision=exact)
    sum_chan = jnp.dot(channel_mask.astype(F32).T, start_of, precision=exact)

    shape = (frames_all, rows_here, cols_here, width)
    return (
        out_patch.reshape(shape),
        grad_patch.reshape(shape),
        sum_chan,
        sum_lead,
        rest[0],
        bias_of.sum(0),
        sum_qkv,
        sum_out,
        rest[4],
        rest[2],
        rest[3],
        sum_up,
        rest[5:].reshape(-1),
        sum_down,
        rest[1],
    )


def solution(mesh):
    lat, lon = mesh.shape["lat"], mesh.shape["lon"]
    fine = Mesh(mesh.devices.reshape(lat, lon // 4, 2, 2), ("lat", "zed", "yy", "core"))
    wide = ("zed", "yy", "core")
    places = P(None, "lat", wide, None)
    return jax.shard_map(
        on_device,
        mesh=fine,
        in_specs=(places,) + (P(),) * 15 + (places,),
        out_specs=(
            places,
            places,
            P(None, wide),
            P(None, wide),
            P(wide),
            P(wide),
            P(wide, None),
            P(wide, None),
            P(wide),
            P(wide),
            P(wide),
            P(wide, None),
            P(wide),
            P(wide, None),
            P(wide),
        ),
        check_vma=False,
    )
```

```python
import functools
import math

import jax
import jax.numpy as jnp
from jax import lax
from jax.experimental import pallas as pl
from jax.experimental.pallas import tpu as pltpu
from jax.sharding import Mesh, PartitionSpec as P

HEADS = 12
EPSILON = 1e-06
SCALING = 0.125
LOG2E = math.log2(math.e)
F32 = jnp.float32
BF = jnp.bfloat16
NN = (((1,), (0,)), ((), ()))
NT = (((1,), (1,)), ((), ()))
TN = (((0,), (0,)), ((), ()))
KEY_CHUNK = 512
SMALLEST = 2.0**-90
VM_ATTEND = 62
VM_BACK = 62
VM_MLP = 62
VM_SUM = 62
VM_QKV = 62
COST = 50
DOWN_TILE = 768
MLP_BLOCK = 512
MLP_SPLIT = 1


def mm(a, b, dims=NN):
    return lax.dot_general(a, b, dims, preferred_element_type=F32)


def of_head(value, head, axis=1):
    lane = lax.broadcasted_iota(jnp.int32, value.shape, axis)
    return jnp.where((lane // 64) == head, value, jnp.zeros_like(value))


def sds(shape, dtype):
    return jax.ShapeDtypeStruct(shape, dtype)


def call(kernel, name, grid, ins, outs, scratch=(), flops=0, deps=(), vmem=32):
    given, skipped = len(ins), len(deps)

    def body(*refs):
        kernel(*refs[:given], *refs[given + skipped :])

    anywhere = pl.BlockSpec(memory_space=pl.ANY)
    moved = sum(math.prod(a.shape) * a.dtype.itemsize for a, spec in list(ins) + list(outs))
    return pl.pallas_call(
        body,
        grid=grid,
        in_specs=[spec for a, spec in ins] + [anywhere] * skipped,
        out_specs=[spec for a, spec in outs],
        out_shape=[a for a, spec in outs],
        scratch_shapes=list(scratch),
        compiler_params=pltpu.CompilerParams(vmem_limit_bytes=vmem << 20),
        cost_estimate=pl.CostEstimate(flops=flops // COST, bytes_accessed=moved // COST, transcendentals=0),
        name=name,
    )(*[a for a, spec in ins], *deps)


def attend_kernel(q_ref, k0, k1, v0, v1, o_ref, full_ref, lse_ref):
    count = q_ref.shape[0]
    n = k0.shape[0]
    q = q_ref[...]
    wide_q = q.astype(F32)
    square_q = (wide_q * wide_q).astype(BF)
    turned, squares = [v0[...].T, v1[...].T], []
    for k in (k0, k1):
        wide_k = k[...].astype(F32)
        squares.append((wide_k * wide_k).astype(BF))
    chunk = min(KEY_CHUNK, n)

    def one_head(head, exact):
        qm = of_head(q, head)
        top = None
        if exact:
            for k in (k0, k1):
                for i in range(0, n, chunk):
                    part = jnp.max(mm(k[i : i + chunk], qm, NT), axis=0, keepdims=True)
                    top = part if top is None else jnp.maximum(top, part)
        else:
            pick = of_head(jnp.ones((8, 128), BF), head)
            for square in squares:
                part = jnp.max(mm(pick, square, NT))
                top = part if top is None else jnp.maximum(top, part)
            top = jnp.sqrt(mm(pick, square_q, NT)[0:1] * (top * 1.05))
        out = total = None
        for k, values in ((k0, turned[0]), (k1, turned[1])):
            for i in range(0, n, chunk):
                probs = jnp.exp2(mm(k[i : i + chunk], qm, NT) - top)
                part = jnp.sum(probs, axis=0, keepdims=True)
                total = part if total is None else total + part
                part = mm(values[:, i : i + chunk], probs.astype(BF))
                out = part if out is None else out + part
        lse = jnp.broadcast_to(top + jnp.log2(total), (64, count))
        return out[64 * head : 64 * head + 64] / total, lse, jnp.min(total)

    def run(exact):
        first, second = one_head(0, exact), one_head(1, exact)
        out = jnp.concatenate([first[0], second[0]], 0).T
        o_ref[...] = out.astype(BF)
        full_ref[...] = out
        lse_ref[...] = jnp.concatenate([first[1], second[1]], 0).T
        return jnp.minimum(first[2], second[2])

    least = run(False)

    @pl.when(jnp.logical_not(least >= SMALLEST))
    def _():
        run(True)


def attend(q, kv_own, kv_peer, frames):
    tokens, width = q.shape
    pairs = width // 128
    n = tokens // frames
    qs = pl.BlockSpec((n, 128), lambda f, p: (f, p))
    vs = pl.BlockSpec((n, 128), lambda f, p: (f, pairs + p))
    return call(
        attend_kernel,
        "attend",
        (frames, pairs),
        [(q, qs), (kv_own, qs), (kv_peer, qs), (kv_own, vs), (kv_peer, vs)],
        [
            (sds((tokens, width), BF), qs),
            (sds((tokens, width), F32), qs),
            (sds((tokens, width), F32), qs),
        ],
        flops=30_000_000_000,
        vmem=VM_ATTEND,
    )


def attend_back_kernel(
    q_ref, k0, k1, v0, v1, go_ref, o_ref, lse_ref, dq_ref, dk0, dk1, dv0, dv1, dka, dva
):
    n = k0.shape[0]
    q = q_ref[...]
    go = go_ref[...]
    turned_q, turned_go = q.T, go.T
    prod = go.astype(F32) * o_ref[...]
    qms = [of_head(q, head) for head in range(2)]
    goms = [of_head(go, head) for head in range(2)]
    lses = [lse_ref[:, 64 * head : 64 * head + 1] for head in range(2)]
    deltas = [jnp.sum(of_head(prod, head), axis=1, keepdims=True) for head in range(2)]
    chunk = min(KEY_CHUNK, n)
    dq = None
    for part, (k, v) in enumerate(((k0, v0), (k1, v1))):
        for i in range(0, n, chunk):
            keys = k[i : i + chunk]
            vals = v[i : i + chunk]
            for head in range(2):
                lanes = slice(64 * head, 64 * head + 64)
                probs = jnp.exp2(mm(qms[head], keys, NT) - lses[head])
                ds = (probs * (mm(goms[head], vals, NT) - deltas[head])).astype(BF)
                dva[part, lanes, i : i + chunk] = mm(turned_go, probs.astype(BF))[lanes]
                dka[part, lanes, i : i + chunk] = mm(turned_q, ds)[lanes]
                term = mm(ds, of_head(keys, head))
                dq = term if dq is None else dq + term
    dq_ref[...] = (dq * SCALING).astype(BF)
    back = 1.0 / LOG2E
    for part, (dk, dv) in enumerate(((dk0, dv0), (dk1, dv1))):
        dk[...] = (dka[part].T * back).astype(BF)
        dv[...] = dva[part].T.astype(BF)


def attend_back(q, kv_own, kv_peer, go, att, lse, frames, first, count, deps):
    tokens, width = q.shape
    pairs = width // 128
    n = tokens // frames
    qs = pl.BlockSpec((n, 128), lambda f, p: (f, first + p))
    vs = pl.BlockSpec((n, 128), lambda f, p: (f, pairs + first + p))
    out = pl.BlockSpec((n, 128), lambda f, p: (f, p))
    shape = sds((tokens, 128 * count), BF)
    return call(
        attend_back_kernel,
        "attend_back",
        (frames, count),
        [(q, qs), (kv_own, qs), (kv_peer, qs), (kv_own, vs), (kv_peer, vs), (go, qs), (att, qs), (lse, qs)],
        [(shape, out)] * 5,
        [pltpu.VMEM((2, 128, n), F32)] * 2,
        11_000_000_000 * count,
        deps,
        VM_BACK,
    )


def normed_of(value):
    row_mean = jnp.mean(value, axis=-1, keepdims=True)
    centered = value - row_mean
    inverse = lax.rsqrt(jnp.mean(centered * centered, axis=-1, keepdims=True) + EPSILON)
    return centered * inverse, inverse


def norm_back(grad_hat, normed, inverse):
    first = jnp.mean(grad_hat, axis=-1, keepdims=True)
    second = jnp.mean(grad_hat * normed, axis=-1, keepdims=True)
    return inverse * (grad_hat - first - normed * second)


def rows_of(block, width):
    return pl.BlockSpec((block, width), lambda i: (i, 0))


def whole_of(shape):
    return pl.BlockSpec(shape, lambda i: (0,) * len(shape))


SMALL = pl.BlockSpec(memory_space=pltpu.SMEM)


def qkv_kernel(x_ref, chan_ref, shift_ref, gain_ref, w, h_ref, kv_ref, q_ref):
    width = x_ref.shape[1]
    normed, inverse = normed_of(x_ref[...].astype(F32) + chan_ref[0])
    hidden = (normed * gain_ref[...] + shift_ref[0]).astype(BF)
    h_ref[...] = hidden
    kv_ref[...] = mm(hidden, w[:, width:]).astype(BF)
    q_ref[...] = (mm(hidden, w[:, :width]) * (SCALING * LOG2E)).astype(BF)


def qkv_of(x, chan_add, shift, gain, weight, frames, deps):
    count, width = x.shape
    block = 256
    per = count // frames // block
    frame = pl.BlockSpec((1, 1, width), lambda i: (i // per, 0, 0))
    narrow = rows_of(block, width)
    return call(
        qkv_kernel,
        "qkv",
        (count // block,),
        [
            (x, narrow),
            (chan_add, frame),
            (shift, frame),
            (gain, whole_of((1, width))),
            (weight, whole_of(weight.shape)),
        ],
        [
            (sds((count, width), BF), narrow),
            (sds((count, 2 * width), BF), rows_of(block, 2 * width)),
            (sds((count, width), BF), narrow),
        ],
        flops=3_600_000_000,
        deps=deps,
        vmem=VM_QKV,
    )


ROOT = math.sqrt(2 / math.pi)
CUBE = ROOT * 0.044715


def gelu_both(x):
    square = x * x
    t = jnp.tanh(x * (ROOT + CUBE * square))
    half = 0.5 * t + 0.5
    slope = half + (0.5 * x) * (1.0 - t * t) * (ROOT + (3.0 * CUBE) * square)
    return x * half, slope


def mlp_kernel(
    x_ref,
    chan_ref,
    att_ref,
    g_ref,
    rows_ref,
    up_bias_ref,
    wo_any,
    wu_any,
    wd_any,
    res_ref,
    act_ref,
    gpre_ref,
    hid_ref,
    mid_ref,
    branch_ref,
    gatt_ref,
    sums_ref,
    wo,
    wu,
    wd,
    sems,
):
    step = pl.program_id(0)
    width = x_ref.shape[1]
    copies = [
        pltpu.make_async_copy(wo_any, wo, sems.at[0]),
        pltpu.make_async_copy(wu_any, wu, sems.at[1]),
        pltpu.make_async_copy(wd_any, wd, sems.at[2]),
    ]

    @pl.when(step == 0)
    def _():
        for c in copies:
            c.start()
        sums_ref[...] = jnp.zeros_like(sums_ref)
        copies[0].wait()

    out_bias, gain, shift, down_bias = [rows_ref[i : i + 1] for i in range(4)]
    middle = x_ref[...].astype(F32) + chan_ref[0] + mm(att_ref[...], wo[...]) + out_bias
    normed, inverse = normed_of(middle)
    hidden = (normed * gain + shift).astype(BF)
    hid_ref[...] = hidden
    g = g_ref[...]

    @pl.when(step == 0)
    def _():
        copies[1].wait()
        copies[2].wait()

    result = middle + down_bias
    grad_hidden = None
    part = width // MLP_SPLIT
    spans = [pl.ds(i * part, part) for i in range(wu.shape[1] // part)]

    def products(cols):
        return mm(hidden, wu[:, cols]), mm(g, wd[cols, :], NT)

    ready = products(spans[0])
    for i, cols in enumerate(spans):
        pre, back = ready
        if i + 1 < len(spans):
            ready = products(spans[i + 1])
        act, slope = gelu_both(pre + up_bias_ref[:, cols])
        act = act.astype(BF)
        act_ref[:, cols] = act
        grad_pre = (back * slope).astype(BF)
        gpre_ref[:, cols] = grad_pre
        at = i % MLP_SPLIT * part
        row = 4 + i // MLP_SPLIT
        sums_ref[row : row + 1, at : at + part] += jnp.sum(
            grad_pre.astype(F32), axis=0, keepdims=True
        )
        result = result + mm(act, wd[cols, :])
        term = mm(grad_pre, wu[:, cols], NT)
        grad_hidden = term if grad_hidden is None else grad_hidden + term
    res_ref[...] = result.astype(BF)
    g = g.astype(F32)
    sums_ref[0:1] += jnp.sum(g, axis=0, keepdims=True)
    sums_ref[1:2] += jnp.sum(grad_hidden * normed, axis=0, keepdims=True)
    sums_ref[2:3] += jnp.sum(grad_hidden, axis=0, keepdims=True)
    grad_middle = g + norm_back(grad_hidden * gain, normed, inverse)
    mid_ref[...] = grad_middle
    branch = grad_middle.astype(BF)
    branch_ref[...] = branch
    sums_ref[3:4] += jnp.sum(branch.astype(F32), axis=0, keepdims=True)
    gatt_ref[...] = mm(branch, wo[...], NT).astype(BF)


def mlp(x, chan_add, att, g, rows, up_bias, wo, wu, wd, frames):
    count, width = x.shape
    wide = wu.shape[1]
    block = MLP_BLOCK
    per = count // frames // block
    narrow, broad = rows_of(block, width), rows_of(block, wide)
    anywhere = pl.BlockSpec(memory_space=pl.ANY)
    return call(
        mlp_kernel,
        "mlp",
        (count // block,),
        [
            (x, narrow),
            (chan_add, pl.BlockSpec((1, 1, width), lambda i: (i // per, 0, 0))),
            (att, narrow),
            (g, narrow),
            (rows, whole_of((4, width))),
            (up_bias, whole_of((1, wide))),
            (wo, anywhere),
            (wu, anywhere),
            (wd, anywhere),
        ],
        [
            (sds((count, width), BF), narrow),
            (sds((count, wide), BF), broad),
            (sds((count, wide), BF), broad),
            (sds((count, width), BF), narrow),
            (sds((count, width), F32), narrow),
            (sds((count, width), BF), narrow),
            (sds((count, width), BF), narrow),
            (sds((4 + wide // width, width), F32), whole_of((4 + wide // width, width))),
        ],
        [
            pltpu.VMEM(wo.shape, BF),
            pltpu.VMEM(wu.shape, BF),
            pltpu.VMEM(wd.shape, BF),
            pltpu.SemaphoreType.DMA((3,)),
        ],
        25_000_000_000,
        vmem=VM_MLP,
    )


def down_grad_kernel(core_ref, act_ref, g_ref, send_ref, keep_ref, scr):
    core = core_ref[0]
    places, share, width = scr.shape[1:]
    scr[...] = mm(act_ref[...], g_ref[...], TN).reshape(scr.shape)
    keep_ref[...] = scr[:, core].astype(BF)
    send_ref[...] = scr[:, 1 - core].astype(BF)


def down_grad(core, act, g, lon, deps):
    count, wide = act.shape
    width = g.shape[1]
    share = wide // lon
    tile = DOWN_TILE
    chips = tile // (2 * share)
    out = sds((lon // 2, share, width), BF)
    spec = pl.BlockSpec((chips, share, width), lambda i: (i, 0, 0))
    return call(
        down_grad_kernel,
        "down_grad",
        (wide // tile,),
        [(core, SMALL), (act, pl.BlockSpec((count, tile), lambda i: (0, i))), (g, whole_of((count, width)))],
        [(out, spec), (out, spec)],
        [pltpu.VMEM((chips, 2, share, width), F32)],
        4_800_000_000,
        deps,
        VM_SUM,
    )


def up_grad_kernel(core_ref, hid_ref, gpre_ref, att_ref, branch_ref, send_ref, keep_ref, turned, scr):
    core = core_ref[0]
    step = pl.program_id(0)
    last = pl.num_programs(0) - 1

    @pl.when(step == 0)
    def _():
        turned[...] = hid_ref[...].T

    @pl.when(step < last)
    def _():
        scr[...] = mm(turned[...], gpre_ref[...]).reshape(scr.shape)

    @pl.when(step == last)
    def _():
        scr[...] = mm(att_ref[...], branch_ref[...], TN).reshape(scr.shape)

    keep_ref[...] = scr[:, core].astype(BF)
    send_ref[...] = scr[:, 1 - core].astype(BF)


def up_grad(core, hidden, gpre, att, branch, lon):
    count, width = hidden.shape
    wide = gpre.shape[1]
    share = width // lon
    last = wide // width - 1
    out = sds((lon // 2, share, wide + width), BF)
    spec = pl.BlockSpec((lon // 2, share, width), lambda i: (0, 0, i))
    full = whole_of((count, width))
    return call(
        up_grad_kernel,
        "up_grad",
        (last + 2,),
        [
            (core, SMALL),
            (hidden, full),
            (gpre, pl.BlockSpec((count, width), lambda i: (0, jnp.minimum(i, last)))),
            (att, full),
            (branch, full),
        ],
        [(out, spec), (out, spec)],
        [pltpu.VMEM((width, count), BF), pltpu.VMEM((lon // 2, 2, share, width), F32)],
        6_000_000_000,
        vmem=VM_SUM,
    )


def fill_part(out, pieces, part):
    at = 0
    for dq, dk0, dv0, got_k, got_v in pieces:
        size = dq.shape[1]
        if part == 0:
            out[:, at : at + size] = dq[...]
        elif part == 1:
            out[:, at : at + size] = dk0[...] + got_k[...]
        else:
            out[:, at : at + size] = dv0[...] + got_v[...]
        at += size


def groups_of(refs):
    return [refs[i : i + 5] for i in range(0, len(refs), 5)]


def qkv_grad_kernel(core_ref, hid_ref, *refs):
    pieces = groups_of(refs[:-5])
    send_ref, keep_ref, turned, grad, scr = refs[-5:]
    core = core_ref[0]
    step = pl.program_id(0)

    @pl.when(step == 0)
    def _():
        turned[...] = hid_ref[...].T

    for part in range(3):

        @pl.when(step == part)
        def _():
            fill_part(grad, pieces, part)

    scr[...] = mm(turned[...], grad[...]).reshape(scr.shape)
    keep_ref[...] = scr[:, core].astype(BF)
    send_ref[...] = scr[:, 1 - core].astype(BF)


def qkv_grad(core, hidden, pieces, lon, deps):
    count, width = hidden.shape
    share = width // lon
    out = sds((lon // 2, share, 3 * width), BF)
    spec = pl.BlockSpec((lon // 2, share, width), lambda i: (0, 0, i))
    return call(
        qkv_grad_kernel,
        "qkv_grad",
        (3,),
        [(core, SMALL), (hidden, whole_of((count, width)))]
        + [(a, whole_of(a.shape)) for group in pieces for a in group],
        [(out, spec), (out, spec)],
        [
            pltpu.VMEM((width, count), BF),
            pltpu.VMEM((count, width), BF),
            pltpu.VMEM((lon // 2, 2, share, width), F32),
        ],
        3_600_000_000,
        deps,
        VM_SUM,
    )


def first_back_kernel_of(groups, frame_blocks):
    def kernel(*refs):
        pieces = groups_of(refs[: 5 * groups])
        x_ref, chan_ref, gain_ref, mid_ref, w, patch_ref, frame_ref, gain_sum, qkv_ref = refs[5 * groups :]
        step = pl.program_id(0)
        width = x_ref.shape[1]
        for part in range(3):
            fill_part(qkv_ref.at[:, part * width : (part + 1) * width], pieces, part)
        grad_hidden = mm(qkv_ref[...], w[...], NT)
        normed, inverse = normed_of(x_ref[...].astype(F32) + chan_ref[0])
        grad_start = mid_ref[...] + norm_back(grad_hidden * gain_ref[...], normed, inverse)
        patch_ref[...] = grad_start.astype(BF)

        @pl.when(step == 0)
        def _():
            gain_sum[...] = jnp.zeros_like(gain_sum)

        @pl.when(lax.rem(step, frame_blocks) == 0)
        def _():
            frame_ref[...] = jnp.zeros_like(frame_ref)

        gain_sum[...] += jnp.sum(grad_hidden * normed, axis=0, keepdims=True)
        frame_ref[0, 0:1] += jnp.sum(grad_hidden, axis=0, keepdims=True)
        frame_ref[0, 1:2] += jnp.sum(grad_start, axis=0, keepdims=True)

    return kernel


def first_back(pieces, x, chan_add, gain, grad_middle, weight, frames, deps):
    count, width = x.shape
    block = 256
    per = count // frames // block
    ins = [(a, rows_of(block, a.shape[1])) for group in pieces for a in group]
    return call(
        first_back_kernel_of(len(pieces), per),
        "first_back",
        (count // block,),
        ins
        + [
            (x, rows_of(block, width)),
            (chan_add, pl.BlockSpec((1, 1, width), lambda i: (i // per, 0, 0))),
            (gain, whole_of((1, width))),
            (grad_middle, rows_of(block, width)),
            (weight, whole_of(weight.shape)),
        ],
        [
            (sds((count, width), BF), rows_of(block, width)),
            (sds((frames, 2, width), F32), pl.BlockSpec((1, 2, width), lambda i: (i // per, 0, 0))),
            (sds((1, width), F32), whole_of((1, width))),
        ],
        [pltpu.VMEM((block, 3 * width), BF)],
        3_600_000_000,
        deps,
        VM_SUM,
    )


def swap_pairs(size, bit):
    return [(i, i ^ (1 << bit)) for i in range(size)]


def bits_of(size):
    return size.bit_length() - 1


def my_bit(axis, bit):
    return ((lax.axis_index(axis) >> bit) & 1).astype(jnp.int32).reshape(1)


def swap(value, axis, bit):
    return lax.ppermute(value, axis, swap_pairs(lax.axis_size(axis), bit))


def cross(value, turn):
    pairs = []
    for i in range(8):
        lat_next = (i & 1) == turn
        pairs.append((i, i ^ (4 if lat_next else 2)))
    return lax.ppermute(value, ("lat", "yy", "core"), pairs)


EVERY = slice(None)


def both(kept_ref, got_ref, *at):
    return (kept_ref[at].astype(F32) + got_ref[at].astype(F32)).astype(BF)


def mlp_part(ins, out, at, yy, half):
    kept_d, got_d, kept_u, got_u = ins
    rows, width = kept_d.shape[1:]
    share = kept_u.shape[1]
    wide = kept_u.shape[2] - width

    @pl.when(half == 0)
    def _():
        out[0, at, :rows] = both(kept_d, got_d, yy)
        out[0, at, rows:] = both(kept_u, got_u, yy, slice(0, share // 2), slice(wide, None))

    @pl.when(half == 1)
    def _():
        for c in range(wide // width):
            out[0, at, c * share : (c + 1) * share] = both(
                kept_u, got_u, yy, EVERY, slice(c * width, (c + 1) * width)
            )
        out[0, at, rows:] = both(kept_u, got_u, yy, slice(share // 2, None), slice(wide, None))


def qkv_part(ins, out, at, yy, half):
    kept, got = ins
    cols = kept.shape[2] // 2
    for side in range(2):

        @pl.when(half == side)
        def _():
            out[0, at] = both(kept, got, yy, slice(None), slice(side * cols, (side + 1) * cols))


def first_add(part, ins, rows, cols, deps=()):
    zed = ins[0].shape[0] // 2

    def kernel(where_ref, *refs):
        core, mine = where_ref[0], where_ref[1]
        for which, out in zip((1 - mine, mine), refs[len(ins) :]):
            for at in range(2):
                yy = jnp.where(core == 0, at, which)
                half = jnp.where(core == 0, which, at)
                part(refs[: len(ins)], out, at, yy, half)

    core = my_bit("core", 0)
    mine = jnp.where(core == 0, my_bit("lat", 0), my_bit("yy", 0))
    out = sds((zed, 2, rows, cols), BF)
    spec = pl.BlockSpec((1, 2, rows, cols), lambda i: (i, 0, 0, 0))
    return call(
        kernel,
        "first_add",
        (zed,),
        [(jnp.concatenate([core, mine]), SMALL)]
        + [(a, pl.BlockSpec((2,) + a.shape[1:], lambda i: (i, 0, 0))) for a in ins],
        [(out, spec)] * 2,
        deps=deps,
        vmem=VM_SUM,
    )


def second_add(kept, got, deps=()):
    zed, two, rows, cols = kept.shape

    def kernel(mine_ref, kept_ref, got_ref, send_ref, keep_ref):
        mine = mine_ref[0]
        send_ref[0] = both(kept_ref, got_ref, 0, 1 - mine)
        keep_ref[0] = both(kept_ref, got_ref, 0, mine)

    mine = jnp.where(my_bit("core", 0) == 0, my_bit("yy", 0), my_bit("lat", 0))
    spec = pl.BlockSpec((1, 2, rows, cols), lambda i: (i, 0, 0, 0))
    out = pl.BlockSpec((1, rows, cols), lambda i: (i, 0, 0))
    return call(
        kernel,
        "second_add",
        (zed,),
        [(mine, SMALL), (kept, spec), (got, spec)],
        [(sds((zed, rows, cols), BF), out)] * 2,
        deps=deps,
        vmem=VM_SUM,
    )


def third_add(kept, got, deps=()):
    zed, rows, cols = kept.shape

    def kernel(me_ref, kept_ref, got_ref, *outs):
        for up, out in enumerate(outs):
            out[...] = both(kept_ref, got_ref, lax.rem(me_ref[0] + up, zed))

    me = lax.axis_index("zed").astype(jnp.int32).reshape(1)
    return call(
        kernel,
        "third_add",
        (1,),
        [(me, SMALL), (kept, whole_of(kept.shape)), (got, whole_of(kept.shape))],
        [(sds((rows, cols), BF), whole_of((rows, cols)))] * zed,
        deps=deps,
        vmem=VM_SUM,
    )


def cut_lead(kept, got, bit, deps=()):
    zed, rows, cols = kept.shape

    def kernel(mine_ref, kept_ref, got_ref, send_ref, keep_ref):
        mine = mine_ref[0]
        send_ref[0] = both(kept_ref, got_ref, 1 - mine)
        keep_ref[0] = both(kept_ref, got_ref, mine)

    spec = pl.BlockSpec((2, rows, cols), lambda i: (i, 0, 0))
    out = pl.BlockSpec((1, rows, cols), lambda i: (i, 0, 0))
    return call(
        kernel,
        "cut_lead",
        (zed // 2,),
        [(my_bit("zed", bit), SMALL), (kept, spec), (got, spec)],
        [(sds((zed // 2, rows, cols), BF), out)] * 2,
        deps=deps,
        vmem=VM_SUM,
    )


def up_zed(value, up):
    zed = lax.axis_size("zed")
    return lax.ppermute(value, "zed", [(i, (i + up) % zed) for i in range(zed)])


def last_add(parts, deps=()):
    rows, cols = parts[0].shape

    def kernel(*refs):
        total = refs[0][...].astype(F32)
        for ref in refs[1:-1]:
            total = total + ref[...].astype(F32)
        refs[-1][...] = total.astype(BF)

    spec = whole_of((rows, cols))
    return call(
        kernel,
        "last_add",
        (1,),
        [(a, spec) for a in parts],
        [(sds((rows, cols), BF), spec)],
        deps=deps,
        vmem=VM_SUM,
    )[0]


def add_and_pass(kept, got, passed):
    rows, cols = kept.shape

    def kernel(kept_ref, got_ref, passed_ref, out_ref, same_ref):
        out_ref[...] = both(kept_ref, got_ref, Ellipsis)

    spec = whole_of((rows, cols))
    anywhere = pl.BlockSpec(memory_space=pl.ANY)
    return pl.pallas_call(
        kernel,
        grid=(1,),
        in_specs=[spec, spec, anywhere],
        out_specs=[spec, anywhere],
        out_shape=[sds((rows, cols), BF), sds(passed.shape, passed.dtype)],
        input_output_aliases={2: 1},
        compiler_params=pltpu.CompilerParams(vmem_limit_bytes=VM_SUM << 20),
        name="add_and_pass",
    )(kept, got, passed)


def spread(mine, other, shapes, fill, deps=()):
    def kernel(high_ref, mine_ref, other_ref, *outs):
        @pl.when(high_ref[0] == 0)
        def _():
            fill(mine_ref, other_ref, outs)

        @pl.when(high_ref[0] == 1)
        def _():
            fill(other_ref, mine_ref, outs)

    spec = whole_of(mine.shape)
    return call(
        kernel,
        "spread",
        (1,),
        [(my_bit("lat", 0), SMALL), (mine, spec), (other, spec)],
        [(sds(shape, F32), whole_of(shape)) for shape in shapes],
        deps=deps,
        vmem=VM_SUM,
    )


def fill_qkv(low, high, outs):
    cols = low.shape[1]
    outs[0][:, :cols] = low[...].astype(F32)
    outs[0][:, cols:] = high[...].astype(F32)


def fill_mlp(low, high, outs):
    down, up, out = outs
    tall, share, width = down.shape[0], up.shape[0], down.shape[1]
    down[...] = low[:tall].astype(F32)
    for c in range(up.shape[1] // width):
        up[:, c * width : (c + 1) * width] = high[c * share : (c + 1) * share].astype(F32)
    out[: share // 2] = low[tall:].astype(F32)
    out[share // 2 :] = high[tall:].astype(F32)


def beside(value):
    value = value[None]
    for axis in ("yy", "lat"):
        for bit in range(bits_of(lax.axis_size(axis))):
            other = swap(value, axis, bit)
            high = my_bit(axis, bit)[0] == 1
            value = jnp.where(
                high, jnp.concatenate([other, value], 0), jnp.concatenate([value, other], 0)
            )
    return value


def held(value, deps):
    def kernel(value_ref, out_ref):
        out_ref[...] = value_ref[...]

    spec = whole_of(value.shape)
    return call(
        kernel, "held", (1,), [(value, spec)], [(sds(value.shape, value.dtype), spec)], deps=deps
    )[0]


def plain_sum(kept, got):
    value = lax.psum_scatter(kept + got, ("zed", "yy"), scatter_dimension=0, tiled=True)[0]
    return lax.psum(value.astype(F32), "lat")


def to_frames(value, chips):
    frames_all, patches, width = value.shape
    frames = frames_all // chips
    value = lax.all_to_all(value, ("lat", "zed", "yy"), 0, 0, tiled=True)
    if frames > 1:
        value = value.reshape(chips, frames, patches, width).swapaxes(0, 1)
    return value.reshape(-1, width)


def to_places(value, chips, frames_all):
    width = value.shape[-1]
    frames = frames_all // chips
    if frames > 1:
        value = value.reshape(frames, chips, -1, width).swapaxes(0, 1)
    value = value.reshape(frames_all, -1, width)
    return lax.all_to_all(value, ("lat", "zed", "yy"), 0, 0, tiled=True)


def on_device(
    tokens,
    channel_mask,
    lead_index,
    chan_embed,
    lead_embed,
    norm1_gain,
    norm1_bias,
    qkv_weight,
    out_weight,
    out_bias,
    norm2_gain,
    norm2_bias,
    up_weight,
    up_bias,
    down_weight,
    down_bias,
    cotangent,
):
    lat = lax.axis_size("lat")
    lon = 4 * lax.axis_size("zed")
    chips = lat * (lon // 2)
    frames_all, rows_here, cols_here, width = tokens.shape
    frames = frames_all // chips
    leads = lead_embed.shape[0]
    wide = up_weight.shape[1]
    share = width // lon
    core = my_bit("core", 0)

    x = to_frames(tokens.reshape(frames_all, -1, width), chips)
    flat = cotangent.reshape(frames_all, -1, width)
    g = to_frames(flat, chips)
    count = x.shape[0]

    first = lax.axis_index(("lat", "zed", "yy")) * frames
    mask_here = lax.dynamic_slice_in_dim(channel_mask, first, frames, 0).astype(BF)
    lead_here = lax.dynamic_slice_in_dim(lead_index, first, frames, 0)
    lead_onehot = (lead_here[:, None] == jnp.arange(leads, dtype=jnp.int32)[None, :]).astype(BF)
    chan_add = mm(mask_here, chan_embed)[:, None, :]
    shift1 = (mm(lead_onehot, lead_embed) + norm1_bias.astype(F32))[:, None, :]
    gain1 = norm1_gain.astype(F32)[None]
    rows2 = jnp.stack([out_bias, norm2_gain, norm2_bias, down_bias]).astype(F32)

    hidden1, kv_own, queries = qkv_of(x, chan_add, shift1, gain1, qkv_weight, frames, (flat,))
    kv_peer = swap(kv_own, "core", 0)
    attended, attended32, lse = attend(queries, kv_own, kv_peer, frames)

    result, activ, grad_pre, hidden2, grad_middle, grad_branch, grad_att, early = mlp(
        x,
        chan_add,
        attended,
        g,
        rows2,
        up_bias.astype(F32)[None],
        out_weight,
        up_weight,
        down_weight,
        frames,
    )
    out_patch = to_places(result, chips, frames_all)
    up_send, up_kept = up_grad(core, hidden2, grad_pre, attended, grad_branch, lon)
    up_got = swap(up_send, "core", 0)
    down_send, down_kept = down_grad(core, activ, g, lon, (up_send,))
    down_got = swap(down_send, "core", 0)

    staged = lat == 2
    rows = down_kept.shape[1] + share // 2
    pieces, pair = [], 0
    deps = (down_kept,)
    if staged:
        sent, kept = first_add(mlp_part, [down_kept, down_got, up_kept, up_got], rows, width)
        got = cross(sent, 0)
        deps = (sent,)
    pairs = width // 128
    plan = [pairs - 2, 1, 1]
    for at, size in enumerate(plan):
        dq, dk0, dk1, dv0, dv1 = attend_back(
            queries, kv_own, kv_peer, grad_att, attended32, lse, frames, pair, size, deps
        )
        pieces.append((dq, dk0, dv0, swap(dk1, "core", 0), swap(dv1, "core", 0)))
        pair += size
        deps = (dq,)
        if staged and at == 0:
            sent, kept = second_add(kept, got, deps)
            got = cross(sent, 1)
            deps = (sent, dq)
        if staged and at == 1:
            sent, kept = cut_lead(kept, got, 0, deps)
            got = swap(sent, "zed", 0)
            deps = (sent, dq)

    if staged:
        for bit in range(1, bits_of(lax.axis_size("zed"))):
            sent, kept = cut_lead(kept, got, bit, deps)
            got = swap(sent, "zed", bit)
            deps = (sent, out_patch)
        mlp_parts = [kept[0], got[0]]
    grad_start, frame_sums, gain_sum = first_back(
        pieces, x, chan_add, gain1, grad_middle, qkv_weight, frames, deps
    )
    if staged:
        mlp_sum, grad_start = add_and_pass(*mlp_parts, grad_start)
    grad_patch = to_places(grad_start, chips, frames_all)

    ups = wide // width
    early_up = early[4:].reshape(lon, ups, share).swapaxes(0, 1).reshape(ups, width)
    late = jnp.concatenate(
        [frame_sums.reshape(2 * frames, width), gain_sum, early[:4], early_up], 0
    )
    late = late.reshape(-1, lon // 2, 2, share)
    mine = core[0]
    late_got = swap(lax.dynamic_index_in_dim(late, 1 - mine, 2, keepdims=False), "core", 0)
    late = lax.dynamic_index_in_dim(late, mine, 2, keepdims=False) + late_got

    deps = (late_got,)
    qkv_send, qkv_kept = qkv_grad(core, hidden1, pieces, lon, deps)
    qkv_got = swap(qkv_send, "core", 0)

    zed = lax.axis_size("zed")

    if staged:
        sent, kept = first_add(qkv_part, [qkv_kept, qkv_got], share, 3 * width // 2)
        got = cross(sent, 0)
        late = beside(held(late.reshape(late.shape[0], -1), (sent,)))
        sent, kept = second_add(kept, got, (grad_patch, late))
        got = cross(sent, 1)
        parts = third_add(kept, got)
        deps = (parts[0],)
        parts = [parts[0]] + [up_zed(part, up) for up, part in enumerate(parts) if up]
        mlp_sum = held(mlp_sum, deps)
        late = held(late, deps)
        tall = wide // lon
        sum_down, sum_up, sum_out = spread(
            mlp_sum, swap(mlp_sum, "lat", 0), [(tall, width), (share, wide), (share, width)], fill_mlp
        )
        total = last_add(parts, (sum_down,))
        sum_qkv = spread(total, swap(total, "lat", 0), [(share, 3 * width)], fill_qkv)[0]
    else:
        sum_down = plain_sum(down_kept, down_got)
        sum_up = plain_sum(up_kept, up_got)
        sum_up, sum_out = sum_up[:, :wide], sum_up[:, wide:]
        sum_qkv = plain_sum(qkv_kept, qkv_got)
        late = beside(late.reshape(late.shape[0], -1))

    late = jnp.stack([late] + [up_zed(late, up) for up in range(1, zed)])
    late = jnp.take(late, (lax.axis_index("zed") - jnp.arange(zed)) % zed, axis=0)
    late = lax.dynamic_slice_in_dim(late, lax.axis_index(("zed", "yy")) * share, share, 3)
    late = late.reshape(zed, lat, 2, -1, share).swapaxes(0, 1).reshape(chips, -1, share)
    bias_of = late[:, 0 : 2 * frames : 2].reshape(frames_all, share)
    start_of = late[:, 1 : 2 * frames : 2].reshape(frames_all, share)
    rest = late[:, 2 * frames :].sum(0)
    hot = (lead_index[:, None] == jnp.arange(leads, dtype=jnp.int32)[None, :]).astype(F32)
    exact = lax.Precision.HIGHEST
    sum_lead = jnp.dot(hot.T, bias_of, precision=exact)
    sum_chan = jnp.dot(channel_mask.astype(F32).T, start_of, precision=exact)

    shape = (frames_all, rows_here, cols_here, width)
    return (
        out_patch.reshape(shape),
        grad_patch.reshape(shape),
        sum_chan,
        sum_lead,
        rest[0],
        bias_of.sum(0),
        sum_qkv,
        sum_out,
        rest[4],
        rest[2],
        rest[3],
        sum_up,
        rest[5:].reshape(-1),
        sum_down,
        rest[1],
    )


def solution(mesh):
    lat, lon = mesh.shape["lat"], mesh.shape["lon"]
    fine = Mesh(mesh.devices.reshape(lat, lon // 4, 2, 2), ("lat", "zed", "yy", "core"))
    wide = ("zed", "yy", "core")
    places = P(None, "lat", wide, None)
    return jax.shard_map(
        on_device,
        mesh=fine,
        in_specs=(places,) + (P(),) * 15 + (places,),
        out_specs=(
            places,
            places,
            P(None, wide),
            P(None, wide),
            P(wide),
            P(wide),
            P(wide, None),
            P(wide, None),
            P(wide),
            P(wide),
            P(wide),
            P(wide, None),
            P(wide),
            P(wide, None),
            P(wide),
        ),
        check_vma=False,
    )
```

```python
import functools
import math

import jax
import jax.numpy as jnp
from jax import lax
from jax.experimental import pallas as pl
from jax.experimental.pallas import tpu as pltpu
from jax.sharding import Mesh, PartitionSpec as P

HEADS = 12
EPSILON = 1e-06
SCALING = 0.125
LOG2E = math.log2(math.e)
F32 = jnp.float32
BF = jnp.bfloat16
NN = (((1,), (0,)), ((), ()))
NT = (((1,), (1,)), ((), ()))
TN = (((0,), (0,)), ((), ()))
KEY_CHUNK = 512
SMALLEST = 2.0**-90
VM_ATTEND = 62
VM_BACK = 62
VM_MLP = 62
VM_SUM = 62
VM_QKV = 62
COST = 50
DOWN_TILE = 768
MLP_BLOCK = 512
MLP_SPLIT = 1


def mm(a, b, dims=NN):
    return lax.dot_general(a, b, dims, preferred_element_type=F32)


def of_head(value, head, axis=1):
    lane = lax.broadcasted_iota(jnp.int32, value.shape, axis)
    return jnp.where((lane // 64) == head, value, jnp.zeros_like(value))


def sds(shape, dtype):
    return jax.ShapeDtypeStruct(shape, dtype)


def call(kernel, name, grid, ins, outs, scratch=(), flops=0, deps=(), vmem=32):
    given, skipped = len(ins), len(deps)

    def body(*refs):
        kernel(*refs[:given], *refs[given + skipped :])

    anywhere = pl.BlockSpec(memory_space=pl.ANY)
    moved = sum(math.prod(a.shape) * a.dtype.itemsize for a, spec in list(ins) + list(outs))
    return pl.pallas_call(
        body,
        grid=grid,
        in_specs=[spec for a, spec in ins] + [anywhere] * skipped,
        out_specs=[spec for a, spec in outs],
        out_shape=[a for a, spec in outs],
        scratch_shapes=list(scratch),
        compiler_params=pltpu.CompilerParams(vmem_limit_bytes=vmem << 20),
        cost_estimate=pl.CostEstimate(flops=flops // COST, bytes_accessed=moved // COST, transcendentals=0),
        name=name,
    )(*[a for a, spec in ins], *deps)


def attend_kernel(q_ref, k0, k1, v0, v1, o_ref, full_ref, lse_ref):
    count = q_ref.shape[0]
    n = k0.shape[0]
    q = q_ref[...]
    wide_q = q.astype(F32)
    square_q = (wide_q * wide_q).astype(BF)
    turned, squares = [v0[...].T, v1[...].T], []
    for k in (k0, k1):
        wide_k = k[...].astype(F32)
        squares.append((wide_k * wide_k).astype(BF))
    chunk = min(KEY_CHUNK, n)

    def one_head(head, exact):
        qm = of_head(q, head)
        top = None
        if exact:
            for k in (k0, k1):
                for i in range(0, n, chunk):
                    part = jnp.max(mm(k[i : i + chunk], qm, NT), axis=0, keepdims=True)
                    top = part if top is None else jnp.maximum(top, part)
        else:
            pick = of_head(jnp.ones((8, 128), BF), head)
            for square in squares:
                part = jnp.max(mm(pick, square, NT))
                top = part if top is None else jnp.maximum(top, part)
            top = jnp.sqrt(mm(pick, square_q, NT)[0:1] * (top * 1.05))
        out = total = None
        for k, values in ((k0, turned[0]), (k1, turned[1])):
            for i in range(0, n, chunk):
                probs = jnp.exp2(mm(k[i : i + chunk], qm, NT) - top)
                part = jnp.sum(probs, axis=0, keepdims=True)
                total = part if total is None else total + part
                part = mm(values[:, i : i + chunk], probs.astype(BF))
                out = part if out is None else out + part
        lse = jnp.broadcast_to(top + jnp.log2(total), (64, count))
        return out[64 * head : 64 * head + 64] / total, lse, jnp.min(total)

    def run(exact):
        first, second = one_head(0, exact), one_head(1, exact)
        out = jnp.concatenate([first[0], second[0]], 0).T
        o_ref[...] = out.astype(BF)
        full_ref[...] = out
        lse_ref[...] = jnp.concatenate([first[1], second[1]], 0).T
        return jnp.minimum(first[2], second[2])

    least = run(False)

    @pl.when(jnp.logical_not(least >= SMALLEST))
    def _():
        run(True)


def attend(q, kv_own, kv_peer, frames):
    tokens, width = q.shape
    pairs = width // 128
    n = tokens // frames
    qs = pl.BlockSpec((n, 128), lambda f, p: (f, p))
    vs = pl.BlockSpec((n, 128), lambda f, p: (f, pairs + p))
    return call(
        attend_kernel,
        "attend",
        (frames, pairs),
        [(q, qs), (kv_own, qs), (kv_peer, qs), (kv_own, vs), (kv_peer, vs)],
        [
            (sds((tokens, width), BF), qs),
            (sds((tokens, width), F32), qs),
            (sds((tokens, width), F32), qs),
        ],
        flops=30_000_000_000,
        vmem=VM_ATTEND,
    )


def attend_back_kernel(
    q_ref, k0, k1, v0, v1, go_ref, o_ref, lse_ref, dq_ref, dk0, dk1, dv0, dv1, dka, dva
):
    n = k0.shape[0]
    q = q_ref[...]
    go = go_ref[...]
    turned_q, turned_go = q.T, go.T
    prod = go.astype(F32) * o_ref[...]
    qms = [of_head(q, head) for head in range(2)]
    goms = [of_head(go, head) for head in range(2)]
    lses = [lse_ref[:, 64 * head : 64 * head + 1] for head in range(2)]
    deltas = [jnp.sum(of_head(prod, head), axis=1, keepdims=True) for head in range(2)]
    chunk = min(KEY_CHUNK, n)
    dq = None
    for part, (k, v) in enumerate(((k0, v0), (k1, v1))):
        for i in range(0, n, chunk):
            keys = k[i : i + chunk]
            vals = v[i : i + chunk]
            for head in range(2):
                lanes = slice(64 * head, 64 * head + 64)
                probs = jnp.exp2(mm(qms[head], keys, NT) - lses[head])
                ds = (probs * (mm(goms[head], vals, NT) - deltas[head])).astype(BF)
                dva[part, lanes, i : i + chunk] = mm(turned_go, probs.astype(BF))[lanes]
                dka[part, lanes, i : i + chunk] = mm(turned_q, ds)[lanes]
                term = mm(ds, of_head(keys, head))
                dq = term if dq is None else dq + term
    dq_ref[...] = (dq * SCALING).astype(BF)
    back = 1.0 / LOG2E
    for part, (dk, dv) in enumerate(((dk0, dv0), (dk1, dv1))):
        dk[...] = (dka[part].T * back).astype(BF)
        dv[...] = dva[part].T.astype(BF)


def attend_back(q, kv_own, kv_peer, go, att, lse, frames, first, count, deps):
    tokens, width = q.shape
    pairs = width // 128
    n = tokens // frames
    qs = pl.BlockSpec((n, 128), lambda f, p: (f, first + p))
    vs = pl.BlockSpec((n, 128), lambda f, p: (f, pairs + first + p))
    out = pl.BlockSpec((n, 128), lambda f, p: (f, p))
    shape = sds((tokens, 128 * count), BF)
    return call(
        attend_back_kernel,
        "attend_back",
        (frames, count),
        [(q, qs), (kv_own, qs), (kv_peer, qs), (kv_own, vs), (kv_peer, vs), (go, qs), (att, qs), (lse, qs)],
        [(shape, out)] * 5,
        [pltpu.VMEM((2, 128, n), F32)] * 2,
        11_000_000_000 * count,
        deps,
        VM_BACK,
    )


def normed_of(value):
    row_mean = jnp.mean(value, axis=-1, keepdims=True)
    centered = value - row_mean
    inverse = lax.rsqrt(jnp.mean(centered * centered, axis=-1, keepdims=True) + EPSILON)
    return centered * inverse, inverse


def norm_back(grad_hat, normed, inverse):
    first = jnp.mean(grad_hat, axis=-1, keepdims=True)
    second = jnp.mean(grad_hat * normed, axis=-1, keepdims=True)
    return inverse * (grad_hat - first - normed * second)


def rows_of(block, width):
    return pl.BlockSpec((block, width), lambda i: (i, 0))


def whole_of(shape):
    return pl.BlockSpec(shape, lambda i: (0,) * len(shape))


SMALL = pl.BlockSpec(memory_space=pltpu.SMEM)


def qkv_kernel(x_ref, chan_ref, shift_ref, gain_ref, w, h_ref, kv_ref, q_ref):
    width = x_ref.shape[1]
    normed, inverse = normed_of(x_ref[...].astype(F32) + chan_ref[0])
    hidden = (normed * gain_ref[...] + shift_ref[0]).astype(BF)
    h_ref[...] = hidden
    kv_ref[...] = mm(hidden, w[:, width:]).astype(BF)
    q_ref[...] = (mm(hidden, w[:, :width]) * (SCALING * LOG2E)).astype(BF)


def qkv_of(x, chan_add, shift, gain, weight, frames, deps):
    count, width = x.shape
    block = 256
    per = count // frames // block
    frame = pl.BlockSpec((1, 1, width), lambda i: (i // per, 0, 0))
    narrow = rows_of(block, width)
    return call(
        qkv_kernel,
        "qkv",
        (count // block,),
        [
            (x, narrow),
            (chan_add, frame),
            (shift, frame),
            (gain, whole_of((1, width))),
            (weight, whole_of(weight.shape)),
        ],
        [
            (sds((count, width), BF), narrow),
            (sds((count, 2 * width), BF), rows_of(block, 2 * width)),
            (sds((count, width), BF), narrow),
        ],
        flops=3_600_000_000,
        deps=deps,
        vmem=VM_QKV,
    )


ROOT = math.sqrt(2 / math.pi)
CUBE = ROOT * 0.044715


def gelu_both(x):
    square = x * x
    t = jnp.tanh(x * (ROOT + CUBE * square))
    half = 0.5 * t + 0.5
    slope = half + (0.5 * x) * (1.0 - t * t) * (ROOT + (3.0 * CUBE) * square)
    return x * half, slope


def mlp_kernel(
    x_ref,
    chan_ref,
    att_ref,
    g_ref,
    rows_ref,
    up_bias_ref,
    wo_any,
    wu_any,
    wd_any,
    res_ref,
    act_ref,
    gpre_ref,
    hid_ref,
    mid_ref,
    branch_ref,
    gatt_ref,
    sums_ref,
    wo,
    wu,
    wd,
    sems,
):
    step = pl.program_id(0)
    width = x_ref.shape[1]
    copies = [
        pltpu.make_async_copy(wo_any, wo, sems.at[0]),
        pltpu.make_async_copy(wu_any, wu, sems.at[1]),
        pltpu.make_async_copy(wd_any, wd, sems.at[2]),
    ]

    @pl.when(step == 0)
    def _():
        for c in copies:
            c.start()
        sums_ref[...] = jnp.zeros_like(sums_ref)
        copies[0].wait()

    out_bias, gain, shift, down_bias = [rows_ref[i : i + 1] for i in range(4)]
    middle = x_ref[...].astype(F32) + chan_ref[0] + mm(att_ref[...], wo[...]) + out_bias
    normed, inverse = normed_of(middle)
    hidden = (normed * gain + shift).astype(BF)
    hid_ref[...] = hidden
    g = g_ref[...]

    @pl.when(step == 0)
    def _():
        copies[1].wait()
        copies[2].wait()

    result = middle + down_bias
    grad_hidden = None
    part = width // MLP_SPLIT
    spans = [pl.ds(i * part, part) for i in range(wu.shape[1] // part)]

    def products(cols):
        return mm(hidden, wu[:, cols]), mm(g, wd[cols, :], NT)

    ready = products(spans[0])
    for i, cols in enumerate(spans):
        pre, back = ready
        if i + 1 < len(spans):
            ready = products(spans[i + 1])
        act, slope = gelu_both(pre + up_bias_ref[:, cols])
        act = act.astype(BF)
        act_ref[:, cols] = act
        grad_pre = (back * slope).astype(BF)
        gpre_ref[:, cols] = grad_pre
        at = i % MLP_SPLIT * part
        row = 4 + i // MLP_SPLIT
        sums_ref[row : row + 1, at : at + part] += jnp.sum(
            grad_pre.astype(F32), axis=0, keepdims=True
        )
        result = result + mm(act, wd[cols, :])
        term = mm(grad_pre, wu[:, cols], NT)
        grad_hidden = term if grad_hidden is None else grad_hidden + term
    res_ref[...] = result.astype(BF)
    g = g.astype(F32)
    sums_ref[0:1] += jnp.sum(g, axis=0, keepdims=True)
    sums_ref[1:2] += jnp.sum(grad_hidden * normed, axis=0, keepdims=True)
    sums_ref[2:3] += jnp.sum(grad_hidden, axis=0, keepdims=True)
    grad_middle = g + norm_back(grad_hidden * gain, normed, inverse)
    mid_ref[...] = grad_middle
    branch = grad_middle.astype(BF)
    branch_ref[...] = branch
    sums_ref[3:4] += jnp.sum(branch.astype(F32), axis=0, keepdims=True)
    gatt_ref[...] = mm(branch, wo[...], NT).astype(BF)


def mlp(x, chan_add, att, g, rows, up_bias, wo, wu, wd, frames):
    count, width = x.shape
    wide = wu.shape[1]
    block = MLP_BLOCK
    per = count // frames // block
    narrow, broad = rows_of(block, width), rows_of(block, wide)
    anywhere = pl.BlockSpec(memory_space=pl.ANY)
    return call(
        mlp_kernel,
        "mlp",
        (count // block,),
        [
            (x, narrow),
            (chan_add, pl.BlockSpec((1, 1, width), lambda i: (i // per, 0, 0))),
            (att, narrow),
            (g, narrow),
            (rows, whole_of((4, width))),
            (up_bias, whole_of((1, wide))),
            (wo, anywhere),
            (wu, anywhere),
            (wd, anywhere),
        ],
        [
            (sds((count, width), BF), narrow),
            (sds((count, wide), BF), broad),
            (sds((count, wide), BF), broad),
            (sds((count, width), BF), narrow),
            (sds((count, width), F32), narrow),
            (sds((count, width), BF), narrow),
            (sds((count, width), BF), narrow),
            (sds((4 + wide // width, width), F32), whole_of((4 + wide // width, width))),
        ],
        [
            pltpu.VMEM(wo.shape, BF),
            pltpu.VMEM(wu.shape, BF),
            pltpu.VMEM(wd.shape, BF),
            pltpu.SemaphoreType.DMA((3,)),
        ],
        25_000_000_000,
        vmem=VM_MLP,
    )


def down_grad_kernel(core_ref, act_ref, g_ref, send_ref, keep_ref, scr):
    core = core_ref[0]
    places, share, width = scr.shape[1:]
    scr[...] = mm(act_ref[...], g_ref[...], TN).reshape(scr.shape)
    keep_ref[...] = scr[:, core].astype(BF)
    send_ref[...] = scr[:, 1 - core].astype(BF)


def down_grad(core, act, g, lon, deps):
    count, wide = act.shape
    width = g.shape[1]
    share = wide // lon
    tile = DOWN_TILE
    chips = tile // (2 * share)
    out = sds((lon // 2, share, width), BF)
    spec = pl.BlockSpec((chips, share, width), lambda i: (i, 0, 0))
    return call(
        down_grad_kernel,
        "down_grad",
        (wide // tile,),
        [(core, SMALL), (act, pl.BlockSpec((count, tile), lambda i: (0, i))), (g, whole_of((count, width)))],
        [(out, spec), (out, spec)],
        [pltpu.VMEM((chips, 2, share, width), F32)],
        4_800_000_000,
        deps,
        VM_SUM,
    )


def up_grad_kernel(core_ref, hid_ref, gpre_ref, att_ref, branch_ref, send_ref, keep_ref, turned, scr):
    core = core_ref[0]
    step = pl.program_id(0)
    last = pl.num_programs(0) - 1

    @pl.when(step == 0)
    def _():
        turned[...] = hid_ref[...].T

    @pl.when(step < last)
    def _():
        scr[...] = mm(turned[...], gpre_ref[...]).reshape(scr.shape)

    @pl.when(step == last)
    def _():
        scr[...] = mm(att_ref[...], branch_ref[...], TN).reshape(scr.shape)

    keep_ref[...] = scr[:, core].astype(BF)
    send_ref[...] = scr[:, 1 - core].astype(BF)


def up_grad(core, hidden, gpre, att, branch, lon):
    count, width = hidden.shape
    wide = gpre.shape[1]
    share = width // lon
    last = wide // width - 1
    out = sds((lon // 2, share, wide + width), BF)
    spec = pl.BlockSpec((lon // 2, share, width), lambda i: (0, 0, i))
    full = whole_of((count, width))
    return call(
        up_grad_kernel,
        "up_grad",
        (last + 2,),
        [
            (core, SMALL),
            (hidden, full),
            (gpre, pl.BlockSpec((count, width), lambda i: (0, jnp.minimum(i, last)))),
            (att, full),
            (branch, full),
        ],
        [(out, spec), (out, spec)],
        [pltpu.VMEM((width, count), BF), pltpu.VMEM((lon // 2, 2, share, width), F32)],
        6_000_000_000,
        vmem=VM_SUM,
    )


def fill_part(out, pieces, part):
    at = 0
    for dq, dk0, dv0, got_k, got_v in pieces:
        size = dq.shape[1]
        if part == 0:
            out[:, at : at + size] = dq[...]
        elif part == 1:
            out[:, at : at + size] = dk0[...] + got_k[...]
        else:
            out[:, at : at + size] = dv0[...] + got_v[...]
        at += size


def groups_of(refs):
    return [refs[i : i + 5] for i in range(0, len(refs), 5)]


def qkv_grad_kernel(core_ref, hid_ref, *refs):
    pieces = groups_of(refs[:-5])
    send_ref, keep_ref, turned, grad, scr = refs[-5:]
    core = core_ref[0]
    step = pl.program_id(0)

    @pl.when(step == 0)
    def _():
        turned[...] = hid_ref[...].T

    for part in range(3):

        @pl.when(step == part)
        def _():
            fill_part(grad, pieces, part)

    scr[...] = mm(turned[...], grad[...]).reshape(scr.shape)
    keep_ref[...] = scr[:, core].astype(BF)
    send_ref[...] = scr[:, 1 - core].astype(BF)


def qkv_grad(core, hidden, pieces, lon, deps):
    count, width = hidden.shape
    share = width // lon
    out = sds((lon // 2, share, 3 * width), BF)
    spec = pl.BlockSpec((lon // 2, share, width), lambda i: (0, 0, i))
    return call(
        qkv_grad_kernel,
        "qkv_grad",
        (3,),
        [(core, SMALL), (hidden, whole_of((count, width)))]
        + [(a, whole_of(a.shape)) for group in pieces for a in group],
        [(out, spec), (out, spec)],
        [
            pltpu.VMEM((width, count), BF),
            pltpu.VMEM((count, width), BF),
            pltpu.VMEM((lon // 2, 2, share, width), F32),
        ],
        3_600_000_000,
        deps,
        VM_SUM,
    )


def first_back_kernel_of(groups, frame_blocks):
    def kernel(*refs):
        pieces = groups_of(refs[: 5 * groups])
        x_ref, chan_ref, gain_ref, mid_ref, w, patch_ref, frame_ref, gain_sum, qkv_ref = refs[5 * groups :]
        step = pl.program_id(0)
        width = x_ref.shape[1]
        for part in range(3):
            fill_part(qkv_ref.at[:, part * width : (part + 1) * width], pieces, part)
        grad_hidden = mm(qkv_ref[...], w[...], NT)
        normed, inverse = normed_of(x_ref[...].astype(F32) + chan_ref[0])
        grad_start = mid_ref[...] + norm_back(grad_hidden * gain_ref[...], normed, inverse)
        patch_ref[...] = grad_start.astype(BF)

        @pl.when(step == 0)
        def _():
            gain_sum[...] = jnp.zeros_like(gain_sum)

        @pl.when(lax.rem(step, frame_blocks) == 0)
        def _():
            frame_ref[...] = jnp.zeros_like(frame_ref)

        gain_sum[...] += jnp.sum(grad_hidden * normed, axis=0, keepdims=True)
        frame_ref[0, 0:1] += jnp.sum(grad_hidden, axis=0, keepdims=True)
        frame_ref[0, 1:2] += jnp.sum(grad_start, axis=0, keepdims=True)

    return kernel


def first_back(pieces, x, chan_add, gain, grad_middle, weight, frames, deps):
    count, width = x.shape
    block = 256
    per = count // frames // block
    ins = [(a, rows_of(block, a.shape[1])) for group in pieces for a in group]
    return call(
        first_back_kernel_of(len(pieces), per),
        "first_back",
        (count // block,),
        ins
        + [
            (x, rows_of(block, width)),
            (chan_add, pl.BlockSpec((1, 1, width), lambda i: (i // per, 0, 0))),
            (gain, whole_of((1, width))),
            (grad_middle, rows_of(block, width)),
            (weight, whole_of(weight.shape)),
        ],
        [
            (sds((count, width), BF), rows_of(block, width)),
            (sds((frames, 2, width), F32), pl.BlockSpec((1, 2, width), lambda i: (i // per, 0, 0))),
            (sds((1, width), F32), whole_of((1, width))),
        ],
        [pltpu.VMEM((block, 3 * width), BF)],
        3_600_000_000,
        deps,
        VM_SUM,
    )


def swap_pairs(size, bit):
    return [(i, i ^ (1 << bit)) for i in range(size)]


def bits_of(size):
    return size.bit_length() - 1


def my_bit(axis, bit):
    return ((lax.axis_index(axis) >> bit) & 1).astype(jnp.int32).reshape(1)


def swap(value, axis, bit):
    return lax.ppermute(value, axis, swap_pairs(lax.axis_size(axis), bit))


def cross(value, turn):
    pairs = []
    for i in range(8):
        lat_next = (i & 1) == turn
        pairs.append((i, i ^ (4 if lat_next else 2)))
    return lax.ppermute(value, ("lat", "yy", "core"), pairs)


EVERY = slice(None)


def both(kept_ref, got_ref, *at):
    return (kept_ref[at].astype(F32) + got_ref[at].astype(F32)).astype(BF)


def mlp_part(ins, out, at, yy, half):
    kept_d, got_d, kept_u, got_u = ins
    rows, width = kept_d.shape[1:]
    share = kept_u.shape[1]
    wide = kept_u.shape[2] - width

    @pl.when(half == 0)
    def _():
        out[0, at, :rows] = both(kept_d, got_d, yy)
        out[0, at, rows:] = both(kept_u, got_u, yy, slice(0, share // 2), slice(wide, None))

    @pl.when(half == 1)
    def _():
        for c in range(wide // width):
            out[0, at, c * share : (c + 1) * share] = both(
                kept_u, got_u, yy, EVERY, slice(c * width, (c + 1) * width)
            )
        out[0, at, rows:] = both(kept_u, got_u, yy, slice(share // 2, None), slice(wide, None))


def qkv_part(ins, out, at, yy, half):
    kept, got = ins
    cols = kept.shape[2] // 2
    for side in range(2):

        @pl.when(half == side)
        def _():
            out[0, at] = both(kept, got, yy, slice(None), slice(side * cols, (side + 1) * cols))


def first_add(part, ins, rows, cols, deps=()):
    zed = ins[0].shape[0] // 2

    def kernel(where_ref, *refs):
        core, mine = where_ref[0], where_ref[1]
        for which, out in zip((1 - mine, mine), refs[len(ins) :]):
            for at in range(2):
                yy = jnp.where(core == 0, at, which)
                half = jnp.where(core == 0, which, at)
                part(refs[: len(ins)], out, at, yy, half)

    core = my_bit("core", 0)
    mine = jnp.where(core == 0, my_bit("lat", 0), my_bit("yy", 0))
    out = sds((zed, 2, rows, cols), BF)
    spec = pl.BlockSpec((1, 2, rows, cols), lambda i: (i, 0, 0, 0))
    return call(
        kernel,
        "first_add",
        (zed,),
        [(jnp.concatenate([core, mine]), SMALL)]
        + [(a, pl.BlockSpec((2,) + a.shape[1:], lambda i: (i, 0, 0))) for a in ins],
        [(out, spec)] * 2,
        deps=deps,
        vmem=VM_SUM,
    )


def second_add(kept, got, deps=()):
    zed, two, rows, cols = kept.shape

    def kernel(mine_ref, kept_ref, got_ref, send_ref, keep_ref):
        mine = mine_ref[0]
        send_ref[0] = both(kept_ref, got_ref, 0, 1 - mine)
        keep_ref[0] = both(kept_ref, got_ref, 0, mine)

    mine = jnp.where(my_bit("core", 0) == 0, my_bit("yy", 0), my_bit("lat", 0))
    spec = pl.BlockSpec((1, 2, rows, cols), lambda i: (i, 0, 0, 0))
    out = pl.BlockSpec((1, rows, cols), lambda i: (i, 0, 0))
    return call(
        kernel,
        "second_add",
        (zed,),
        [(mine, SMALL), (kept, spec), (got, spec)],
        [(sds((zed, rows, cols), BF), out)] * 2,
        deps=deps,
        vmem=VM_SUM,
    )


def third_add(kept, got, deps=()):
    zed, rows, cols = kept.shape

    def kernel(me_ref, kept_ref, got_ref, *outs):
        for up, out in enumerate(outs):
            out[...] = both(kept_ref, got_ref, lax.rem(me_ref[0] + up, zed))

    me = lax.axis_index("zed").astype(jnp.int32).reshape(1)
    return call(
        kernel,
        "third_add",
        (1,),
        [(me, SMALL), (kept, whole_of(kept.shape)), (got, whole_of(kept.shape))],
        [(sds((rows, cols), BF), whole_of((rows, cols)))] * zed,
        deps=deps,
        vmem=VM_SUM,
    )


def cut_lead(kept, got, bit, deps=()):
    zed, rows, cols = kept.shape

    def kernel(mine_ref, kept_ref, got_ref, send_ref, keep_ref):
        mine = mine_ref[0]
        send_ref[0] = both(kept_ref, got_ref, 1 - mine)
        keep_ref[0] = both(kept_ref, got_ref, mine)

    spec = pl.BlockSpec((2, rows, cols), lambda i: (i, 0, 0))
    out = pl.BlockSpec((1, rows, cols), lambda i: (i, 0, 0))
    return call(
        kernel,
        "cut_lead",
        (zed // 2,),
        [(my_bit("zed", bit), SMALL), (kept, spec), (got, spec)],
        [(sds((zed // 2, rows, cols), BF), out)] * 2,
        deps=deps,
        vmem=VM_SUM,
    )


def up_zed(value, up):
    zed = lax.axis_size("zed")
    return lax.ppermute(value, "zed", [(i, (i + up) % zed) for i in range(zed)])


def last_add(parts, deps=()):
    rows, cols = parts[0].shape

    def kernel(*refs):
        total = refs[0][...].astype(F32)
        for ref in refs[1:-1]:
            total = total + ref[...].astype(F32)
        refs[-1][...] = total.astype(BF)

    spec = whole_of((rows, cols))
    return call(
        kernel,
        "last_add",
        (1,),
        [(a, spec) for a in parts],
        [(sds((rows, cols), BF), spec)],
        deps=deps,
        vmem=VM_SUM,
    )[0]


def passed_after(value, deps):
    def kernel(*refs):
        pass

    anywhere = pl.BlockSpec(memory_space=pl.ANY)
    return pl.pallas_call(
        kernel,
        grid=(1,),
        in_specs=[anywhere] * (1 + len(deps)),
        out_specs=anywhere,
        out_shape=sds(value.shape, value.dtype),
        input_output_aliases={0: 0},
        compiler_params=pltpu.CompilerParams(vmem_limit_bytes=VM_SUM << 20),
        name="passed_after",
    )(value, *deps)


def spread(mine, other, shapes, fill, deps=()):
    def kernel(high_ref, mine_ref, other_ref, *outs):
        @pl.when(high_ref[0] == 0)
        def _():
            fill(mine_ref, other_ref, outs)

        @pl.when(high_ref[0] == 1)
        def _():
            fill(other_ref, mine_ref, outs)

    spec = whole_of(mine.shape)
    return call(
        kernel,
        "spread",
        (1,),
        [(my_bit("lat", 0), SMALL), (mine, spec), (other, spec)],
        [(sds(shape, F32), whole_of(shape)) for shape in shapes],
        deps=deps,
        vmem=VM_SUM,
    )


def fill_qkv(low, high, outs):
    cols = low.shape[1]
    outs[0][:, :cols] = low[...].astype(F32)
    outs[0][:, cols:] = high[...].astype(F32)


def fill_mlp(low, high, outs):
    down, up, out = outs
    tall, share, width = down.shape[0], up.shape[0], down.shape[1]
    down[...] = low[:tall].astype(F32)
    for c in range(up.shape[1] // width):
        up[:, c * width : (c + 1) * width] = high[c * share : (c + 1) * share].astype(F32)
    out[: share // 2] = low[tall:].astype(F32)
    out[share // 2 :] = high[tall:].astype(F32)


def beside(value):
    value = value[None]
    for axis in ("yy", "lat"):
        for bit in range(bits_of(lax.axis_size(axis))):
            other = swap(value, axis, bit)
            high = my_bit(axis, bit)[0] == 1
            value = jnp.where(
                high, jnp.concatenate([other, value], 0), jnp.concatenate([value, other], 0)
            )
    return value


def held(value, deps):
    def kernel(value_ref, out_ref):
        out_ref[...] = value_ref[...]

    spec = whole_of(value.shape)
    return call(
        kernel, "held", (1,), [(value, spec)], [(sds(value.shape, value.dtype), spec)], deps=deps
    )[0]


def plain_sum(kept, got):
    value = lax.psum_scatter(kept + got, ("zed", "yy"), scatter_dimension=0, tiled=True)[0]
    return lax.psum(value.astype(F32), "lat")


def to_frames(value, chips):
    frames_all, patches, width = value.shape
    frames = frames_all // chips
    value = lax.all_to_all(value, ("lat", "zed", "yy"), 0, 0, tiled=True)
    if frames > 1:
        value = value.reshape(chips, frames, patches, width).swapaxes(0, 1)
    return value.reshape(-1, width)


def to_places(value, chips, frames_all):
    width = value.shape[-1]
    frames = frames_all // chips
    if frames > 1:
        value = value.reshape(frames, chips, -1, width).swapaxes(0, 1)
    value = value.reshape(frames_all, -1, width)
    return lax.all_to_all(value, ("lat", "zed", "yy"), 0, 0, tiled=True)


def on_device(
    tokens,
    channel_mask,
    lead_index,
    chan_embed,
    lead_embed,
    norm1_gain,
    norm1_bias,
    qkv_weight,
    out_weight,
    out_bias,
    norm2_gain,
    norm2_bias,
    up_weight,
    up_bias,
    down_weight,
    down_bias,
    cotangent,
):
    lat = lax.axis_size("lat")
    lon = 4 * lax.axis_size("zed")
    chips = lat * (lon // 2)
    frames_all, rows_here, cols_here, width = tokens.shape
    frames = frames_all // chips
    leads = lead_embed.shape[0]
    wide = up_weight.shape[1]
    share = width // lon
    core = my_bit("core", 0)

    x = to_frames(tokens.reshape(frames_all, -1, width), chips)
    flat = cotangent.reshape(frames_all, -1, width)
    g = to_frames(flat, chips)
    count = x.shape[0]

    first = lax.axis_index(("lat", "zed", "yy")) * frames
    mask_here = lax.dynamic_slice_in_dim(channel_mask, first, frames, 0).astype(BF)
    lead_here = lax.dynamic_slice_in_dim(lead_index, first, frames, 0)
    lead_onehot = (lead_here[:, None] == jnp.arange(leads, dtype=jnp.int32)[None, :]).astype(BF)
    chan_add = mm(mask_here, chan_embed)[:, None, :]
    shift1 = (mm(lead_onehot, lead_embed) + norm1_bias.astype(F32))[:, None, :]
    gain1 = norm1_gain.astype(F32)[None]
    rows2 = jnp.stack([out_bias, norm2_gain, norm2_bias, down_bias]).astype(F32)

    hidden1, kv_own, queries = qkv_of(x, chan_add, shift1, gain1, qkv_weight, frames, (flat,))
    kv_peer = swap(kv_own, "core", 0)
    attended, attended32, lse = attend(queries, kv_own, kv_peer, frames)

    result, activ, grad_pre, hidden2, grad_middle, grad_branch, grad_att, early = mlp(
        x,
        chan_add,
        attended,
        g,
        rows2,
        up_bias.astype(F32)[None],
        out_weight,
        up_weight,
        down_weight,
        frames,
    )
    out_patch = to_places(result, chips, frames_all)
    up_send, up_kept = up_grad(core, hidden2, grad_pre, attended, grad_branch, lon)
    up_got = swap(up_send, "core", 0)
    down_send, down_kept = down_grad(core, activ, g, lon, (up_send,))
    down_got = swap(down_send, "core", 0)

    staged = lat == 2
    rows = down_kept.shape[1] + share // 2
    pieces, pair = [], 0
    deps = (down_kept,)
    if staged:
        sent, kept = first_add(mlp_part, [down_kept, down_got, up_kept, up_got], rows, width)
        got = cross(sent, 0)
        deps = (sent,)
    pairs = width // 128
    plan = [pairs - 2, 1, 1]
    for at, size in enumerate(plan):
        dq, dk0, dk1, dv0, dv1 = attend_back(
            queries, kv_own, kv_peer, grad_att, attended32, lse, frames, pair, size, deps
        )
        pieces.append((dq, dk0, dv0, swap(dk1, "core", 0), swap(dv1, "core", 0)))
        pair += size
        deps = (dq,)
        if staged and at == 0:
            sent, kept = second_add(kept, got, deps)
            got = cross(sent, 1)
            deps = (sent, dq)
        if staged and at == 1:
            sent, kept = cut_lead(kept, got, 0, deps)
            got = swap(sent, "zed", 0)
            deps = (sent, dq)

    if staged:
        for bit in range(1, bits_of(lax.axis_size("zed"))):
            sent, kept = cut_lead(kept, got, bit, deps)
            got = swap(sent, "zed", bit)
            deps = (sent, out_patch)
        mlp_parts = [kept[0], got[0]]
    grad_start, frame_sums, gain_sum = first_back(
        pieces, x, chan_add, gain1, grad_middle, qkv_weight, frames, deps
    )
    if staged:
        grad_start = passed_after(grad_start, (mlp_parts[1],))
        mlp_sum = last_add(mlp_parts, (grad_start,))
    grad_patch = to_places(grad_start, chips, frames_all)

    ups = wide // width
    early_up = early[4:].reshape(lon, ups, share).swapaxes(0, 1).reshape(ups, width)
    late = jnp.concatenate(
        [frame_sums.reshape(2 * frames, width), gain_sum, early[:4], early_up], 0
    )
    late = late.reshape(-1, lon // 2, 2, share)
    mine = core[0]
    late_got = swap(lax.dynamic_index_in_dim(late, 1 - mine, 2, keepdims=False), "core", 0)
    late = lax.dynamic_index_in_dim(late, mine, 2, keepdims=False) + late_got

    deps = (late_got,)
    qkv_send, qkv_kept = qkv_grad(core, hidden1, pieces, lon, deps)
    qkv_got = swap(qkv_send, "core", 0)

    zed = lax.axis_size("zed")

    if staged:
        sent, kept = first_add(qkv_part, [qkv_kept, qkv_got], share, 3 * width // 2)
        got = cross(sent, 0)
        late = beside(held(late.reshape(late.shape[0], -1), (sent,)))
        sent, kept = second_add(kept, got, (grad_patch, late))
        got = cross(sent, 1)
        parts = third_add(kept, got)
        deps = (parts[0],)
        parts = [parts[0]] + [up_zed(part, up) for up, part in enumerate(parts) if up]
        mlp_sum = held(mlp_sum, deps)
        late = held(late, deps)
        tall = wide // lon
        sum_down, sum_up, sum_out = spread(
            mlp_sum, swap(mlp_sum, "lat", 0), [(tall, width), (share, wide), (share, width)], fill_mlp
        )
        total = last_add(parts, (sum_down,))
        sum_qkv = spread(total, swap(total, "lat", 0), [(share, 3 * width)], fill_qkv)[0]
    else:
        sum_down = plain_sum(down_kept, down_got)
        sum_up = plain_sum(up_kept, up_got)
        sum_up, sum_out = sum_up[:, :wide], sum_up[:, wide:]
        sum_qkv = plain_sum(qkv_kept, qkv_got)
        late = beside(late.reshape(late.shape[0], -1))

    late = jnp.stack([late] + [up_zed(late, up) for up in range(1, zed)])
    late = jnp.take(late, (lax.axis_index("zed") - jnp.arange(zed)) % zed, axis=0)
    late = lax.dynamic_slice_in_dim(late, lax.axis_index(("zed", "yy")) * share, share, 3)
    late = late.reshape(zed, lat, 2, -1, share).swapaxes(0, 1).reshape(chips, -1, share)
    bias_of = late[:, 0 : 2 * frames : 2].reshape(frames_all, share)
    start_of = late[:, 1 : 2 * frames : 2].reshape(frames_all, share)
    rest = late[:, 2 * frames :].sum(0)
    hot = (lead_index[:, None] == jnp.arange(leads, dtype=jnp.int32)[None, :]).astype(F32)
    exact = lax.Precision.HIGHEST
    sum_lead = jnp.dot(hot.T, bias_of, precision=exact)
    sum_chan = jnp.dot(channel_mask.astype(F32).T, start_of, precision=exact)

    shape = (frames_all, rows_here, cols_here, width)
    return (
        out_patch.reshape(shape),
        grad_patch.reshape(shape),
        sum_chan,
        sum_lead,
        rest[0],
        bias_of.sum(0),
        sum_qkv,
        sum_out,
        rest[4],
        rest[2],
        rest[3],
        sum_up,
        rest[5:].reshape(-1),
        sum_down,
        rest[1],
    )


def solution(mesh):
    lat, lon = mesh.shape["lat"], mesh.shape["lon"]
    fine = Mesh(mesh.devices.reshape(lat, lon // 4, 2, 2), ("lat", "zed", "yy", "core"))
    wide = ("zed", "yy", "core")
    places = P(None, "lat", wide, None)
    return jax.shard_map(
        on_device,
        mesh=fine,
        in_specs=(places,) + (P(),) * 15 + (places,),
        out_specs=(
            places,
            places,
            P(None, wide),
            P(None, wide),
            P(wide),
            P(wide),
            P(wide, None),
            P(wide, None),
            P(wide),
            P(wide),
            P(wide),
            P(wide, None),
            P(wide),
            P(wide, None),
            P(wide),
        ),
        check_vma=False,
    )
```
